32 devices in a mesh: dp: 8 (over y, x, core), mp: 4 (over z).
Axes of the slice: x: 2, y: 2, z: 4, core: 2. Of those that a mesh axis runs over, the one named last changes fastest.
Arguments:
- tokens: bfloat16 [4096, 768], P(('dp', 'mp')), may hold values from -6 to 6
- page_lengths: int32 [8, 8], P('dp'), may hold values from 1 to 256, 512 in all within a row
- norm_gains: float32 [2, 768], replicated, may hold values from 0.1 to 1.9
- norm_biases: float32 [2, 768], replicated, may hold values from -1.5 to 1.5
- layer_scales: float32 [2, 768], replicated, may hold values from 0.5 to 2
- w_qkv: bfloat16 [768, 3, 768], P(None, None, 'mp'), may hold values from -0.3125 to 0.3125
- rel_table: float32 [32, 12], replicated, may hold values from -4 to 4
- w_out: bfloat16 [768, 768], P('mp'), may hold values from -0.875 to 0.875
- w_up: bfloat16 [768, 3072], P(None, 'mp'), may hold values from -0.21875 to 0.21875
- w_down: bfloat16 [3072, 768], P('mp'), may hold values from -0.109375 to 0.109375
- cotangent: bfloat16 [4096, 768], P(('dp', 'mp')), may hold values from -6 to 6
Outputs:
- output: bfloat16 [4096, 768], P(('dp', 'mp'))
- grad_input: bfloat16 [4096, 768], P(('dp', 'mp'))
- grad_norm_gains: float32 [2, 768], replicated
- grad_norm_biases: float32 [2, 768], replicated
- grad_layer_scales: float32 [2, 768], replicated
- grad_w_qkv: float32 [768, 3, 768], P('dp', None, 'mp')
- grad_rel_table: float32 [32, 12], replicated
- grad_w_out: float32 [768, 768], P('mp', 'dp')
- grad_w_up: float32 [768, 3072], P('dp', 'mp')
- grad_w_down: float32 [3072, 768], P('mp', 'dp')
The draws below stay inside these ranges and needn't reach their ends.
Inputs may be any that keep to these rules, and one draw needn't show every extreme that they name: Each row of page_lengths sums to 512, and its largest entry is exactly 256; the last page of each row is padding.
All inputs are finite; a program needn't handle non-finite values.
Results may differ from the reference program's by a relative error of at most 0.013.
The reference program's roundings to bfloat16 on the way count: a program that leaves them out, or rounds other values in their place, can miss the bound.
Values may be sent and summed in bfloat16 or wider, within the bound.
No kernel may reach another device: no remote copies, remote signals or barrier semaphores. Data moves between devices by JAX's collectives and lax.ppermute only.
A program may use at most 128 MiB of HBM per device.

```python
import math
import jax
import jax.numpy as jnp
import numpy as np
from jax import lax

D = 768
HEADS = 12
HEAD_DIM = 64
FF = 3072
TOK_DEV = 512
PAGES = 8
BUCKETS = 32
PAGE_MOST = 256
TOKENS = 4096
N_DP = 8


def block_levels(key, shape, shards, low, high):
    def one(axis_at, blocks):
        steps = jax.random.uniform(jax.random.fold_in(jax.random.fold_in(key, 6), axis_at), (blocks,), jnp.float32, low / len(shards), high / len(shards))
        return jnp.repeat(jnp.exp(steps), shape[axis_at] // blocks).reshape((-1,) + (1,) * (len(shape) - axis_at - 1))

    loudness = one(*shards[0])
    for cut in shards[1:]:
        loudness = loudness * one(*cut)
    return loudness


def profile(number_of, total, most, slope):
    portions = [(1 << 20) // math.isqrt(standing ** slope) + 1 for standing in range(2, number_of + 1)]
    spare, holding = total - most - (number_of - 1), [1] * (number_of - 1)
    while spare > 0:
        candidates = [i for i in range(number_of - 1) if holding[i] < most]
        whole, budget = sum([portions[i] for i in candidates]), spare
        for i in candidates:
            addition = min(most - holding[i], max(1, budget * portions[i] // whole), spare)
            holding[i] = holding[i] + addition
            spare = spare - addition
    return np.array([most] + holding)


def ragged(stream_key, amount, total, most, skew):
    if amount == 2:
        one = jax.random.randint(stream_key, (), max(1, total - most), min(most, total - 1) + 1)
        return jnp.stack([one, total - one])
    tallies = jnp.asarray(profile(amount, total, most, skew), jnp.int32)
    pairs = (amount - 1) // 2
    donor, taker = tallies[1:1 + 2 * pairs:2], tallies[2:2 + 2 * pairs:2]
    room = jnp.minimum(donor - 1, most - taker)
    moved = jax.random.randint(jax.random.fold_in(stream_key, 1), (pairs,), 0, 1 << 20) % (room + 1)
    tallies = tallies.at[1:1 + 2 * pairs:2].set(donor - moved).at[2:2 + 2 * pairs:2].set(taker + moved)
    return tallies[jax.random.permutation(jax.random.fold_in(stream_key, 2), amount)]


def noise(stream_key, shape, scale, most, pieces=(), held_as=jnp.bfloat16):
    array = scale * jax.random.normal(stream_key, shape, jnp.float32)
    if pieces:
        array = array * block_levels(stream_key, shape, pieces, -0.22, 0.18)
    return jnp.clip(array, -most, most).astype(held_as)


def setup_inputs(seed: int = 0) -> dict:
    seeds = jax.random.split(jax.random.key(seed), 12)
    return {
        "tokens": noise(seeds[0], (TOKENS, D), 1.0, 6.0, ((0, 32),)),
        "page_lengths": jax.vmap(lambda own: ragged(own, PAGES, TOK_DEV, PAGE_MOST, 2))(jax.random.split(seeds[1], N_DP)).reshape((N_DP, PAGES)).astype(jnp.int32),
        "norm_gains": jnp.clip(1.0 + 0.18 * jax.random.normal(seeds[2], (2, D), jnp.float32), 0.1, 1.9),
        "norm_biases": noise(seeds[3], (2, D), 0.3, 1.5, (), jnp.float32),
        "layer_scales": jnp.clip(jnp.exp(jax.random.uniform(seeds[4], (2, D), jnp.float32, math.log(0.5), math.log(2.0))), 0.5, 2.0),
        "w_qkv": noise(seeds[5], (D, 3, D), (D // 2) ** -0.5, 0.3125, ((2, 4),)),
        "rel_table": noise(seeds[6], (BUCKETS, HEADS), 1.0, 4.0, (), jnp.float32),
        "w_out": noise(seeds[7], (D, D), (D // 16) ** -0.5, 0.875, ((0, 4),)),
        "w_up": noise(seeds[8], (D, FF), D ** -0.5, 0.21875, ((1, 4),)),
        "w_down": noise(seeds[9], (FF, D), FF ** -0.5, 0.109375, ((0, 4),)),
        "cotangent": noise(seeds[10], (TOKENS, D), 1.0, 6.0, ((0, 32),)),
    }


@jax.custom_vjp
def low(v):
    return lax.optimization_barrier(v.astype(jnp.bfloat16)).astype(jnp.float32)

@jax.custom_vjp
def low_back(v):
    return v

def low_keep(v):
    return (low(v), None)

def low_pass(kept, grad):
    return (grad,)

def back_keep(v):
    return (v, None)

def back_low(kept, grad):
    return (low(grad),)
low.defvjp(low_keep, low_pass)
low_back.defvjp(back_keep, back_low)
norm_eps = 1e-06
masked_score = -1000000000.0

def layer_norm(values, norm_gain, norm_shift):
    row_mean = lax.optimization_barrier(jnp.mean(values, axis=-1, keepdims=True))
    centred = values - row_mean
    spread = lax.optimization_barrier(jnp.mean(centred * centred, axis=-1, keepdims=True))
    return centred * lax.rsqrt(spread + norm_eps) * norm_gain + norm_shift

def gelu_exact(values):
    return jax.nn.gelu(values, approximate=False)

def page_layout(page_lengths, group_rows):
    page_ends = jnp.cumsum(page_lengths, dtype=jnp.int32)
    positions = jnp.arange(group_rows, dtype=jnp.int32)
    segment = lax.optimization_barrier(jnp.sum((positions[:, None] >= page_ends[None, :]).astype(jnp.int32), axis=1, dtype=jnp.int32))
    live_rows = segment < page_lengths.shape[0] - 1
    return (positions, segment, live_rows)

def bucket_offsets(query_pos, key_pos, buckets):
    half_span = buckets // 2
    return jnp.clip(query_pos[:, None] - key_pos[None, :], -half_span, half_span - 1) + half_span

def shard_forward(params, inputs):
    norm_gains, norm_biases, layer_scales, w_qkv, rel_table, w_out, w_up, w_down = params
    x_rows, page_lengths = inputs
    highest = lax.Precision.HIGHEST
    group_rows = x_rows.shape[0]
    positions, segment, live_rows = page_layout(page_lengths, group_rows)
    first_input = low(layer_norm(x_rows, norm_gains[0], norm_biases[0]))
    packed = low(low_back(jnp.einsum('td,dce->tce', first_input, w_qkv, precision=highest)))
    packed = packed.reshape(group_rows, 3, HEADS, HEAD_DIM)
    queries = packed[:, 0]
    key_rows = packed[:, 1]
    value_rows = packed[:, 2]
    block_rows = min(512, group_rows)
    score_scale = HEAD_DIM ** (-0.5)
    labels = jnp.arange(BUCKETS, dtype=jnp.int32)

    def attend(start_row):
        query_block = lax.dynamic_slice_in_dim(queries, start_row, block_rows, 0)
        raw_scores = jnp.einsum('qhe,khe->hqk', query_block, key_rows, precision=highest) * score_scale
        query_pos = start_row + jnp.arange(block_rows, dtype=jnp.int32)
        offsets = bucket_offsets(query_pos, positions, BUCKETS)
        one_hot = (offsets[:, :, None] == labels).astype(jnp.float32)
        bias_terms = jnp.einsum('qkb,bh->hqk', one_hot, rel_table, precision=highest)
        raw_scores = low_back(raw_scores + bias_terms)
        query_page = lax.dynamic_slice_in_dim(segment, start_row, block_rows, 0)
        allowed = (query_page[:, None] == segment[None, :]) & live_rows[None, :]
        scores = jnp.where(allowed[None], raw_scores, masked_score)
        row_top = lax.optimization_barrier(jnp.max(scores, axis=-1, keepdims=True))
        raised = jnp.exp(scores - row_top)
        weights = low(raised / lax.optimization_barrier(jnp.sum(raised, axis=-1, keepdims=True)))
        mixed_rows = jnp.einsum('hqk,khe->qhe', weights, value_rows, precision=highest)
        query_live = lax.dynamic_slice_in_dim(live_rows, start_row, block_rows, 0)
        return jnp.where(query_live[:, None, None], mixed_rows, 0.0)
    starts = jnp.arange(group_rows // block_rows, dtype=jnp.int32) * block_rows
    mixed_all = lax.map(jax.checkpoint(attend), starts)
    attended = low(low_back(mixed_all.reshape(group_rows, D)))
    attn_rows = low_back(jnp.dot(attended, w_out, precision=highest))
    middle = x_rows + layer_scales[0] * attn_rows
    second_input = low(layer_norm(middle, norm_gains[1], norm_biases[1]))
    up_rows = low_back(jnp.dot(second_input, w_up, precision=highest))
    act_rows = low(gelu_exact(up_rows))
    mlp_rows = low_back(jnp.dot(act_rows, w_down, precision=highest))
    return middle + layer_scales[1] * mlp_rows

def reference(tokens, page_lengths, norm_gains, norm_biases, layer_scales, w_qkv, rel_table, w_out, w_up, w_down, cotangent):
    params = (norm_gains.astype(jnp.float32), norm_biases.astype(jnp.float32), layer_scales.astype(jnp.float32), w_qkv.astype(jnp.float32), rel_table.astype(jnp.float32), w_out.astype(jnp.float32), w_up.astype(jnp.float32), w_down.astype(jnp.float32))
    inputs_all = tokens.astype(jnp.float32).reshape(N_DP, TOK_DEV, D)
    checked = jax.checkpoint(shard_forward)

    def forward(x_all, weights_all):

        def shard_step(carried, inputs):
            return (carried, checked(weights_all, (inputs[0], inputs[1])))
        unused, outputs = lax.scan(shard_step, jnp.zeros((), jnp.float32), (x_all, page_lengths))
        return outputs
    outputs, pullback = jax.vjp(forward, inputs_all, params)
    input_grad, param_grads = pullback(cotangent.astype(jnp.float32).reshape(N_DP, TOK_DEV, D))
    return (outputs.reshape(TOKENS, D).astype(jnp.bfloat16), input_grad.reshape(TOKENS, D).astype(jnp.bfloat16), param_grads[0], param_grads[1], param_grads[2], param_grads[3], param_grads[4], param_grads[5], param_grads[6], param_grads[7])
```

```python
import jax
import jax.numpy as jnp
from jax import lax
from jax.experimental import pallas as pl
from jax.experimental.pallas import tpu as pltpu
from jax.sharding import PartitionSpec as P

HEAD_DIM = 64
norm_eps = 1e-06
masked_score = -1000000000.0
F32 = jnp.float32
BF16 = jnp.bfloat16
SMEM = pl.BlockSpec(memory_space=pltpu.SMEM)
VMEM = pl.BlockSpec(memory_space=pltpu.VMEM)
CHUNK = 64
GAIN0, BIAS0, GAIN1, BIAS1, SCALE0, SCALE1 = range(6)


def call(kernel, outs, args, n_smem=0, scratch=(), flops=0, limit=40):
    moved = sum(a.size * a.dtype.itemsize for a in args) + sum(
        o.size * o.dtype.itemsize for o in outs
    )
    return pl.pallas_call(
        kernel,
        out_shape=tuple(outs),
        in_specs=[SMEM] * n_smem + [VMEM] * (len(args) - n_smem),
        out_specs=tuple([VMEM] * len(outs)),
        scratch_shapes=list(scratch),
        compiler_params=pltpu.CompilerParams(vmem_limit_bytes=limit << 20),
        cost_estimate=pl.CostEstimate(flops=flops, bytes_accessed=moved, transcendentals=0),
    )(*args)


def like(shape, dtype):
    return jax.ShapeDtypeStruct(shape, dtype)


def nn(a, b):
    return lax.dot_general(a, b, (((1,), (0,)), ((), ())), preferred_element_type=F32)


def nt(a, b):
    return lax.dot_general(a, b, (((1,), (1,)), ((), ())), preferred_element_type=F32)


def fold(v):
    return jnp.sum(v.reshape(v.shape[0] // 8, 8, v.shape[1]), axis=0)


def across(v):
    return jnp.sum(v, axis=0, keepdims=True)


def passes(rows, step, start):
    return lax.fori_loop(0, rows // CHUNK, step, start)


def chunk(i):
    return pl.ds(pl.multiple_of(i * CHUNK, CHUNK), CHUNK)


def page_ids(lengths, shape, axis, dead):
    at = lax.broadcasted_iota(jnp.int32, shape, axis)
    page = jnp.zeros(shape, jnp.int32)
    end = jnp.int32(0)
    pages = lengths.shape[1]
    for p in range(pages):
        end = end + lengths[0, p]
        page = page + (at >= end).astype(jnp.int32)
    return jnp.where(page < pages - 1, page, dead)


def turn_kernel(wq, wu, wd, wq_o, wu_o, wd_o):
    wq_o[...] = wq[...].T
    wu_o[...] = wu[...].T
    wd_o[...] = wd[...].T


def out_weight_kernel(place, *refs):
    pieces, (w_o, wt_o) = refs[:-2], refs[-2:]
    m, d = place[0], place[1]
    rows, cols = pieces[0].shape[-2:]
    shard = rows * 4
    n = 0
    for c in range(2):
        for b in range(4):
            s = d ^ (c + 2 * b)
            half = s & 1
            quarter = (s >> 1) & 3
            ref = pieces[n]
            n += 1
            for k in range(4):
                at = pl.multiple_of((m ^ k) * shard + quarter * rows, 16)
                w_o[pl.ds(at, rows), pl.ds(pl.multiple_of(half * cols, 128), cols)] = ref[k]
    wt_o[...] = w_o[...].T


def head_kernel(
    place, lengths, table, x0, x1, x2, x3, cols, wq,
    xt_o, h1_o, stat_o, qkv_o, pt_o, att_o,
    score, ids, pattern,
):
    m = place[0]
    rows = x0.shape[0]
    width, tokens = xt_o.shape
    channels = att_o.shape[0]
    heads = channels // HEAD_DIM
    buckets = table.shape[0]
    half = buckets // 2
    for k, ref in enumerate((x0, x1, x2, x3)):
        at = pl.multiple_of((m ^ k) * rows, rows)
        xt_o[:, pl.ds(at, rows)] = ref[...].T

    def add(i, acc):
        return acc + fold(xt_o[chunk(i), :].astype(F32))

    zero = jnp.zeros((8, tokens), F32)
    mean = across(passes(width, add, zero)) / width

    def spread(i, acc):
        v = xt_o[chunk(i), :].astype(F32) - mean
        return acc + fold(v * v)

    rstd = lax.rsqrt(across(passes(width, spread, zero)) / width + norm_eps)
    stat_o[0:1, :] = mean
    stat_o[1:2, :] = rstd

    def norm(i, carry):
        v = (xt_o[chunk(i), :].astype(F32) - mean) * rstd
        w = cols[chunk(i), :]
        h1_o[chunk(i), :] = (v * w[:, GAIN0 : GAIN0 + 1] + w[:, BIAS0 : BIAS0 + 1]).astype(BF16)
        return carry

    passes(width, norm, 0)
    qkv_o[...] = nn(wq[...], h1_o[...]).astype(BF16)
    qkv_o[0:channels, :] = qkv_o[0:channels, :] * BF16(HEAD_DIM**-0.5)

    ids[...] = page_ids(lengths, ids.shape, 0, -2)
    own_ids = page_ids(lengths, (1, tokens), 1, -1)
    live = (own_ids >= 0).astype(F32)
    blk = 128
    n_blk = tokens // blk
    off = lax.broadcasted_iota(jnp.int32, (blk, blk), 1) - lax.broadcasted_iota(
        jnp.int32, (blk, blk), 0
    )

    def one_head(h, carry):
        col = m * heads + h
        low, high = table[0, col], table[buckets - 1, col]
        near = jnp.where(off >= half - 1, high, low)
        for b in range(1, buckets - 1):
            near = jnp.where(off == b - half, table[b, col], near)
        pattern[1] = near
        before = jnp.full((blk, blk), low, F32)
        for b in range(1, half):
            before = jnp.where(off - blk == b - half, table[b, col], before)
        pattern[0] = before
        after = jnp.full((blk, blk), high, F32)
        for b in range(half + 1, buckets - 1):
            after = jnp.where(off + blk == b - half, table[b, col], after)
        pattern[2] = after

        def rows_of(which):
            return pl.ds(pl.multiple_of(which * channels + h * HEAD_DIM, HEAD_DIM), HEAD_DIM)

        q, k, v = qkv_o[rows_of(0), :], qkv_o[rows_of(1), :], qkv_o[rows_of(2), :]
        score[...] = nn(k.T, q)
        for i in range(n_blk):
            lanes = slice(i * blk, (i + 1) * blk)
            query_id = own_ids[:, lanes]
            top = jnp.full((8, blk), -3e38, F32)
            for j in range(n_blk):
                at = slice(j * blk, (j + 1) * blk)
                if abs(i - j) <= 1:
                    bias = pattern[i - j + 1]
                else:
                    bias = low if i < j else high
                s = jnp.where(ids[at, :] == query_id, score[at, lanes] + bias, masked_score)
                score[at, lanes] = s
                top = jnp.maximum(top, jnp.max(s.reshape(blk // 8, 8, blk), axis=0))
            top = jnp.max(top, axis=0, keepdims=True)
            total = jnp.zeros((8, blk), F32)
            for j in range(n_blk):
                at = slice(j * blk, (j + 1) * blk)
                e = jnp.exp(score[at, lanes] - top)
                score[at, lanes] = e
                total = total + fold(e)
            scale = 1.0 / across(total)
            for j in range(n_blk):
                at = slice(j * blk, (j + 1) * blk)
                pt_o[h, at, lanes] = (score[at, lanes] * scale).astype(BF16)
        mixed = nn(v, pt_o[h]) * live
        att_o[pl.ds(pl.multiple_of(h * HEAD_DIM, HEAD_DIM), HEAD_DIM), :] = mixed.astype(BF16)
        return carry

    lax.fori_loop(0, heads, one_head, 0)


def middle_kernel(
    place, a0, a1, a2, a3, c0, c1, c2, c3, xt, cols, w_out, w_out_t, w_up, w_up_t, w_down,
    d0, d1, d2, d3, nb_o, h2_o, act_o, dup_o, gm_o, ga_o, at_o, dy_o, mid_o, vec_o,
    attn, mid, wide, other, sums,
):
    m = place[0]
    rows = c0.shape[0]
    channels = a0.shape[0]
    width, tokens = xt.shape
    hidden = w_up.shape[1]
    for k, (a, c) in enumerate(zip((a0, a1, a2, a3), (c0, c1, c2, c3))):
        at_o[pl.ds(pl.multiple_of((m ^ k) * channels, channels), channels), :] = a[...]
        dy_o[:, pl.ds(pl.multiple_of((m ^ k) * rows, rows), rows)] = c[...].T
    attn[...] = nn(w_out_t[...], at_o[...])
    zero = jnp.zeros((8, tokens), F32)

    def residual(i, acc):
        w = cols[chunk(i), :]
        v = xt[chunk(i), :].astype(F32) + w[:, SCALE0 : SCALE0 + 1] * attn[chunk(i), :]
        mid[chunk(i), :] = v
        gm_o[chunk(i), :] = (
            dy_o[chunk(i), :].astype(F32) * w[:, SCALE1 : SCALE1 + 1]
        ).astype(BF16)
        return acc + fold(v)

    mean = across(passes(width, residual, zero)) / width
    mid_o[...] = mid[:, pl.ds(pl.multiple_of(m * rows, rows), rows)]

    def spread(i, acc):
        v = mid[chunk(i), :] - mean
        return acc + fold(v * v)

    rstd = lax.rsqrt(across(passes(width, spread, zero)) / width + norm_eps)

    def norm(i, carry):
        w = cols[chunk(i), :]
        v = (mid[chunk(i), :] - mean) * rstd
        mid[chunk(i), :] = v
        h2_o[chunk(i), :] = (v * w[:, GAIN1 : GAIN1 + 1] + w[:, BIAS1 : BIAS1 + 1]).astype(BF16)
        return carry

    passes(width, norm, 0)
    wide[...] = nn(w_up_t[...], h2_o[...])
    other[...] = nn(w_down[...], gm_o[...])

    def gelu(i, carry):
        u = wide[chunk(i), :]
        cdf = 0.5 + 0.5 * lax.erf(u * (0.5**0.5))
        act_o[chunk(i), :] = (u * cdf).astype(BF16)
        slope = cdf + u * (jnp.exp(-0.5 * u * u) * 0.3989422804014327)
        dup_o[chunk(i), :] = (slope * other[chunk(i), :]).astype(BF16)
        return carry

    passes(hidden, gelu, 0)
    wide[...] = nn(w_up[...], dup_o[...])

    def gather(i, acc):
        d = wide[chunk(i), :]
        hat = mid[chunk(i), :]
        u = d * cols[chunk(i), :][:, GAIN1 : GAIN1 + 1]
        sums[chunk(i), 0:1] = jnp.sum(d * hat, axis=1, keepdims=True)
        sums[chunk(i), 1:2] = jnp.sum(d, axis=1, keepdims=True)
        return acc[0] + fold(u), acc[1] + fold(u * hat)

    first, second = passes(width, gather, (zero, zero))
    first, second = across(first) / width, across(second) / width
    lane = lax.broadcasted_iota(jnp.int32, (1, tokens), 1)
    mine = ((lane >= m * rows) & (lane < (m + 1) * rows)).astype(F32)

    def back(i, carry):
        w = cols[chunk(i), :]
        u = wide[chunk(i), :] * w[:, GAIN1 : GAIN1 + 1]
        v = rstd * (u - first - mid[chunk(i), :] * second)
        nb_o[chunk(i), :] = v
        v = v + mine * dy_o[chunk(i), :].astype(F32)
        sums[chunk(i), 2:3] = jnp.sum(v * attn[chunk(i), :], axis=1, keepdims=True)
        ga_o[chunk(i), :] = (v * w[:, SCALE0 : SCALE0 + 1]).astype(BF16)
        return carry

    passes(width, back, 0)
    other[...] = nn(w_out[...], ga_o[...])
    for k, ref in enumerate((d0, d1, d2, d3)):
        ref[...] = other[
            pl.ds(pl.multiple_of((m ^ k) * channels, channels), channels), :
        ].astype(BF16)
    turned = sums[...].T
    vec_o[...] = jnp.zeros(vec_o.shape, F32)
    vec_o[1:2, :] = turned[0:1, :]
    vec_o[3:4, :] = turned[1:2, :]
    vec_o[4:5, :] = turned[2:3, :]


def mlp_kernel(
    place, vec, act, dup, gm, ga, att, h2, dy, w_down_t,
    m0, m1, m2, m3, g_o, vec_o,
    mlp, sums,
):
    m = place[0]
    rows = m0.shape[1]
    width, tokens = dy.shape
    mlp[...] = nn(w_down_t[...], act[...])
    for k, ref in enumerate((m0, m1, m2, m3)):
        ref[...] = mlp[:, pl.ds(pl.multiple_of((m ^ k) * rows, rows), rows)].astype(BF16)

    def scale(i, carry):
        v = dy[chunk(i), :].astype(F32) * mlp[chunk(i), :]
        sums[chunk(i), 0:1] = jnp.sum(v, axis=1, keepdims=True)
        return carry

    passes(width, scale, 0)
    vec_o[...] = vec[...]
    vec_o[5:6, :] = sums[...].T[0:1, :]
    hidden = act.shape[0]
    g_o[:, 0:hidden] = nt(h2[...], dup[...]).astype(BF16)
    g_o[:, hidden : 2 * hidden] = nt(gm[...], act[...]).astype(BF16)
    g_o[:, 2 * hidden : 2 * hidden + width] = nt(ga[...], att[...]).astype(BF16)


def back_kernel(
    place, lengths, d0, d1, d2, d3, qkv, pt, xt, stat, nb, cols, wq_t, vec,
    p0, p1, p2, p3, dqkv_o, vec_o,
    score, ds, acc, buckets_of, wide, sums,
):
    m = place[0]
    channels, tokens = d0.shape
    heads = channels // HEAD_DIM
    width = xt.shape[0]
    rows = p0.shape[1]
    blk = 128
    n_blk = tokens // blk
    n_rows = buckets_of.shape[0]
    buckets = n_rows // heads
    half = buckets // 2
    live = (page_ids(lengths, (1, tokens), 1, -1) >= 0).astype(F32)
    off = lax.broadcasted_iota(jnp.int32, (blk, blk), 1) - lax.broadcasted_iota(
        jnp.int32, (blk, blk), 0
    )

    def one_head(h, carry):
        def rows_of(which):
            return pl.ds(pl.multiple_of(which * channels + h * HEAD_DIM, HEAD_DIM), HEAD_DIM)

        q, k, v = qkv[rows_of(0), :], qkv[rows_of(1), :], qkv[rows_of(2), :]
        mine = rows_of(0)
        d_att = (
            d0[mine, :].astype(F32) + d1[mine, :].astype(F32)
            + d2[mine, :].astype(F32) + d3[mine, :].astype(F32)
        )
        d_att = (d_att.astype(BF16).astype(F32) * live).astype(BF16)
        dqkv_o[rows_of(2), :] = nt(d_att, pt[h]).astype(BF16)
        score[...] = nn(v.T, d_att)
        acc[...] = jnp.zeros(acc.shape, F32)
        for i in range(n_blk):
            lanes = slice(i * blk, (i + 1) * blk)
            total = jnp.zeros((8, blk), F32)
            for j in range(n_blk):
                at = slice(j * blk, (j + 1) * blk)
                prod = score[at, lanes] * pt[h, at, lanes].astype(F32)
                score[at, lanes] = prod
                total = total + fold(prod)
            total = across(total)
            for j in range(n_blk):
                at = slice(j * blk, (j + 1) * blk)
                g = score[at, lanes] - pt[h, at, lanes].astype(F32) * total
                g = g.astype(BF16)
                ds[at, lanes] = g
                slot = max(min(i - j, 2), -2) + 2
                acc[slot] = acc[slot] + g.astype(F32)
        dqkv_o[rows_of(0), :] = (nn(k, ds[...]) * HEAD_DIM**-0.5).astype(BF16)
        dqkv_o[rows_of(1), :] = nt(q, ds[...]).astype(BF16)
        near, before, after = acc[2], acc[1], acc[3]
        corner_b, off_b = before[0:16, :], off[0:16, :] - blk
        corner_a, off_a = after[blk - 16 : blk, :], off[blk - 16 : blk, :] + blk
        first = h * buckets
        for b in range(buckets):
            if b == 0:
                v = fold(acc[0]) + fold(jnp.where(off - blk <= -half, before, 0.0))
                v = v + fold(jnp.where(off <= -half, near, 0.0))
            elif b == buckets - 1:
                v = fold(acc[4]) + fold(jnp.where(off + blk >= half - 1, after, 0.0))
                v = v + fold(jnp.where(off >= half - 1, near, 0.0))
            else:
                v = fold(jnp.where(off == b - half, near, 0.0))
                if b < half:
                    v = v + fold(jnp.where(off_b == b - half, corner_b, 0.0))
                elif b > half:
                    v = v + fold(jnp.where(off_a == b - half, corner_a, 0.0))
            buckets_of[pl.ds(first + b, 1), :] = across(v)
        return carry

    lax.fori_loop(0, heads, one_head, 0)
    wide[...] = nn(wq_t[...], dqkv_o[...])
    mean, rstd = stat[0:1, :], stat[1:2, :]
    zero = jnp.zeros((8, tokens), F32)

    def gather(i, part):
        d = wide[chunk(i), :]
        hat = (xt[chunk(i), :].astype(F32) - mean) * rstd
        u = d * cols[chunk(i), :][:, GAIN0 : GAIN0 + 1]
        sums[chunk(i), 0:1] = jnp.sum(d * hat, axis=1, keepdims=True)
        sums[chunk(i), 1:2] = jnp.sum(d, axis=1, keepdims=True)
        return part[0] + fold(u), part[1] + fold(u * hat)

    first, second = passes(width, gather, (zero, zero))
    first, second = across(first) / width, across(second) / width

    def back(i, carry):
        hat = (xt[chunk(i), :].astype(F32) - mean) * rstd
        u = wide[chunk(i), :] * cols[chunk(i), :][:, GAIN0 : GAIN0 + 1]
        wide[chunk(i), :] = nb[chunk(i), :] + rstd * (u - first - hat * second)
        return carry

    passes(width, back, 0)
    for k, ref in enumerate((p0, p1, p2, p3)):
        ref[...] = wide[:, pl.ds(pl.multiple_of((m ^ k) * rows, rows), rows)].astype(ref.dtype)
    turned = sums[...].T
    vec_o[...] = vec[...]
    vec_o[0:1, :] = turned[0:1, :]
    vec_o[2:3, :] = turned[1:2, :]
    each = jnp.sum(buckets_of[...], axis=1, keepdims=True)
    shape = (n_rows, width)
    lane = lax.broadcasted_iota(jnp.int32, shape, 1)
    row = lax.broadcasted_iota(jnp.int32, shape, 0)
    vec_o[6:7, :] = across(jnp.where(lane == row + m * n_rows, each, 0.0))


def qkv_grad_kernel(h1, dqkv, g_o):
    g_o[...] = nt(h1[...], dqkv[...]).astype(BF16)


def input_kernel(p0, p1, p2, p3, dy, out):
    total = p0[...] + p1[...].astype(F32) + p2[...].astype(F32) + p3[...].astype(F32)
    out[...] = (dy[...].astype(F32) + total.T).astype(BF16)


def output_kernel(m0, m1, m2, m3, mid, cols, out):
    total = m0[...].astype(F32) + m1[...].astype(F32) + m2[...].astype(F32) + m3[...].astype(F32)
    out[...] = (mid[...] + cols[:, SCALE1 : SCALE1 + 1] * total).T.astype(BF16)


def body(
    tokens,
    page_lengths,
    norm_gains,
    norm_biases,
    layer_scales,
    w_qkv,
    rel_table,
    w_out,
    w_up,
    w_down,
    cotangent,
):
    mp, dp = lax.axis_size("mp"), lax.axis_size("dp")
    rows, width = tokens.shape
    group = rows * mp
    channels = w_qkv.shape[2]
    hidden = w_up.shape[1]
    heads = channels // HEAD_DIM
    buckets = rel_table.shape[0]
    m, d = lax.axis_index("mp"), lax.axis_index("dp")
    place = jnp.stack([m, d]).astype(jnp.int32)

    def swap(v, k, axis="mp"):
        n = mp if axis == "mp" else dp
        return lax.ppermute(v, axis, [(i, i ^ k) for i in range(n)])

    def gathered(v):
        return [v] + [swap(v, k) for k in range(1, mp)]

    cols = jnp.concatenate(
        [norm_gains[0:1], norm_biases[0:1], norm_gains[1:2], norm_biases[1:2], layer_scales]
    ).T
    wq = jnp.transpose(w_qkv, (1, 2, 0)).reshape(3 * channels, width)

    x = gathered(tokens)

    piece_rows, piece_cols = channels // 4, width // 2
    piece = lax.dynamic_slice(
        w_out, (((d >> 1) & 3) * piece_rows, (d & 1) * piece_cols), (piece_rows, piece_cols)
    )
    part = jnp.stack(gathered(piece))
    one = swap(part, 4, "dp")
    two = swap(jnp.stack([part, one]), 2, "dp")
    mine4 = jnp.stack([part, two[0], one, two[1]])
    three = swap(mine4, 1, "dp")
    pieces = [mine4[i] for i in range(4)] + [three[i] for i in range(4)]
    w_out_full, w_out_t = call(
        out_weight_kernel,
        [like((width, width), BF16)] * 2,
        [place] + pieces,
        n_smem=1,
    )
    wq_t, w_up_t, w_down_t = call(
        turn_kernel,
        [like((width, 3 * channels), BF16), like((hidden, width), BF16), like((width, hidden), BF16)],
        [wq, w_up, w_down],
    )

    cot_after, x3 = lax.optimization_barrier((cotangent, x[3]))
    x[3] = x3
    dy = gathered(cot_after)
    xt, h1, stat, qkv, pt, att = call(
        head_kernel,
        [
            like((width, group), BF16),
            like((width, group), BF16),
            like((8, group), F32),
            like((3 * channels, group), BF16),
            like((heads, group, group), BF16),
            like((channels, group), BF16),
        ],
        [place, page_lengths, rel_table] + x + [cols, wq],
        n_smem=3,
        scratch=[
            pltpu.VMEM((group, group), F32),
            pltpu.VMEM((group, 128), jnp.int32),
            pltpu.VMEM((3, 128, 128), F32),
        ],
        flops=2 * group * width * 3 * channels + 4 * heads * group * group * HEAD_DIM,
    )
    atts = gathered(att)
    act_like = like((width, group), BF16)
    hid_like = like((hidden, group), BF16)
    d0, d1, d2, d3, nb, h2, act, dup, gm, ga, att_all, dy_t, mid, vec = call(
        middle_kernel,
        [like((channels, group), BF16)] * 4
        + [like((width, group), F32), act_like, hid_like, hid_like, act_like, act_like]
        + [act_like, act_like, like((width, rows), F32), like((8, width), F32)],
        [place] + atts + dy + [xt, cols, w_out_full, w_out_t, w_up, w_up_t, w_down],
        n_smem=1,
        scratch=[
            pltpu.VMEM((width, group), F32),
            pltpu.VMEM((width, group), F32),
            pltpu.VMEM((hidden, group), F32),
            pltpu.VMEM((hidden, group), F32),
            pltpu.VMEM((width, 128), F32),
        ],
        flops=10 * width * width * group,
    )
    d_att = [d0] + [swap(v, k) for k, v in ((1, d1), (2, d2), (3, d3))]
    m0, m1, m2, m3, grads, vec = call(
        mlp_kernel,
        [like((width, rows), BF16)] * 4
        + [like((width, 2 * hidden + width), BF16), like((8, width), F32)],
        [place, vec, act, dup, gm, ga, att_all, h2, dy_t, w_down_t],
        n_smem=1,
        scratch=[pltpu.VMEM((width, group), F32), pltpu.VMEM((width, 128), F32)],
        flops=8 * width * width * group,
    )
    mlp = [m0] + [swap(v, k) for k, v in ((1, m1), (2, m2), (3, m3))]

    p0, p1, p2, p3, dqkv, vec = call(
        back_kernel,
        [like((width, rows), F32)]
        + [like((width, rows), BF16)] * 3
        + [like((3 * channels, group), BF16), like((8, width), F32)],
        [place, page_lengths] + d_att + [qkv, pt, xt, stat, nb, cols, wq_t, vec],
        n_smem=2,
        scratch=[
            pltpu.VMEM((group, group), F32),
            pltpu.VMEM((group, group), BF16),
            pltpu.VMEM((5, 128, 128), F32),
            pltpu.VMEM((heads * buckets, 128), F32),
            pltpu.VMEM((width, group), F32),
            pltpu.VMEM((width, 128), F32),
        ],
        flops=2 * group * width * 3 * channels + 8 * heads * group * group * HEAD_DIM,
    )
    back = [p0] + [swap(v, k) for k, v in ((1, p1), (2, p2), (3, p3))]
    (qkv_grads,) = call(
        qkv_grad_kernel,
        [like((width, 3 * channels), BF16)],
        [h1, dqkv],
        flops=2 * group * width * 3 * channels,
    )

    def reduced(g):
        g = g.reshape(dp, width // dp, g.shape[1])
        bit = 1
        while bit < dp:
            g = g.reshape(g.shape[0] // 2, 2, width // dp, g.shape[-1])
            here = (d & bit) // bit
            sent = lax.dynamic_index_in_dim(g, 1 - here, 1, keepdims=False)
            kept = lax.dynamic_index_in_dim(g, here, 1, keepdims=False)
            g = kept.astype(F32) + swap(sent, bit, "dp").astype(F32)
            bit *= 2
            if bit < dp:
                g = g.astype(BF16)
        return g[0]

    grads = reduced(grads)
    qkv_grads = reduced(qkv_grads)
    out_grad = grads[:, 2 * hidden :]

    def out_part(k):
        return lax.dynamic_slice_in_dim(out_grad, (m ^ k) * channels, channels, 1)

    out_sum = out_part(0)
    for k in range(1, mp):
        out_sum = out_sum + swap(out_part(k).astype(BF16), k).astype(F32)

    bit = 1
    while bit < dp:
        vec = vec + swap(vec, bit, "dp")
        bit *= 2
    for k in (1, 2):
        vec = vec + swap(vec, k)

    (output,) = call(output_kernel, [like((rows, width), BF16)], mlp + [mid, cols])
    (grad_input,) = call(input_kernel, [like((rows, width), BF16)], back + [cotangent])
    grad_table = vec[6, : heads * mp * buckets].reshape(heads * mp, buckets).T
    return (
        output,
        grad_input,
        vec[0:2],
        vec[2:4],
        vec[4:6],
        qkv_grads.reshape(width // dp, 3, channels),
        grad_table,
        out_sum.T,
        grads[:, :hidden],
        grads[:, hidden : 2 * hidden].T,
    )


def solution(mesh):
    placed = (
        P(("dp", "mp"), None),
        P("dp", None),
        P(),
        P(),
        P(),
        P(None, None, "mp"),
        P(),
        P("mp", None),
        P(None, "mp"),
        P("mp", None),
        P(("dp", "mp"), None),
    )
    return jax.shard_map(
        body,
        mesh=mesh,
        in_specs=placed,
        out_specs=(
            P(("dp", "mp"), None),
            P(("dp", "mp"), None),
            P(),
            P(),
            P(),
            P("dp", None, "mp"),
            P(),
            P("mp", "dp"),
            P("dp", "mp"),
            P("mp", "dp"),
        ),
        check_vma=False,
    )
```

```python
import jax
import jax.numpy as jnp
from jax import lax
from jax.experimental import pallas as pl
from jax.experimental.pallas import tpu as pltpu
from jax.sharding import PartitionSpec as P

HEAD_DIM = 64
SPEED = 1.15e9
norm_eps = 1e-06
masked_score = -1000000000.0
F32 = jnp.float32
BF16 = jnp.bfloat16
SMEM = pl.BlockSpec(memory_space=pltpu.SMEM)
VMEM = pl.BlockSpec(memory_space=pltpu.VMEM)
CHUNK = 64
GAIN0, BIAS0, GAIN1, BIAS1, SCALE0, SCALE1 = range(6)


def call(kernel, outs, args, n_smem=0, scratch=(), us=0.01, limit=16):
    return pl.pallas_call(
        kernel,
        out_shape=tuple(outs),
        in_specs=[SMEM] * n_smem + [VMEM] * (len(args) - n_smem),
        out_specs=tuple([VMEM] * len(outs)),
        scratch_shapes=list(scratch),
        compiler_params=pltpu.CompilerParams(vmem_limit_bytes=limit << 20),
        name=kernel.__name__,
        cost_estimate=pl.CostEstimate(flops=int(us * SPEED), bytes_accessed=8, transcendentals=0),
    )(*args)


def like(shape, dtype):
    return jax.ShapeDtypeStruct(shape, dtype)


def nn(a, b):
    return lax.dot_general(a, b, (((1,), (0,)), ((), ())), preferred_element_type=F32)


def nt(a, b):
    return lax.dot_general(a, b, (((1,), (1,)), ((), ())), preferred_element_type=F32)


def fold(v):
    return jnp.sum(v.reshape(v.shape[0] // 8, 8, v.shape[1]), axis=0)


def across(v):
    return jnp.sum(v, axis=0, keepdims=True)


def passes(rows, step, start):
    return lax.fori_loop(0, rows // CHUNK, step, start)


def chunk(i):
    return pl.ds(pl.multiple_of(i * CHUNK, CHUNK), CHUNK)


def page_ids(lengths, shape, axis, dead):
    at = lax.broadcasted_iota(jnp.int32, shape, axis)
    page = jnp.zeros(shape, jnp.int32)
    end = jnp.int32(0)
    pages = lengths.shape[1]
    for p in range(pages):
        end = end + lengths[0, p]
        page = page + (at >= end).astype(jnp.int32)
    return jnp.where(page < pages - 1, page, dead)


def turn_kernel(wq, wu, wd, wq_o, wu_o, wd_o):
    wq_o[...] = wq[...].T
    wu_o[...] = wu[...].T
    wd_o[...] = wd[...].T


def message_kernel(place, tokens, w_out, out):
    d = place[1]
    rows, half = tokens.shape[0], tokens.shape[1] // 2
    n = w_out.shape[0] // 2
    out[0:rows, :] = tokens[:, :half]
    out[rows : 2 * rows, :] = tokens[:, half:]
    piece = w_out[pl.ds(pl.multiple_of(((d >> 1) & 1) * n, n), n), :]
    out[2 * rows :, :] = jnp.where((d & 1) == 0, piece[:, :half], piece[:, half:])


def pieces_kernel(x0, x1, x2, x3, out):
    n = out.shape[1]
    for k, ref in enumerate((x0, x1, x2, x3)):
        out[k] = ref[ref.shape[0] - n :, :]


def out_weight_kernel(place, p00, p01, p10, p11, w_o, wt_o):
    m, d = place[0], place[1]
    _, rows, cols = p00.shape
    for c, b, ref in ((0, 0, p00), (0, 1, p01), (1, 0, p10), (1, 1, p11)):
        half, part = (d & 1) ^ c, ((d >> 1) & 1) ^ b
        for k in range(4):
            at = pl.multiple_of((m ^ k) * 2 * rows + part * rows, rows)
            w_o[pl.ds(at, rows), pl.ds(pl.multiple_of(half * cols, cols), cols)] = ref[k]
    wt_o[...] = w_o[...].T


def head_kernel(
    place, lengths, table, x0, x1, x2, x3, cols, wq,
    xt_o, h1_o, stat_o, qkv_o, pt_o, att_o,
    score, ids, pattern,
):
    m = place[0]
    width, tokens = xt_o.shape
    rows = tokens // 4
    channels = att_o.shape[0]
    heads = channels // HEAD_DIM
    buckets = table.shape[0]
    half = buckets // 2
    for k, ref in enumerate((x0, x1, x2, x3)):
        at = pl.multiple_of((m ^ k) * rows, rows)
        xt_o[: width // 2, pl.ds(at, rows)] = ref[0:rows, :].T
        xt_o[width // 2 :, pl.ds(at, rows)] = ref[rows : 2 * rows, :].T

    def add(i, acc):
        return acc + fold(xt_o[chunk(i), :].astype(F32))

    zero = jnp.zeros((8, tokens), F32)
    mean = across(passes(width, add, zero)) / width

    def spread(i, acc):
        v = xt_o[chunk(i), :].astype(F32) - mean
        return acc + fold(v * v)

    rstd = lax.rsqrt(across(passes(width, spread, zero)) / width + norm_eps)
    stat_o[0:1, :] = mean
    stat_o[1:2, :] = rstd

    def norm(i, carry):
        v = (xt_o[chunk(i), :].astype(F32) - mean) * rstd
        w = cols[chunk(i), :]
        h1_o[chunk(i), :] = (v * w[:, GAIN0 : GAIN0 + 1] + w[:, BIAS0 : BIAS0 + 1]).astype(BF16)
        return carry

    passes(width, norm, 0)
    qkv_o[...] = nn(wq[...], h1_o[...]).astype(BF16)
    qkv_o[0:channels, :] = qkv_o[0:channels, :] * BF16(HEAD_DIM**-0.5)

    ids[...] = page_ids(lengths, ids.shape, 0, -2)
    own_ids = page_ids(lengths, (1, tokens), 1, -1)
    live = (own_ids >= 0).astype(F32)
    blk = 128
    n_blk = tokens // blk
    off = lax.broadcasted_iota(jnp.int32, (blk, blk), 1) - lax.broadcasted_iota(
        jnp.int32, (blk, blk), 0
    )

    def one_head(h, carry):
        col = m * heads + h
        low, high = table[0, col], table[buckets - 1, col]
        near = jnp.where(off >= half - 1, high, low)
        for b in range(1, buckets - 1):
            near = jnp.where(off == b - half, table[b, col], near)
        pattern[1] = near
        before = jnp.full((blk, blk), low, F32)
        for b in range(1, half):
            before = jnp.where(off - blk == b - half, table[b, col], before)
        pattern[0] = before
        after = jnp.full((blk, blk), high, F32)
        for b in range(half + 1, buckets - 1):
            after = jnp.where(off + blk == b - half, table[b, col], after)
        pattern[2] = after

        def rows_of(which):
            return pl.ds(pl.multiple_of(which * channels + h * HEAD_DIM, HEAD_DIM), HEAD_DIM)

        q, k, v = qkv_o[rows_of(0), :], qkv_o[rows_of(1), :], qkv_o[rows_of(2), :]
        score[...] = nn(k.T, q)
        for i in range(n_blk):
            lanes = slice(i * blk, (i + 1) * blk)
            query_id = own_ids[:, lanes]
            top = jnp.full((8, blk), -3e38, F32)
            for j in range(n_blk):
                at = slice(j * blk, (j + 1) * blk)
                if abs(i - j) <= 1:
                    bias = pattern[i - j + 1]
                else:
                    bias = low if i < j else high
                s = jnp.where(ids[at, :] == query_id, score[at, lanes] + bias, masked_score)
                score[at, lanes] = s
                top = jnp.maximum(top, jnp.max(s.reshape(blk // 8, 8, blk), axis=0))
            top = jnp.max(top, axis=0, keepdims=True)
            total = jnp.zeros((8, blk), F32)
            for j in range(n_blk):
                at = slice(j * blk, (j + 1) * blk)
                e = jnp.exp(score[at, lanes] - top)
                score[at, lanes] = e
                total = total + fold(e)
            scale = 1.0 / across(total)
            for j in range(n_blk):
                at = slice(j * blk, (j + 1) * blk)
                pt_o[h, at, lanes] = (score[at, lanes] * scale).astype(BF16)
        mixed = nn(v, pt_o[h]) * live
        att_o[pl.ds(pl.multiple_of(h * HEAD_DIM, HEAD_DIM), HEAD_DIM), :] = mixed.astype(BF16)
        return carry

    lax.fori_loop(0, heads, one_head, 0)


def middle_kernel(
    place, a0, a1, a2, a3, c0, c1, c2, c3, xt, cols, w_out, w_out_t, w_up, w_up_t, w_down,
    d0, d1, d2, d3, nb_o, h2_o, act_o, dup_o, gm_o, ga_o, at_o, dy_o, mid_o, vec_o,
    attn, mid, wide, other, sums,
):
    m = place[0]
    rows = c0.shape[0]
    channels = a0.shape[0]
    width, tokens = xt.shape
    hidden = w_up.shape[1]
    for k, (a, c) in enumerate(zip((a0, a1, a2, a3), (c0, c1, c2, c3))):
        at_o[pl.ds(pl.multiple_of((m ^ k) * channels, channels), channels), :] = a[...]
        dy_o[:, pl.ds(pl.multiple_of((m ^ k) * rows, rows), rows)] = c[...].T
    attn[...] = nn(w_out_t[...], at_o[...])
    zero = jnp.zeros((8, tokens), F32)

    def residual(i, acc):
        w = cols[chunk(i), :]
        v = xt[chunk(i), :].astype(F32) + w[:, SCALE0 : SCALE0 + 1] * attn[chunk(i), :]
        mid[chunk(i), :] = v
        gm_o[chunk(i), :] = (
            dy_o[chunk(i), :].astype(F32) * w[:, SCALE1 : SCALE1 + 1]
        ).astype(BF16)
        return acc + fold(v)

    mean = across(passes(width, residual, zero)) / width
    mid_o[...] = mid[:, pl.ds(pl.multiple_of(m * rows, rows), rows)]

    def spread(i, acc):
        v = mid[chunk(i), :] - mean
        return acc + fold(v * v)

    rstd = lax.rsqrt(across(passes(width, spread, zero)) / width + norm_eps)

    def norm(i, carry):
        w = cols[chunk(i), :]
        v = (mid[chunk(i), :] - mean) * rstd
        mid[chunk(i), :] = v
        h2_o[chunk(i), :] = (v * w[:, GAIN1 : GAIN1 + 1] + w[:, BIAS1 : BIAS1 + 1]).astype(BF16)
        return carry

    passes(width, norm, 0)
    wide[...] = nn(w_up_t[...], h2_o[...])
    other[...] = nn(w_down[...], gm_o[...])

    def gelu(i, carry):
        u = wide[chunk(i), :]
        cdf = 0.5 + 0.5 * lax.erf(u * (0.5**0.5))
        act_o[chunk(i), :] = (u * cdf).astype(BF16)
        slope = cdf + u * (jnp.exp(-0.5 * u * u) * 0.3989422804014327)
        dup_o[chunk(i), :] = (slope * other[chunk(i), :]).astype(BF16)
        return carry

    passes(hidden, gelu, 0)
    wide[...] = nn(w_up[...], dup_o[...])

    def gather(i, acc):
        d = wide[chunk(i), :]
        hat = mid[chunk(i), :]
        u = d * cols[chunk(i), :][:, GAIN1 : GAIN1 + 1]
        sums[chunk(i), 0:1] = jnp.sum(d * hat, axis=1, keepdims=True)
        sums[chunk(i), 1:2] = jnp.sum(d, axis=1, keepdims=True)
        return acc[0] + fold(u), acc[1] + fold(u * hat)

    first, second = passes(width, gather, (zero, zero))
    first, second = across(first) / width, across(second) / width
    lane = lax.broadcasted_iota(jnp.int32, (1, tokens), 1)
    mine = ((lane >= m * rows) & (lane < (m + 1) * rows)).astype(F32)

    def back(i, carry):
        w = cols[chunk(i), :]
        u = wide[chunk(i), :] * w[:, GAIN1 : GAIN1 + 1]
        v = rstd * (u - first - mid[chunk(i), :] * second)
        nb_o[chunk(i), :] = v
        v = v + mine * dy_o[chunk(i), :].astype(F32)
        sums[chunk(i), 2:3] = jnp.sum(v * attn[chunk(i), :], axis=1, keepdims=True)
        ga_o[chunk(i), :] = (v * w[:, SCALE0 : SCALE0 + 1]).astype(BF16)
        return carry

    passes(width, back, 0)
    other[...] = nn(w_out[...], ga_o[...])
    for k, ref in enumerate((d0, d1, d2, d3)):
        ref[...] = other[
            pl.ds(pl.multiple_of((m ^ k) * channels, channels), channels), :
        ].astype(BF16)
    turned = sums[...].T
    vec_o[...] = jnp.zeros(vec_o.shape, F32)
    vec_o[1:2, :] = turned[0:1, :]
    vec_o[3:4, :] = turned[1:2, :]
    vec_o[4:5, :] = turned[2:3, :]


def mlp_kernel(
    place, vec, act, dup, gm, ga, att, h2, dy, w_down_t,
    m0, m1, m2, m3, vec_o, *rest,
):
    grads, (mlp, sums) = rest[:-2], rest[-2:]
    m, d = place[0], place[1]
    rows = m0.shape[1]
    width, tokens = dy.shape
    mlp[...] = nn(w_down_t[...], act[...])
    for k, ref in enumerate((m0, m1, m2, m3)):
        ref[...] = mlp[:, pl.ds(pl.multiple_of((m ^ k) * rows, rows), rows)].astype(BF16)

    def scale(i, carry):
        v = dy[chunk(i), :].astype(F32) * mlp[chunk(i), :]
        sums[chunk(i), 0:1] = jnp.sum(v, axis=1, keepdims=True)
        return carry

    passes(width, scale, 0)
    vec_o[...] = vec[...]
    vec_o[5:6, :] = sums[...].T[0:1, :]
    pairs = ((h2, dup), (gm, act), (ga, att))
    put_blocks([nt(a[...], b[...]).astype(BF16) for a, b in pairs], d & 1, grads)


def put_blocks(parts, here, grads):
    at = 0
    for p in parts:
        cols = slice(at, at + p.shape[1])
        at += p.shape[1]
        if len(grads) == 1:
            grads[0][:, cols] = p
            continue
        sent, kept = grads
        n = sent.shape[0] // 4
        for b in range(4):
            even, odd = p[2 * b * n : (2 * b + 1) * n], p[(2 * b + 1) * n : (2 * b + 2) * n]
            sent[b * n : (b + 1) * n, cols] = pick(here, odd, even)
            kept[b * n : (b + 1) * n, cols] = pick(here, even, odd)


def pick(bit, a, b):
    return jnp.where(bit == 0, a, b)


def back_kernel(
    place, lengths, d0, d1, d2, d3, qkv, pt, xt, stat, nb, cols, wq_t, vec,
    p0, p1, p2, p3, dqkv_o, vec_o,
    score, ds, acc, buckets_of, wide, sums,
):
    m = place[0]
    channels, tokens = d0.shape
    heads = channels // HEAD_DIM
    width = xt.shape[0]
    rows = p0.shape[1]
    blk = 128
    n_blk = tokens // blk
    n_rows = buckets_of.shape[0]
    buckets = n_rows // heads
    half = buckets // 2
    live = (page_ids(lengths, (1, tokens), 1, -1) >= 0).astype(F32)
    off = lax.broadcasted_iota(jnp.int32, (blk, blk), 1) - lax.broadcasted_iota(
        jnp.int32, (blk, blk), 0
    )

    def one_head(h, carry):
        def rows_of(which):
            return pl.ds(pl.multiple_of(which * channels + h * HEAD_DIM, HEAD_DIM), HEAD_DIM)

        q, k, v = qkv[rows_of(0), :], qkv[rows_of(1), :], qkv[rows_of(2), :]
        mine = rows_of(0)
        d_att = (
            d0[mine, :].astype(F32) + d1[mine, :].astype(F32)
            + d2[mine, :].astype(F32) + d3[mine, :].astype(F32)
        )
        d_att = (d_att.astype(BF16).astype(F32) * live).astype(BF16)
        dqkv_o[rows_of(2), :] = nt(d_att, pt[h]).astype(BF16)
        score[...] = nn(v.T, d_att)
        acc[...] = jnp.zeros(acc.shape, F32)
        for i in range(n_blk):
            lanes = slice(i * blk, (i + 1) * blk)
            total = jnp.zeros((8, blk), F32)
            for j in range(n_blk):
                at = slice(j * blk, (j + 1) * blk)
                prod = score[at, lanes] * pt[h, at, lanes].astype(F32)
                score[at, lanes] = prod
                total = total + fold(prod)
            total = across(total)
            for j in range(n_blk):
                at = slice(j * blk, (j + 1) * blk)
                g = score[at, lanes] - pt[h, at, lanes].astype(F32) * total
                g = g.astype(BF16)
                ds[at, lanes] = g
                slot = max(min(i - j, 2), -2) + 2
                acc[slot] = acc[slot] + g.astype(F32)
        dqkv_o[rows_of(0), :] = (nn(k, ds[...]) * HEAD_DIM**-0.5).astype(BF16)
        dqkv_o[rows_of(1), :] = nt(q, ds[...]).astype(BF16)
        near, before, after = acc[2], acc[1], acc[3]
        corner_b, off_b = before[0:16, :], off[0:16, :] - blk
        corner_a, off_a = after[blk - 16 : blk, :], off[blk - 16 : blk, :] + blk
        first = h * buckets
        for b in range(buckets):
            if b == 0:
                v = fold(acc[0]) + fold(jnp.where(off - blk <= -half, before, 0.0))
                v = v + fold(jnp.where(off <= -half, near, 0.0))
            elif b == buckets - 1:
                v = fold(acc[4]) + fold(jnp.where(off + blk >= half - 1, after, 0.0))
                v = v + fold(jnp.where(off >= half - 1, near, 0.0))
            else:
                v = fold(jnp.where(off == b - half, near, 0.0))
                if b < half:
                    v = v + fold(jnp.where(off_b == b - half, corner_b, 0.0))
                elif b > half:
                    v = v + fold(jnp.where(off_a == b - half, corner_a, 0.0))
            buckets_of[pl.ds(first + b, 1), :] = across(v)
        return carry

    lax.fori_loop(0, heads, one_head, 0)
    wide[...] = nn(wq_t[...], dqkv_o[...])
    mean, rstd = stat[0:1, :], stat[1:2, :]
    zero = jnp.zeros((8, tokens), F32)

    def gather(i, part):
        d = wide[chunk(i), :]
        hat = (xt[chunk(i), :].astype(F32) - mean) * rstd
        u = d * cols[chunk(i), :][:, GAIN0 : GAIN0 + 1]
        sums[chunk(i), 0:1] = jnp.sum(d * hat, axis=1, keepdims=True)
        sums[chunk(i), 1:2] = jnp.sum(d, axis=1, keepdims=True)
        return part[0] + fold(u), part[1] + fold(u * hat)

    first, second = passes(width, gather, (zero, zero))
    first, second = across(first) / width, across(second) / width

    def back(i, carry):
        hat = (xt[chunk(i), :].astype(F32) - mean) * rstd
        u = wide[chunk(i), :] * cols[chunk(i), :][:, GAIN0 : GAIN0 + 1]
        wide[chunk(i), :] = nb[chunk(i), :] + rstd * (u - first - hat * second)
        return carry

    passes(width, back, 0)
    for k, ref in enumerate((p0, p1, p2, p3)):
        ref[...] = wide[:, pl.ds(pl.multiple_of((m ^ k) * rows, rows), rows)].astype(ref.dtype)
    turned = sums[...].T
    vec_o[...] = vec[...]
    vec_o[0:1, :] = turned[0:1, :]
    vec_o[2:3, :] = turned[1:2, :]
    each = jnp.sum(buckets_of[...], axis=1, keepdims=True)
    shape = (n_rows, width)
    lane = lax.broadcasted_iota(jnp.int32, shape, 1)
    row = lax.broadcasted_iota(jnp.int32, shape, 0)
    vec_o[6:7, :] = across(jnp.where(lane == row + m * n_rows, each, 0.0))


def qkv_grad_kernel(place, h1, dqkv, *grads):
    put_blocks([nt(h1[...], dqkv[...]).astype(BF16)], place[1] & 1, grads)


def plane_kernel(place, keep, recv, b0, b1, b2, b3):
    at = (place[1] >> 1) & 3
    n = b0.shape[0]
    for k, ref in enumerate((b0, b1, b2, b3)):
        rows = pl.ds(pl.multiple_of((at ^ k) * n, n), n)
        total = keep[rows, :].astype(F32) + recv[rows, :].astype(F32)
        ref[...] = total.astype(ref.dtype)


def four(refs):
    total = refs[0][...].astype(F32)
    for r in refs[1:]:
        total = total + r[...].astype(F32)
    return total


def grads_last_kernel(place, b0, b1, b2, b3, up_o, down_o, o0, o1, o2, o3, turned):
    m = place[0]
    hidden = up_o.shape[1]
    channels = o0.shape[0]
    g = four((b0, b1, b2, b3))
    up_o[...] = g[:, :hidden]
    down_o[...] = g[:, hidden : 2 * hidden]
    turned[...] = g[:, 2 * hidden :].T
    for k, ref in enumerate((o0, o1, o2, o3)):
        v = turned[pl.ds(pl.multiple_of((m ^ k) * channels, channels), channels), :]
        ref[...] = v.astype(ref.dtype)


def out_sum_kernel(o0, o1, o2, o3, out):
    out[...] = four((o0, o1, o2, o3))


def qkv_last_kernel(b0, b1, b2, b3, out):
    total = four((b0, b1, b2, b3))
    channels = out.shape[2]
    for i in range(3):
        out[i] = total[:, i * channels : (i + 1) * channels]


def input_kernel(p0, p1, p2, p3, dy, out):
    total = p0[...] + p1[...].astype(F32) + p2[...].astype(F32) + p3[...].astype(F32)
    out[...] = (dy[...].astype(F32) + total.T).astype(BF16)


def output_kernel(m0, m1, m2, m3, mid, cols, out):
    total = m0[...].astype(F32) + m1[...].astype(F32) + m2[...].astype(F32) + m3[...].astype(F32)
    out[...] = (mid[...] + cols[:, SCALE1 : SCALE1 + 1] * total).T.astype(BF16)


def body(
    tokens,
    page_lengths,
    norm_gains,
    norm_biases,
    layer_scales,
    w_qkv,
    rel_table,
    w_out,
    w_up,
    w_down,
    cotangent,
):
    mp, dp = lax.axis_size("mp"), lax.axis_size("dp")
    rows, width = tokens.shape
    group = rows * mp
    channels = w_qkv.shape[2]
    hidden = w_up.shape[1]
    heads = channels // HEAD_DIM
    buckets = rel_table.shape[0]
    m, d = lax.axis_index("mp"), lax.axis_index("dp")
    place = jnp.stack([m, d]).astype(jnp.int32)

    def swap(v, k, axis="mp", name="rows"):
        n = mp if axis == "mp" else dp
        with jax.named_scope(name):
            return lax.ppermute(v, axis, [(i, i ^ k) for i in range(n)])

    def after(v, *seen):
        return lax.optimization_barrier((v,) + seen)[0]

    fast = dp == 8 and (width // dp) % 16 == 0 and hidden == width

    cols = jnp.concatenate(
        [norm_gains[0:1], norm_biases[0:1], norm_gains[1:2], norm_biases[1:2], layer_scales]
    ).T
    wq = jnp.transpose(w_qkv, (1, 2, 0)).reshape(3 * channels, width)

    piece = (channels // 2, width // 2)
    (sent,) = call(
        message_kernel, [like((2 * rows + piece[0], piece[1]), BF16)], [place, tokens, w_out], n_smem=1
    )
    x = [sent] + [swap(sent, k, name="x") for k in (1, 2, 3)]
    dy1 = swap(cotangent, 1, name="dy")
    wq_t, w_up_t, w_down_t = call(
        turn_kernel,
        [like((width, 3 * channels), BF16), like((hidden, width), BF16), like((width, hidden), BF16)],
        [wq, w_up, w_down],
    )
    (part,) = call(pieces_kernel, [like((4,) + piece, BF16)], x)
    part_x = swap(part, 2, "dp", name="w")
    dy2 = swap(after(cotangent, x[3]), 2, name="dy")
    wq_now = after(wq, wq_t, w_up_t, w_down_t)
    xt, h1, stat, qkv, pt, att = call(
        head_kernel,
        [
            like((width, group), BF16),
            like((width, group), BF16),
            like((8, group), F32),
            like((3 * channels, group), BF16),
            like((heads, group, group), BF16),
            like((channels, group), BF16),
        ],
        [place, page_lengths, rel_table] + x + [cols, wq_now],
        n_smem=3,
        scratch=[
            pltpu.VMEM((group, group), F32),
            pltpu.VMEM((group, 128), jnp.int32),
            pltpu.VMEM((3, 128, 128), F32),
        ],
        us=7,
    )
    atts = [att] + [swap(att, k, name="att") for k in (1, 2, 3)]
    dy = [cotangent, dy1, dy2, swap(after(dy2, atts[1]), 1, name="dy")]
    w_pieces = [part, part_x, swap(part, 1, "dp", name="w"), swap(part_x, 1, "dp", name="w")]
    w_out_full, w_out_t = call(
        out_weight_kernel, [like((width, width), BF16)] * 2, [place] + w_pieces, n_smem=1
    )
    act_like = like((width, group), BF16)
    hid_like = like((hidden, group), BF16)
    d0, d1, d2, d3, nb, h2, act, dup, gm, ga, att_all, dy_t, mid, vec = call(
        middle_kernel,
        [like((channels, group), BF16)] * 4
        + [like((width, group), F32), act_like, hid_like, hid_like, act_like, act_like]
        + [act_like, act_like, like((width, rows), F32), like((8, width), F32)],
        [place] + atts + dy + [xt, cols, w_out_full, w_out_t, w_up, w_up_t, w_down],
        n_smem=1,
        scratch=[
            pltpu.VMEM((width, group), F32),
            pltpu.VMEM((width, group), F32),
            pltpu.VMEM((hidden, group), F32),
            pltpu.VMEM((hidden, group), F32),
            pltpu.VMEM((width, 128), F32),
        ],
        us=12,
    )
    d_att = [d0] + [swap(v, k, name="d_att") for k, v in ((1, d1), (2, d2), (3, d3))]
    grad_cols = 2 * hidden + width
    share = width // dp
    grad_like = [like((width // 2, grad_cols), BF16)] * 2 if fast else [like((width, grad_cols), BF16)]
    m0, m1, m2, m3, vec, *grads = call(
        mlp_kernel,
        [like((width, rows), BF16)] * 4 + [like((8, width), F32)] + grad_like,
        [place, vec, act, dup, gm, ga, att_all, h2, dy_t, w_down_t],
        n_smem=1,
        scratch=[pltpu.VMEM((width, group), F32), pltpu.VMEM((width, 128), F32)],
    )
    mlp = [m0] + [swap(v, k, name="mlp") for k, v in ((1, m1), (2, m2), (3, m3))]

    def planes(grads, n, name):
        kept = grads[1]
        recv = swap(grads[0], 1, "dp", name=name + "_core")
        b = call(
            plane_kernel,
            [like((share, n), F32)] + [like((share, n), BF16)] * 3,
            [place, kept, recv],
            n_smem=1,
        )
        return [b[0]] + [swap(b[k], 2 * k, "dp", name=name + "_plane") for k in (1, 2, 3)]

    if fast:
        blocks = planes(grads, grad_cols, "grads")

    p0, p1, p2, p3, dqkv, vec = call(
        back_kernel,
        [like((width, rows), F32)]
        + [like((width, rows), BF16)] * 3
        + [like((3 * channels, group), BF16), like((8, width), F32)],
        [place, page_lengths] + d_att + [qkv, pt, xt, stat, nb, cols, wq_t, vec],
        n_smem=2,
        scratch=[
            pltpu.VMEM((group, group), F32),
            pltpu.VMEM((group, group), BF16),
            pltpu.VMEM((5, 128, 128), F32),
            pltpu.VMEM((heads * buckets, 128), F32),
            pltpu.VMEM((width, group), F32),
            pltpu.VMEM((width, 128), F32),
        ],
        us=9,
    )
    (output,) = call(output_kernel, [like((rows, width), BF16)], mlp + [mid, cols])
    p1, p2, p3, output = lax.optimization_barrier((p1, p2, p3, output))
    back = [p0] + [swap(v, k, name="back") for k, v in ((1, p1), (2, p2), (3, p3))]
    n = 3 * channels
    grad_like = [like((width // 2, n), BF16)] * 2 if fast else [like((width, n), BF16)]
    qkv_grads = call(qkv_grad_kernel, grad_like, [place, h1, dqkv], n_smem=1)

    def reduced(g):
        g = g.reshape(dp, width // dp, g.shape[1])
        bit = 1
        while bit < dp:
            g = g.reshape(g.shape[0] // 2, 2, width // dp, g.shape[-1])
            here = (d & bit) // bit
            sent = lax.dynamic_index_in_dim(g, 1 - here, 1, keepdims=False)
            kept = lax.dynamic_index_in_dim(g, here, 1, keepdims=False)
            g = kept.astype(F32) + swap(sent, bit, "dp").astype(F32)
            bit *= 2
            if bit < dp:
                g = g.astype(BF16)
        return g[0]

    if fast:
        qkv_blocks = planes(qkv_grads, n, "qkv")
        grad_up, grad_down, o0, o1, o2, o3 = call(
            grads_last_kernel,
            [like((share, hidden), F32)] * 2
            + [like((channels, share), F32)]
            + [like((channels, share), BF16)] * 3,
            [place] + blocks,
            n_smem=1,
            scratch=[pltpu.VMEM((width, share), F32)],
        )
        o1, o2, o3 = (swap(v, k, name="out") for k, v in ((1, o1), (2, o2), (3, o3)))
        (grad_out,) = call(out_sum_kernel, [like((channels, share), F32)], [o0, o1, o2, o3])
        (grad_qkv,) = call(qkv_last_kernel, [like((3, share, channels), F32)], qkv_blocks)
        grad_qkv = jnp.transpose(grad_qkv, (1, 0, 2))
    else:
        summed = reduced(grads[0])
        grad_qkv = reduced(qkv_grads[0]).reshape(share, 3, channels)
        grad_up, grad_down = summed[:, :hidden], summed[:, hidden : 2 * hidden]
        turned = summed[:, 2 * hidden :].T

        def out_part(k):
            return lax.dynamic_slice_in_dim(turned, (m ^ k) * channels, channels, 0)

        grad_out = out_part(0)
        for k in range(1, mp):
            grad_out = grad_out + swap(out_part(k).astype(BF16), k).astype(F32)

    bit = 1
    while bit < dp:
        vec = vec + swap(vec, bit, "dp", name="vec")
        bit *= 2
    for k in (1, 2):
        vec = vec + swap(vec, k, name="vec")

    (output,) = call(output_kernel, [like((rows, width), BF16)], mlp + [mid, cols])
    (grad_input,) = call(input_kernel, [like((rows, width), BF16)], back + [cotangent])
    grad_table = vec[6, : heads * mp * buckets].reshape(heads * mp, buckets).T
    return (
        output,
        grad_input,
        vec[0:2],
        vec[2:4],
        vec[4:6],
        grad_qkv,
        grad_table,
        grad_out,
        grad_up,
        grad_down.T,
    )


def solution(mesh):
    placed = (
        P(("dp", "mp"), None),
        P("dp", None),
        P(),
        P(),
        P(),
        P(None, None, "mp"),
        P(),
        P("mp", None),
        P(None, "mp"),
        P("mp", None),
        P(("dp", "mp"), None),
    )
    return jax.shard_map(
        body,
        mesh=mesh,
        in_specs=placed,
        out_specs=(
            P(("dp", "mp"), None),
            P(("dp", "mp"), None),
            P(),
            P(),
            P(),
            P("dp", None, "mp"),
            P(),
            P("mp", "dp"),
            P("dp", "mp"),
            P("mp", "dp"),
        ),
        check_vma=False,
    )
```

```python
import jax
import jax.numpy as jnp
from jax import lax
from jax.experimental import pallas as pl
from jax.experimental.pallas import tpu as pltpu
from jax.sharding import PartitionSpec as P

HEAD_DIM = 64
SPEED = 1.15e9
norm_eps = 1e-06
masked_score = -1000000000.0
F32 = jnp.float32
BF16 = jnp.bfloat16
SMEM = pl.BlockSpec(memory_space=pltpu.SMEM)
VMEM = pl.BlockSpec(memory_space=pltpu.VMEM)
CHUNK = 64
GAIN0, BIAS0, GAIN1, BIAS1, SCALE0, SCALE1 = range(6)


def call(kernel, outs, args, n_smem=0, scratch=(), us=0.01, limit=16):
    return pl.pallas_call(
        kernel,
        out_shape=tuple(outs),
        in_specs=[SMEM] * n_smem + [VMEM] * (len(args) - n_smem),
        out_specs=tuple([VMEM] * len(outs)),
        scratch_shapes=list(scratch),
        compiler_params=pltpu.CompilerParams(vmem_limit_bytes=limit << 20),
        name=kernel.__name__,
        cost_estimate=pl.CostEstimate(flops=int(us * SPEED), bytes_accessed=8, transcendentals=0),
    )(*args)


def like(shape, dtype):
    return jax.ShapeDtypeStruct(shape, dtype)


def nn(a, b):
    return lax.dot_general(a, b, (((1,), (0,)), ((), ())), preferred_element_type=F32)


def nt(a, b):
    return lax.dot_general(a, b, (((1,), (1,)), ((), ())), preferred_element_type=F32)


def fold(v):
    return jnp.sum(v.reshape(v.shape[0] // 8, 8, v.shape[1]), axis=0)


def across(v):
    return jnp.sum(v, axis=0, keepdims=True)


def passes(rows, step, start):
    return lax.fori_loop(0, rows // CHUNK, step, start)


def chunk(i):
    return pl.ds(pl.multiple_of(i * CHUNK, CHUNK), CHUNK)


def page_ids(lengths, shape, axis, dead):
    at = lax.broadcasted_iota(jnp.int32, shape, axis)
    page = jnp.zeros(shape, jnp.int32)
    end = jnp.int32(0)
    pages = lengths.shape[1]
    for p in range(pages):
        end = end + lengths[0, p]
        page = page + (at >= end).astype(jnp.int32)
    return jnp.where(page < pages - 1, page, dead)


def turn_kernel(wq, wu, wd, wq_o, wu_o, wd_o):
    wq_o[...] = wq[...].T
    wu_o[...] = wu[...].T
    wd_o[...] = wd[...].T


def pieces_kernel(x0, x1, x2, x3, out):
    n = out.shape[1]
    for k, ref in enumerate((x0, x1, x2, x3)):
        out[k] = ref[ref.shape[0] - n :, :]


def pair_kernel(a, b, out):
    out[0:4] = a[...]
    out[4:8] = b[...]


def out_weight_kernel(place, here, there, w_o, wt_o):
    m, d = place[0], place[1]
    rows = here.shape[1]
    for c, ref in enumerate((here, there)):
        for b in range(2):
            part = (d & 3) ^ (c + 2 * b)
            for k in range(4):
                at = pl.multiple_of((m ^ k) * 4 * rows + part * rows, rows)
                w_o[pl.ds(at, rows), :] = ref[4 * b + k]
    wt_o[...] = w_o[...].T


def head_kernel(
    place, lengths, table, x0, x1, x2, x3, cols, wq,
    xt_o, h1_o, stat_o, qkv_o, pt_o, att_o,
    score, ids, pattern,
):
    m = place[0]
    width, tokens = xt_o.shape
    rows = tokens // 4
    channels = att_o.shape[0]
    heads = channels // HEAD_DIM
    buckets = table.shape[0]
    half = buckets // 2
    for k, ref in enumerate((x0, x1, x2, x3)):
        at = pl.multiple_of((m ^ k) * rows, rows)
        xt_o[:, pl.ds(at, rows)] = ref[0:rows, :].T

    def add(i, acc):
        return acc + fold(xt_o[chunk(i), :].astype(F32))

    zero = jnp.zeros((8, tokens), F32)
    mean = across(passes(width, add, zero)) / width

    def spread(i, acc):
        v = xt_o[chunk(i), :].astype(F32) - mean
        return acc + fold(v * v)

    rstd = lax.rsqrt(across(passes(width, spread, zero)) / width + norm_eps)
    stat_o[0:1, :] = mean
    stat_o[1:2, :] = rstd

    def norm(i, carry):
        v = (xt_o[chunk(i), :].astype(F32) - mean) * rstd
        w = cols[chunk(i), :]
        h1_o[chunk(i), :] = (v * w[:, GAIN0 : GAIN0 + 1] + w[:, BIAS0 : BIAS0 + 1]).astype(BF16)
        return carry

    passes(width, norm, 0)
    qkv_o[...] = nn(wq[...], h1_o[...]).astype(BF16)
    qkv_o[0:channels, :] = qkv_o[0:channels, :] * BF16(HEAD_DIM**-0.5)

    ids[...] = page_ids(lengths, ids.shape, 0, -2)
    own_ids = page_ids(lengths, (1, tokens), 1, -1)
    live = (own_ids >= 0).astype(F32)
    blk = 128
    n_blk = tokens // blk
    off = lax.broadcasted_iota(jnp.int32, (blk, blk), 1) - lax.broadcasted_iota(
        jnp.int32, (blk, blk), 0
    )

    def one_head(h, carry):
        col = m * heads + h
        low, high = table[0, col], table[buckets - 1, col]
        near = jnp.where(off >= half - 1, high, low)
        for b in range(1, buckets - 1):
            near = jnp.where(off == b - half, table[b, col], near)
        pattern[1] = near
        before = jnp.full((blk, blk), low, F32)
        for b in range(1, half):
            before = jnp.where(off - blk == b - half, table[b, col], before)
        pattern[0] = before
        after = jnp.full((blk, blk), high, F32)
        for b in range(half + 1, buckets - 1):
            after = jnp.where(off + blk == b - half, table[b, col], after)
        pattern[2] = after

        def rows_of(which):
            return pl.ds(pl.multiple_of(which * channels + h * HEAD_DIM, HEAD_DIM), HEAD_DIM)

        q, k, v = qkv_o[rows_of(0), :], qkv_o[rows_of(1), :], qkv_o[rows_of(2), :]
        score[...] = nn(k.T, q)
        for i in range(n_blk):
            lanes = slice(i * blk, (i + 1) * blk)
            query_id = own_ids[:, lanes]
            top = jnp.full((8, blk), -3e38, F32)
            for j in range(n_blk):
                at = slice(j * blk, (j + 1) * blk)
                if abs(i - j) <= 1:
                    bias = pattern[i - j + 1]
                else:
                    bias = low if i < j else high
                s = jnp.where(ids[at, :] == query_id, score[at, lanes] + bias, masked_score)
                score[at, lanes] = s
                top = jnp.maximum(top, jnp.max(s.reshape(blk // 8, 8, blk), axis=0))
            top = jnp.max(top, axis=0, keepdims=True)
            total = jnp.zeros((8, blk), F32)
            for j in range(n_blk):
                at = slice(j * blk, (j + 1) * blk)
                e = jnp.exp(score[at, lanes] - top)
                score[at, lanes] = e
                total = total + fold(e)
            scale = 1.0 / across(total)
            for j in range(n_blk):
                at = slice(j * blk, (j + 1) * blk)
                pt_o[h, at, lanes] = (score[at, lanes] * scale).astype(BF16)
        mixed = nn(v, pt_o[h]) * live
        att_o[pl.ds(pl.multiple_of(h * HEAD_DIM, HEAD_DIM), HEAD_DIM), :] = mixed.astype(BF16)
        return carry

    lax.fori_loop(0, heads, one_head, 0)


def middle_kernel(
    place, a0, a1, a2, a3, c0, c1, c2, c3, xt, cols, w_out, w_out_t, w_up, w_up_t, w_down,
    d0, d1, d2, d3, nb_o, h2_o, act_o, dup_o, gm_o, ga_o, at_o, dy_o, mid_o, vec_o,
    attn, mid, wide, other, sums,
):
    m = place[0]
    rows = c0.shape[0]
    channels = a0.shape[0]
    width, tokens = xt.shape
    hidden = w_up.shape[1]
    for k, (a, c) in enumerate(zip((a0, a1, a2, a3), (c0, c1, c2, c3))):
        at_o[pl.ds(pl.multiple_of((m ^ k) * channels, channels), channels), :] = a[...]
        dy_o[:, pl.ds(pl.multiple_of((m ^ k) * rows, rows), rows)] = c[...].T
    attn[...] = nn(w_out_t[...], at_o[...])
    zero = jnp.zeros((8, tokens), F32)

    def residual(i, acc):
        w = cols[chunk(i), :]
        v = xt[chunk(i), :].astype(F32) + w[:, SCALE0 : SCALE0 + 1] * attn[chunk(i), :]
        mid[chunk(i), :] = v
        gm_o[chunk(i), :] = (
            dy_o[chunk(i), :].astype(F32) * w[:, SCALE1 : SCALE1 + 1]
        ).astype(BF16)
        return acc + fold(v)

    mean = across(passes(width, residual, zero)) / width
    mid_o[...] = mid[:, pl.ds(pl.multiple_of(m * rows, rows), rows)]

    def spread(i, acc):
        v = mid[chunk(i), :] - mean
        return acc + fold(v * v)

    rstd = lax.rsqrt(across(passes(width, spread, zero)) / width + norm_eps)

    def norm(i, carry):
        w = cols[chunk(i), :]
        v = (mid[chunk(i), :] - mean) * rstd
        mid[chunk(i), :] = v
        h2_o[chunk(i), :] = (v * w[:, GAIN1 : GAIN1 + 1] + w[:, BIAS1 : BIAS1 + 1]).astype(BF16)
        return carry

    passes(width, norm, 0)
    wide[...] = nn(w_up_t[...], h2_o[...])
    other[...] = nn(w_down[...], gm_o[...])

    def gelu(i, carry):
        u = wide[chunk(i), :]
        cdf = 0.5 + 0.5 * lax.erf(u * (0.5**0.5))
        act_o[chunk(i), :] = (u * cdf).astype(BF16)
        slope = cdf + u * (jnp.exp(-0.5 * u * u) * 0.3989422804014327)
        dup_o[chunk(i), :] = (slope * other[chunk(i), :]).astype(BF16)
        return carry

    passes(hidden, gelu, 0)
    wide[...] = nn(w_up[...], dup_o[...])

    def gather(i, acc):
        d = wide[chunk(i), :]
        hat = mid[chunk(i), :]
        u = d * cols[chunk(i), :][:, GAIN1 : GAIN1 + 1]
        sums[chunk(i), 0:1] = jnp.sum(d * hat, axis=1, keepdims=True)
        sums[chunk(i), 1:2] = jnp.sum(d, axis=1, keepdims=True)
        return acc[0] + fold(u), acc[1] + fold(u * hat)

    first, second = passes(width, gather, (zero, zero))
    first, second = across(first) / width, across(second) / width
    lane = lax.broadcasted_iota(jnp.int32, (1, tokens), 1)
    mine = ((lane >= m * rows) & (lane < (m + 1) * rows)).astype(F32)

    def back(i, carry):
        w = cols[chunk(i), :]
        u = wide[chunk(i), :] * w[:, GAIN1 : GAIN1 + 1]
        v = rstd * (u - first - mid[chunk(i), :] * second)
        nb_o[chunk(i), :] = v
        v = v + mine * dy_o[chunk(i), :].astype(F32)
        sums[chunk(i), 2:3] = jnp.sum(v * attn[chunk(i), :], axis=1, keepdims=True)
        ga_o[chunk(i), :] = (v * w[:, SCALE0 : SCALE0 + 1]).astype(BF16)
        return carry

    passes(width, back, 0)
    other[...] = nn(w_out[...], ga_o[...])
    for k, ref in enumerate((d0, d1, d2, d3)):
        ref[...] = other[
            pl.ds(pl.multiple_of((m ^ k) * channels, channels), channels), :
        ].astype(BF16)
    turned = sums[...].T
    vec_o[...] = jnp.zeros(vec_o.shape, F32)
    vec_o[1:2, :] = turned[0:1, :]
    vec_o[3:4, :] = turned[1:2, :]
    vec_o[4:5, :] = turned[2:3, :]


def mlp_kernel(
    place, vec, act, dup, gm, ga, att, h2, dy, w_down_t,
    m0, m2, m13, vec_o, *rest,
):
    grads, (mlp, sums) = rest[:-2], rest[-2:]
    m, d = place[0], place[1]
    rows = m0.shape[1]
    width, tokens = dy.shape
    mlp[...] = nn(w_down_t[...], act[...])
    put_halves(m, mlp, m0, m2, m13)

    def scale(i, carry):
        v = dy[chunk(i), :].astype(F32) * mlp[chunk(i), :]
        sums[chunk(i), 0:1] = jnp.sum(v, axis=1, keepdims=True)
        return carry

    passes(width, scale, 0)
    vec_o[...] = vec[...]
    vec_o[5:6, :] = sums[...].T[0:1, :]
    pairs = ((h2, dup), (gm, act), (ga, att))
    put_blocks([nt(a[...], b[...]).astype(BF16) for a, b in pairs], d & 1, grads)


def put_halves(m, ref, own, next_to, sent):
    rows, width = own.shape[1], own.shape[0]

    def of(k):
        return ref[:, pl.ds(pl.multiple_of((m ^ k) * rows, rows), rows)]

    own[...], next_to[...] = of(0), of(2)
    sent[0:width, :] = of(1).astype(BF16)
    sent[width:, :] = of(3).astype(BF16)


def halve_kernel(own, next_to, recv, own_o, sent):
    width = own.shape[0]
    own_o[...] = own[...] + recv[0:width, :].astype(F32)
    sent[...] = (next_to[...] + recv[width:, :].astype(F32)).astype(BF16)


def put_blocks(parts, here, grads):
    at = 0
    for p in parts:
        cols = slice(at, at + p.shape[1])
        at += p.shape[1]
        if len(grads) == 1:
            grads[0][:, cols] = p
            continue
        sent, kept = grads
        n = kept.shape[0] // 4
        for b in range(4):
            even, odd = p[2 * b * n : (2 * b + 1) * n], p[(2 * b + 1) * n : (2 * b + 2) * n]
            sent[b * n : (b + 1) * n, cols] = pick(here, odd, even)
            kept[b * n : (b + 1) * n, cols] = pick(here, even, odd)


def pick(bit, a, b):
    return jnp.where(bit == 0, a, b)


def back_kernel(
    place, lengths, d0, d1, d2, d3, qkv, pt, xt, stat, nb, cols, wq_t, vec,
    p0, p2, p13, dqkv_o, vec_o,
    score, ds, acc, buckets_of, wide, sums,
):
    m = place[0]
    channels, tokens = d0.shape
    heads = channels // HEAD_DIM
    width = xt.shape[0]
    rows = p0.shape[1]
    blk = 128
    n_blk = tokens // blk
    n_rows = buckets_of.shape[0]
    buckets = n_rows // heads
    half = buckets // 2
    live = (page_ids(lengths, (1, tokens), 1, -1) >= 0).astype(F32)
    off = lax.broadcasted_iota(jnp.int32, (blk, blk), 1) - lax.broadcasted_iota(
        jnp.int32, (blk, blk), 0
    )

    def one_head(h, carry):
        def rows_of(which):
            return pl.ds(pl.multiple_of(which * channels + h * HEAD_DIM, HEAD_DIM), HEAD_DIM)

        q, k, v = qkv[rows_of(0), :], qkv[rows_of(1), :], qkv[rows_of(2), :]
        mine = rows_of(0)
        d_att = (
            d0[mine, :].astype(F32) + d1[mine, :].astype(F32)
            + d2[mine, :].astype(F32) + d3[mine, :].astype(F32)
        )
        d_att = (d_att.astype(BF16).astype(F32) * live).astype(BF16)
        dqkv_o[rows_of(2), :] = nt(d_att, pt[h]).astype(BF16)
        score[...] = nn(v.T, d_att)
        acc[...] = jnp.zeros(acc.shape, F32)
        for i in range(n_blk):
            lanes = slice(i * blk, (i + 1) * blk)
            total = jnp.zeros((8, blk), F32)
            for j in range(n_blk):
                at = slice(j * blk, (j + 1) * blk)
                prod = score[at, lanes] * pt[h, at, lanes].astype(F32)
                score[at, lanes] = prod
                total = total + fold(prod)
            total = across(total)
            for j in range(n_blk):
                at = slice(j * blk, (j + 1) * blk)
                g = score[at, lanes] - pt[h, at, lanes].astype(F32) * total
                g = g.astype(BF16)
                ds[at, lanes] = g
                slot = max(min(i - j, 2), -2) + 2
                acc[slot] = acc[slot] + g.astype(F32)
        dqkv_o[rows_of(0), :] = (nn(k, ds[...]) * HEAD_DIM**-0.5).astype(BF16)
        dqkv_o[rows_of(1), :] = nt(q, ds[...]).astype(BF16)
        near, before, after = acc[2], acc[1], acc[3]
        corner_b, off_b = before[0:16, :], off[0:16, :] - blk
        corner_a, off_a = after[blk - 16 : blk, :], off[blk - 16 : blk, :] + blk
        first = h * buckets
        for b in range(buckets):
            if b == 0:
                v = fold(acc[0]) + fold(jnp.where(off - blk <= -half, before, 0.0))
                v = v + fold(jnp.where(off <= -half, near, 0.0))
            elif b == buckets - 1:
                v = fold(acc[4]) + fold(jnp.where(off + blk >= half - 1, after, 0.0))
                v = v + fold(jnp.where(off >= half - 1, near, 0.0))
            else:
                v = fold(jnp.where(off == b - half, near, 0.0))
                if b < half:
                    v = v + fold(jnp.where(off_b == b - half, corner_b, 0.0))
                elif b > half:
                    v = v + fold(jnp.where(off_a == b - half, corner_a, 0.0))
            buckets_of[pl.ds(first + b, 1), :] = across(v)
        return carry

    lax.fori_loop(0, heads, one_head, 0)
    wide[...] = nn(wq_t[...], dqkv_o[...])
    mean, rstd = stat[0:1, :], stat[1:2, :]
    zero = jnp.zeros((8, tokens), F32)

    def gather(i, part):
        d = wide[chunk(i), :]
        hat = (xt[chunk(i), :].astype(F32) - mean) * rstd
        u = d * cols[chunk(i), :][:, GAIN0 : GAIN0 + 1]
        sums[chunk(i), 0:1] = jnp.sum(d * hat, axis=1, keepdims=True)
        sums[chunk(i), 1:2] = jnp.sum(d, axis=1, keepdims=True)
        return part[0] + fold(u), part[1] + fold(u * hat)

    first, second = passes(width, gather, (zero, zero))
    first, second = across(first) / width, across(second) / width

    def back(i, carry):
        hat = (xt[chunk(i), :].astype(F32) - mean) * rstd
        u = wide[chunk(i), :] * cols[chunk(i), :][:, GAIN0 : GAIN0 + 1]
        wide[chunk(i), :] = nb[chunk(i), :] + rstd * (u - first - hat * second)
        return carry

    passes(width, back, 0)
    put_halves(m, wide, p0, p2, p13)
    turned = sums[...].T
    vec_o[...] = vec[...]
    vec_o[0:1, :] = turned[0:1, :]
    vec_o[2:3, :] = turned[1:2, :]
    each = jnp.sum(buckets_of[...], axis=1, keepdims=True)
    shape = (n_rows, width)
    lane = lax.broadcasted_iota(jnp.int32, shape, 1)
    row = lax.broadcasted_iota(jnp.int32, shape, 0)
    vec_o[6:7, :] = across(jnp.where(lane == row + m * n_rows, each, 0.0))


def qkv_grad_kernel(place, h1, dqkv, vec, *grads):
    put_blocks([nt(h1[...], dqkv[...]).astype(BF16)], place[1] & 1, grads)
    if len(grads) > 1:
        put_vec(vec[...], grads[0])


def put_vec(vec, ref):
    half = vec.shape[1] // 2
    v = jnp.concatenate([vec[:, :half], vec[:, half:]])
    high = v.astype(BF16)
    n, rows = ref.shape[0], v.shape[0]
    ref[n - 2 * rows : n - rows, :half] = high
    ref[n - rows :, :half] = (v - high.astype(F32)).astype(BF16)


def get_vec(ref, width):
    n, rows, half = ref.shape[0], 16, width // 2
    v = ref[n - 2 * rows : n - rows, :half].astype(F32) + ref[n - rows :, :half].astype(F32)
    return jnp.concatenate([v[:8], v[8:]], axis=1)


def grads_second_kernel(place, keep, recv, a_sent, a_kept, b_sent, b_kept):
    x, y = (place[1] >> 1) & 1, (place[1] >> 2) & 1
    n = keep.shape[0] // 4
    half = a_sent.shape[1]

    def block(i, cols):
        rows = pl.ds(pl.multiple_of(i * n, n), n)
        return keep[rows, cols].astype(F32) + recv[rows, cols].astype(F32)

    left, right = slice(0, half), slice(half, 2 * half)
    for i in range(2):
        at = slice(i * n, (i + 1) * n)
        a_sent[at, :] = block(2 * i + 1 - x, left).astype(BF16)
        a_kept[at, :] = block(2 * i + x, left)
        b_sent[at, :] = block(2 * (1 - y) + i, right).astype(BF16)
        b_kept[at, :] = block(2 * y + i, right)


def grads_third_kernel(place, a_keep, a_recv, b_keep, b_recv, a_sent, a_kept, b_sent, b_kept):
    x, y = (place[1] >> 1) & 1, (place[1] >> 2) & 1
    halve_rows(y, a_keep, a_recv, a_sent, a_kept)
    halve_rows(x, b_keep, b_recv, b_sent, b_kept)


def halve_rows(bit, keep, recv, sent, kept):
    n = kept.shape[0]
    for ref, b in ((sent, 1 - bit), (kept, bit)):
        rows = pl.ds(pl.multiple_of(b * n, n), n)
        ref[0:n, :] = (keep[rows, :] + recv[rows, :].astype(F32)).astype(ref.dtype)


def qkv_second_kernel(place, vec, keep, recv, sent, kept, vec_o):
    x = (place[1] >> 1) & 1
    n = kept.shape[0] // 2
    for i in range(2):
        for ref, b in ((sent, 1 - x), (kept, x)):
            rows = pl.ds(pl.multiple_of((2 * i + b) * n, n), n)
            total = keep[rows, :].astype(F32) + recv[rows, :].astype(F32)
            ref[i * n : (i + 1) * n, :] = total.astype(ref.dtype)
    vec_o[...] = vec[...] + get_vec(recv, vec.shape[1])
    put_vec(vec_o[...], sent)


def qkv_third_kernel(place, vec, keep, recv, sent, kept, vec_o):
    halve_rows((place[1] >> 2) & 1, keep, recv, sent, kept)
    vec_o[...] = vec[...] + get_vec(recv, vec.shape[1])
    put_vec(vec_o[...], sent)


def last_kernel(
    place, vec, a_keep, a_recv, b_keep, b_recv, q_keep, q_recv,
    up_o, down_o, qkv_o, vec_o, o0, o1, o2, o3, turned,
):
    m = place[0]
    hidden = up_o.shape[1]
    channels = o0.shape[0]
    a = a_keep[...] + a_recv[...].astype(F32)
    b = b_keep[...] + b_recv[...].astype(F32)
    share, half = a.shape
    up_o[...] = a[:, :hidden]
    down_o[:, : half - hidden] = a[:, hidden:]
    down_o[:, half - hidden :] = b[:, : 2 * hidden - half]
    turned[...] = b[:, 2 * hidden - half :].T
    v = vec[...] + get_vec(q_recv, vec.shape[1])
    vec_o[...] = v
    tiles = v.shape[1] // 128
    high = v.astype(BF16)
    low = (v - high.astype(F32)).astype(BF16)
    both = jnp.concatenate([high.astype(F32), low.astype(F32)]).astype(BF16)
    for k, ref in enumerate((o0, o1, o2, o3)):
        t = turned[pl.ds(pl.multiple_of((m ^ k) * channels, channels), channels), :]
        ref[0:channels, 0:share] = t.astype(ref.dtype)
        if k:
            for i in range(tiles):
                at = channels + 16 * i
                ref[at : at + 16, :] = both[:, 128 * i : 128 * (i + 1)]
    q = q_keep[...] + q_recv[0:share, :].astype(F32)
    for i in range(3):
        qkv_o[i] = q[:, i * channels : (i + 1) * channels]


def small_kernel(vec, o0, o1, o2, o3, out, gains, biases, scales, table):
    channels, share = out.shape
    others = (o1, o2, o3)
    total = o0[...]
    v = vec[...]
    for ref in others:
        total = total + ref[0:channels, 0:share].astype(F32)
        parts = []
        for i in range(v.shape[1] // 128):
            at = channels + 16 * i
            both = ref[at : at + 16, :].astype(F32)
            parts.append(both[:8] + both[8:])
        v = v + jnp.concatenate(parts, axis=1)
    out[...] = total
    gains[...] = v[0:2]
    biases[...] = v[2:4]
    scales[...] = v[4:6]
    n = table.shape[1]
    for h in range(table.shape[0]):
        table[h : h + 1, :] = v[6:7, h * n : (h + 1) * n]


def input_kernel(own, recv, dy, out):
    total = own[...] + recv[...].astype(F32)
    out[...] = (dy[...].astype(F32) + total.T).astype(BF16)


def output_kernel(own, recv, mid, cols, out):
    total = own[...] + recv[...].astype(F32)
    out[...] = (mid[...] + cols[:, SCALE1 : SCALE1 + 1] * total).T.astype(BF16)


def body(
    tokens,
    page_lengths,
    norm_gains,
    norm_biases,
    layer_scales,
    w_qkv,
    rel_table,
    w_out,
    w_up,
    w_down,
    cotangent,
):
    mp, dp = lax.axis_size("mp"), lax.axis_size("dp")
    rows, width = tokens.shape
    group = rows * mp
    channels = w_qkv.shape[2]
    hidden = w_up.shape[1]
    heads = channels // HEAD_DIM
    buckets = rel_table.shape[0]
    m, d = lax.axis_index("mp"), lax.axis_index("dp")
    place = jnp.stack([m, d]).astype(jnp.int32)

    def swap(v, k, axis="mp", name="rows"):
        n = mp if axis == "mp" else dp
        with jax.named_scope(name):
            return lax.ppermute(v, axis, [(i, i ^ k) for i in range(n)])

    def after(v, *seen):
        return lax.optimization_barrier((v,) + seen)[0]

    fast = dp == 8 and (width // dp) % 16 == 0 and hidden == width

    cols = jnp.concatenate(
        [norm_gains[0:1], norm_biases[0:1], norm_gains[1:2], norm_biases[1:2], layer_scales]
    ).T
    wq = jnp.transpose(w_qkv, (1, 2, 0)).reshape(3 * channels, width)

    piece = channels // 4
    sent = jnp.concatenate([tokens, lax.dynamic_slice_in_dim(w_out, (d & 3) * piece, piece, 0)])
    x = [sent] + [swap(sent, k, name="x") for k in (1, 2, 3)]
    dy1 = swap(cotangent, 1, name="dy")
    wq_t, w_up_t, w_down_t = call(
        turn_kernel,
        [like((width, 3 * channels), BF16), like((hidden, width), BF16), like((width, hidden), BF16)],
        [wq, w_up, w_down],
    )
    x[1:] = lax.optimization_barrier((x[1:], wq_t))[0]
    (part,) = call(pieces_kernel, [like((4, piece, width), BF16)], x)
    part_x = swap(part, 2, "dp", name="w")
    dy2 = swap(after(cotangent, *x[1:]), 2, name="dy")
    wq_now = after(wq, wq_t, w_up_t, w_down_t, dy1)
    xt, h1, stat, qkv, pt, att = call(
        head_kernel,
        [
            like((width, group), BF16),
            like((width, group), BF16),
            like((8, group), F32),
            like((3 * channels, group), BF16),
            like((heads, group, group), BF16),
            like((channels, group), BF16),
        ],
        [place, page_lengths, rel_table] + x + [cols, wq_now],
        n_smem=3,
        scratch=[
            pltpu.VMEM((group, group), F32),
            pltpu.VMEM((group, 128), jnp.int32),
            pltpu.VMEM((3, 128, 128), F32),
        ],
        us=200,
    )
    (parts,) = call(pair_kernel, [like((8, piece, width), BF16)], [part, after(part_x, att, dy2)])
    att_sent = after(att, parts)
    atts = [att] + [swap(att_sent, k, name="att") for k in (1, 2, 3)]
    dy = [cotangent, dy1, dy2, swap(after(dy2, parts), 1, name="dy")]
    w_pieces = [parts, swap(parts, 1, "dp", name="w")]
    w_out_full, w_out_t = call(
        out_weight_kernel, [like((width, width), BF16)] * 2, [place] + w_pieces, n_smem=1
    )
    act_like = like((width, group), BF16)
    hid_like = like((hidden, group), BF16)
    d0, d1, d2, d3, nb, h2, act, dup, gm, ga, att_all, dy_t, mid, vec = call(
        middle_kernel,
        [like((channels, group), BF16)] * 4
        + [like((width, group), F32), act_like, hid_like, hid_like, act_like, act_like]
        + [act_like, act_like, like((width, rows), F32), like((8, width), F32)],
        [place] + atts + dy + [xt, cols, w_out_full, w_out_t, w_up, w_up_t, w_down],
        n_smem=1,
        scratch=[
            pltpu.VMEM((width, group), F32),
            pltpu.VMEM((width, group), F32),
            pltpu.VMEM((hidden, group), F32),
            pltpu.VMEM((hidden, group), F32),
            pltpu.VMEM((width, 128), F32),
        ],
        us=200,
    )
    d_att = [d0] + [swap(v, k, name="d_att") for k, v in ((1, d1), (2, d2), (3, d3))]
    grad_cols = 2 * hidden + width
    share = width // dp
    grad_like = [like((width // 2, grad_cols), BF16)] * 2 if fast else [like((width, grad_cols), BF16)]
    block = like((width, rows), F32)
    blocks = [block, block, like((2 * width, rows), BF16)]
    m0, m2, m13, vec, *grads = call(
        mlp_kernel,
        blocks + [like((8, width), F32)] + grad_like,
        [place, vec, act, dup, gm, ga, att_all, h2, dy_t, w_down_t],
        n_smem=1,
        scratch=[pltpu.VMEM((width, group), F32), pltpu.VMEM((width, 128), F32)],
    )

    def halved(own, next_to, recv, name):
        half_like = [block, like((width, rows), BF16)]
        own, sent = call(halve_kernel, half_like, [own, next_to, recv])
        return [own, swap(sent, 2, name=name)]

    m_recv = swap(after(m13, *d_att[1:]), 1, name="mlp")
    half = grad_cols // 2
    if fast:
        g_recv = swap(grads[0], 1, "dp", name="grads_core")

    p0, p2, p13, dqkv, vec = call(
        back_kernel,
        blocks + [like((3 * channels, group), BF16), like((8, width), F32)],
        [place, page_lengths] + d_att + [qkv, pt, xt, stat, nb, cols, wq_t, vec],
        n_smem=2,
        scratch=[
            pltpu.VMEM((group, group), F32),
            pltpu.VMEM((group, group), BF16),
            pltpu.VMEM((5, 128, 128), F32),
            pltpu.VMEM((heads * buckets, 128), F32),
            pltpu.VMEM((width, group), F32),
            pltpu.VMEM((width, 128), F32),
        ],
        us=200,
    )
    mlp = halved(m0, m2, m_recv, "mlp")
    p_recv = swap(after(p13, m_recv), 1, name="back")
    back = halved(after(p0, mlp[1]), p2, p_recv, "back")
    n = 3 * channels
    extra = 4 * vec.shape[0]
    if fast:
        grad_like = [like((width // 2 + extra, n), BF16), like((width // 2, n), BF16)]
    else:
        grad_like = [like((width, n), BF16)]
    qkv_grads = call(qkv_grad_kernel, grad_like, [place, h1, dqkv, vec], n_smem=1)

    def reduced(g):
        g = g.reshape(dp, width // dp, g.shape[1])
        bit = 1
        while bit < dp:
            g = g.reshape(g.shape[0] // 2, 2, width // dp, g.shape[-1])
            here = (d & bit) // bit
            sent = lax.dynamic_index_in_dim(g, 1 - here, 1, keepdims=False)
            kept = lax.dynamic_index_in_dim(g, here, 1, keepdims=False)
            g = kept.astype(F32) + swap(sent, bit, "dp").astype(F32)
            bit *= 2
            if bit < dp:
                g = g.astype(BF16)
        return g[0]

    if fast:
        q_recv = swap(after(qkv_grads[0], m_recv), 1, "dp", name="qkv_core")
        a_sent, a_kept, b_sent, b_kept = call(
            grads_second_kernel,
            [like((2 * share, half), BF16), like((2 * share, half), F32)] * 2,
            [place, after(grads[1], q_recv), g_recv],
            n_smem=1,
        )
        a_recv = swap(a_sent, 2, "dp", name="grads_a")
        b_recv = swap(b_sent, 4, "dp", name="grads_b")
        vec_like = [like(vec.shape, F32)]
        sent, kept, vec = call(
            qkv_second_kernel,
            [like((2 * share + extra, n), BF16), like((2 * share, n), F32)] + vec_like,
            [place, vec, qkv_grads[1], q_recv],
            n_smem=1,
        )
        recv = swap(sent, 2, "dp", name="qkv_x")
        sent, kept, vec = call(
            qkv_third_kernel,
            [like((share + extra, n), BF16), like((share, n), F32)] + vec_like,
            [place, vec, kept, recv],
            n_smem=1,
        )
        recv = swap(sent, 4, "dp", name="qkv_y")
        a_sent, a_kept, b_sent, b_kept = call(
            grads_third_kernel,
            [like((share, half), BF16), like((share, half), F32)] * 2,
            [place, after(a_kept, kept, back[0]), a_recv, b_kept, b_recv],
            n_smem=1,
        )
        a_recv = swap(a_sent, 4, "dp", name="grads_a")
        b_recv = swap(b_sent, 2, "dp", name="grads_b")
        message = like((channels + 2 * vec.size // 128, 128), BF16)
        grad_up, grad_down, grad_qkv, vec, o0, o1, o2, o3 = call(
            last_kernel,
            [like((share, hidden), F32)] * 2
            + [like((3, share, channels), F32), like(vec.shape, F32)]
            + [like((channels, share), F32)]
            + [message] * 3,
            [place, vec, a_kept, a_recv, b_kept, b_recv, kept, recv],
            n_smem=1,
            scratch=[pltpu.VMEM((width, share), F32)],
        )
        o1, o2, o3 = (swap(v, k, name="out") for k, v in ((1, o1), (2, o2), (3, o3)))
        grad_out, gains, biases, scales, grad_table = call(
            small_kernel,
            [like((channels, share), F32)]
            + [like((2, width), F32)] * 3
            + [like((heads * mp, buckets), F32)],
            [vec, o0, o1, o2, o3],
        )
        grad_qkv = jnp.transpose(grad_qkv, (1, 0, 2))
    else:
        summed = reduced(grads[0])
        grad_qkv = reduced(qkv_grads[0]).reshape(share, 3, channels)
        grad_up, grad_down = summed[:, :hidden], summed[:, hidden : 2 * hidden]
        turned = summed[:, 2 * hidden :].T

        def out_part(k):
            return lax.dynamic_slice_in_dim(turned, (m ^ k) * channels, channels, 0)

        grad_out = out_part(0)
        for k in range(1, mp):
            grad_out = grad_out + swap(out_part(k).astype(BF16), k).astype(F32)
        bit = 1
        while bit < dp:
            vec = vec + swap(vec, bit, "dp", name="vec")
            bit *= 2
        for k in (1, 2):
            vec = vec + swap(vec, k, name="vec")
        gains, biases, scales = vec[0:2], vec[2:4], vec[4:6]
        grad_table = vec[6, : heads * mp * buckets].reshape(heads * mp, buckets)

    (output,) = call(output_kernel, [like((rows, width), BF16)], mlp + [mid, cols])
    (grad_input,) = call(input_kernel, [like((rows, width), BF16)], back + [cotangent])
    return (
        output,
        grad_input,
        gains,
        biases,
        scales,
        grad_qkv,
        grad_table.T,
        grad_out,
        grad_up,
        grad_down.T,
    )


def solution(mesh):
    placed = (
        P(("dp", "mp"), None),
        P("dp", None),
        P(),
        P(),
        P(),
        P(None, None, "mp"),
        P(),
        P("mp", None),
        P(None, "mp"),
        P("mp", None),
        P(("dp", "mp"), None),
    )
    return jax.shard_map(
        body,
        mesh=mesh,
        in_specs=placed,
        out_specs=(
            P(("dp", "mp"), None),
            P(("dp", "mp"), None),
            P(),
            P(),
            P(),
            P("dp", None, "mp"),
            P(),
            P("mp", "dp"),
            P("dp", "mp"),
            P("mp", "dp"),
        ),
        check_vma=False,
    )
```

```python
import jax
import jax.numpy as jnp
from jax import lax
from jax.experimental import pallas as pl
from jax.experimental.pallas import tpu as pltpu
from jax.sharding import PartitionSpec as P

HEAD_DIM = 64
SPEED = 1.15e9
norm_eps = 1e-06
masked_score = -1000000000.0
F32 = jnp.float32
BF16 = jnp.bfloat16
SMEM = pl.BlockSpec(memory_space=pltpu.SMEM)
VMEM = pl.BlockSpec(memory_space=pltpu.VMEM)
CHUNK = 64
GAIN0, BIAS0, GAIN1, BIAS1, SCALE0, SCALE1 = range(6)


def call(kernel, outs, args, n_smem=0, scratch=(), us=0.01, limit=8):
    return pl.pallas_call(
        kernel,
        out_shape=tuple(outs),
        in_specs=[SMEM] * n_smem + [VMEM] * (len(args) - n_smem),
        out_specs=tuple([VMEM] * len(outs)),
        scratch_shapes=list(scratch),
        compiler_params=pltpu.CompilerParams(vmem_limit_bytes=limit << 20),
        name=kernel.__name__,
        cost_estimate=pl.CostEstimate(flops=int(us * SPEED), bytes_accessed=8, transcendentals=0),
    )(*args)


def like(shape, dtype):
    return jax.ShapeDtypeStruct(shape, dtype)


def nn(a, b):
    return lax.dot_general(a, b, (((1,), (0,)), ((), ())), preferred_element_type=F32)


def nt(a, b):
    return lax.dot_general(a, b, (((1,), (1,)), ((), ())), preferred_element_type=F32)


def fold(v):
    return jnp.sum(v.reshape(v.shape[0] // 8, 8, v.shape[1]), axis=0)


def across(v):
    return jnp.sum(v, axis=0, keepdims=True)


def passes(rows, step, start):
    return lax.fori_loop(0, rows // CHUNK, step, start, unroll=True)


def chunk(i):
    return pl.ds(pl.multiple_of(i * CHUNK, CHUNK), CHUNK)


def page_ids(lengths, shape, axis, dead):
    at = lax.broadcasted_iota(jnp.int32, shape, axis)
    page = jnp.zeros(shape, jnp.int32)
    end = jnp.int32(0)
    pages = lengths.shape[1]
    for p in range(pages):
        end = end + lengths[0, p]
        page = page + (at >= end).astype(jnp.int32)
    return jnp.where(page < pages - 1, page, dead)


def turn_kernel(wq, wu, wd, wq_o, wu_o, wd_o):
    wq_o[...] = wq[...].T
    wu_o[...] = wu[...].T
    wd_o[...] = wd[...].T


def pieces_kernel(x0, x1, x2, x3, out):
    n = out.shape[1]
    for k, ref in enumerate((x0, x1, x2, x3)):
        out[k] = ref[ref.shape[0] - n :, :]


def pair_kernel(a, b, out):
    out[0:4] = a[...]
    out[4:8] = b[...]


def out_weight_kernel(place, here, there, w_o, wt_o):
    m, d = place[0], place[1]
    rows = here.shape[1]
    for c, ref in enumerate((here, there)):
        for b in range(2):
            part = (d & 3) ^ (c + 2 * b)
            for k in range(4):
                at = pl.multiple_of((m ^ k) * 4 * rows + part * rows, rows)
                w_o[pl.ds(at, rows), :] = ref[4 * b + k]
    wt_o[...] = w_o[...].T


def head_kernel(
    place, lengths, table, x0, x1, x2, x3, cols, wq,
    xt_o, h1_o, stat_o, qkv_o, pt_o, att_o,
    score, ids, pattern,
):
    m = place[0]
    width, tokens = xt_o.shape
    rows = tokens // 4
    channels = att_o.shape[0]
    heads = channels // HEAD_DIM
    buckets = table.shape[0]
    half = buckets // 2
    for k, ref in enumerate((x0, x1, x2, x3)):
        at = pl.multiple_of((m ^ k) * rows, rows)
        xt_o[:, pl.ds(at, rows)] = ref[0:rows, :].T

    def add(i, acc):
        return acc + fold(xt_o[chunk(i), :].astype(F32))

    zero = jnp.zeros((8, tokens), F32)
    mean = across(passes(width, add, zero)) / width

    def spread(i, acc):
        v = xt_o[chunk(i), :].astype(F32) - mean
        return acc + fold(v * v)

    rstd = lax.rsqrt(across(passes(width, spread, zero)) / width + norm_eps)
    stat_o[0:1, :] = mean
    stat_o[1:2, :] = rstd

    def norm(i, carry):
        v = (xt_o[chunk(i), :].astype(F32) - mean) * rstd
        w = cols[chunk(i), :]
        h1_o[chunk(i), :] = (v * w[:, GAIN0 : GAIN0 + 1] + w[:, BIAS0 : BIAS0 + 1]).astype(BF16)
        return carry

    passes(width, norm, 0)
    qkv_o[...] = nn(wq[...], h1_o[...]).astype(BF16)
    qkv_o[0:channels, :] = qkv_o[0:channels, :] * BF16(HEAD_DIM**-0.5)

    ids[...] = page_ids(lengths, ids.shape, 0, -2)
    own_ids = page_ids(lengths, (1, tokens), 1, -1)
    live = (own_ids >= 0).astype(F32)
    blk = 128
    n_blk = tokens // blk
    off = lax.broadcasted_iota(jnp.int32, (blk, blk), 1) - lax.broadcasted_iota(
        jnp.int32, (blk, blk), 0
    )

    def one_head(h, carry):
        col = m * heads + h
        low, high = table[0, col], table[buckets - 1, col]
        near = jnp.where(off >= half - 1, high, low)
        for b in range(1, buckets - 1):
            near = jnp.where(off == b - half, table[b, col], near)
        pattern[1] = near
        before = jnp.full((blk, blk), low, F32)
        for b in range(1, half):
            before = jnp.where(off - blk == b - half, table[b, col], before)
        pattern[0] = before
        after = jnp.full((blk, blk), high, F32)
        for b in range(half + 1, buckets - 1):
            after = jnp.where(off + blk == b - half, table[b, col], after)
        pattern[2] = after

        def rows_of(which):
            return pl.ds(pl.multiple_of(which * channels + h * HEAD_DIM, HEAD_DIM), HEAD_DIM)

        q, k, v = qkv_o[rows_of(0), :], qkv_o[rows_of(1), :], qkv_o[rows_of(2), :]
        score[...] = nn(k.T, q)
        for i in range(n_blk):
            lanes = slice(i * blk, (i + 1) * blk)
            query_id = own_ids[:, lanes]
            top = jnp.full((8, blk), -3e38, F32)
            for j in range(n_blk):
                at = slice(j * blk, (j + 1) * blk)
                if abs(i - j) <= 1:
                    bias = pattern[i - j + 1]
                else:
                    bias = low if i < j else high
                s = jnp.where(ids[at, :] == query_id, score[at, lanes] + bias, masked_score)
                score[at, lanes] = s
                top = jnp.maximum(top, jnp.max(s.reshape(blk // 8, 8, blk), axis=0))
            top = jnp.max(top, axis=0, keepdims=True)
            total = jnp.zeros((8, blk), F32)
            for j in range(n_blk):
                at = slice(j * blk, (j + 1) * blk)
                e = jnp.exp(score[at, lanes] - top)
                score[at, lanes] = e
                total = total + fold(e)
            scale = 1.0 / across(total)
            for j in range(n_blk):
                at = slice(j * blk, (j + 1) * blk)
                pt_o[h, at, lanes] = (score[at, lanes] * scale).astype(BF16)
        mixed = nn(v, pt_o[h]) * live
        att_o[pl.ds(pl.multiple_of(h * HEAD_DIM, HEAD_DIM), HEAD_DIM), :] = mixed.astype(BF16)
        return carry

    lax.fori_loop(0, heads, one_head, 0, unroll=True)


def up_kernel(
    place, a0, a1, a2, a3, xt, cols, w_out_t, w_up_t, w_down_t,
    at_o, attn_o, hat_o, rstd_o, h2_o, act_o, slope_o, mid_o, mlp_o, m0, m2, m13,
    wide,
):
    m = place[0]
    rows = mid_o.shape[1]
    channels = a0.shape[0]
    width, tokens = xt.shape
    hidden = act_o.shape[0]
    for k, a in enumerate((a0, a1, a2, a3)):
        at_o[pl.ds(pl.multiple_of((m ^ k) * channels, channels), channels), :] = a[...]
    attn_o[...] = nn(w_out_t[...], at_o[...])
    zero = jnp.zeros((8, tokens), F32)

    def residual(i, acc):
        scale = cols[chunk(i), :][:, SCALE0 : SCALE0 + 1]
        v = xt[chunk(i), :].astype(F32) + scale * attn_o[chunk(i), :]
        hat_o[chunk(i), :] = v
        return acc + fold(v)

    mean = across(passes(width, residual, zero)) / width
    mid_o[...] = hat_o[:, pl.ds(pl.multiple_of(m * rows, rows), rows)]

    def spread(i, acc):
        v = hat_o[chunk(i), :] - mean
        return acc + fold(v * v)

    rstd = lax.rsqrt(across(passes(width, spread, zero)) / width + norm_eps)
    rstd_o[0:1, :] = rstd

    def norm(i, carry):
        w = cols[chunk(i), :]
        v = (hat_o[chunk(i), :] - mean) * rstd
        hat_o[chunk(i), :] = v
        h2_o[chunk(i), :] = (v * w[:, GAIN1 : GAIN1 + 1] + w[:, BIAS1 : BIAS1 + 1]).astype(BF16)
        return carry

    passes(width, norm, 0)
    wide[...] = nn(w_up_t[...], h2_o[...])

    def gelu(i, carry):
        u = wide[chunk(i), :]
        cdf = 0.5 + 0.5 * lax.erf(u * (0.5**0.5))
        act_o[chunk(i), :] = (u * cdf).astype(BF16)
        slope_o[chunk(i), :] = cdf + u * (jnp.exp(-0.5 * u * u) * 0.3989422804014327)
        return carry

    passes(hidden, gelu, 0)
    mlp_o[...] = nn(w_down_t[...], act_o[...])
    put_halves(m, mlp_o, m0, m2, m13)


def down_kernel(
    place, c0, c1, c2, c3, cols, attn, hat, rstd, slope, w_out, w_up, w_down,
    d0, d1, d2, d3, nb_o, dup_o, gm_o, ga_o, dy_o, vec_o,
    wide, sums,
):
    m = place[0]
    rows = c0.shape[0]
    channels = d0.shape[0]
    width, tokens = hat.shape
    hidden = slope.shape[0]
    for k, c in enumerate((c0, c1, c2, c3)):
        at = pl.ds(pl.multiple_of((m ^ k) * rows, rows), rows)
        turned = c[...].T
        dy_o[:, at] = turned
        scale = cols[:, SCALE1 : SCALE1 + 1]
        gm_o[:, at] = (turned.astype(F32) * scale).astype(BF16)
    wide[...] = nn(w_down[...], gm_o[...])

    def d_up(i, carry):
        dup_o[chunk(i), :] = (slope[chunk(i), :] * wide[chunk(i), :]).astype(BF16)
        return carry

    passes(hidden, d_up, 0)
    wide[...] = nn(w_up[...], dup_o[...])
    zero = jnp.zeros((8, tokens), F32)

    def gather(i, acc):
        d = wide[chunk(i), :]
        u = d * cols[chunk(i), :][:, GAIN1 : GAIN1 + 1]
        return acc[0] + fold(u), acc[1] + fold(u * hat[chunk(i), :])

    first, second = passes(width, gather, (zero, zero))
    first, second = across(first) / width, across(second) / width
    lane = lax.broadcasted_iota(jnp.int32, (1, tokens), 1)
    mine = ((lane >= m * rows) & (lane < (m + 1) * rows)).astype(F32)
    rstd = rstd[0:1, :]

    def back(i, carry):
        w = cols[chunk(i), :]
        d = wide[chunk(i), :]
        h = hat[chunk(i), :]
        v = rstd * (d * w[:, GAIN1 : GAIN1 + 1] - first - h * second)
        nb_o[chunk(i), :] = v
        v = v + mine * dy_o[chunk(i), :].astype(F32)
        ga_o[chunk(i), :] = (v * w[:, SCALE0 : SCALE0 + 1]).astype(BF16)
        sums[chunk(i), 0:1] = jnp.sum(d * h, axis=1, keepdims=True)
        sums[chunk(i), 1:2] = jnp.sum(d, axis=1, keepdims=True)
        sums[chunk(i), 2:3] = jnp.sum(v * attn[chunk(i), :], axis=1, keepdims=True)
        return carry

    passes(width, back, 0)
    wide[...] = nn(w_out[...], ga_o[...])
    for k, ref in enumerate((d0, d1, d2, d3)):
        at = pl.ds(pl.multiple_of((m ^ k) * channels, channels), channels)
        ref[...] = wide[at, :].astype(BF16)
    turned = sums[...].T
    vec_o[...] = jnp.zeros(vec_o.shape, F32)
    vec_o[1:2, :] = turned[0:1, :]
    vec_o[3:4, :] = turned[1:2, :]
    vec_o[4:5, :] = turned[2:3, :]


def mlp_grad_kernel(place, vec, mlp, act, dup, gm, ga, att, h2, dy, vec_o, *rest):
    grads, sums = rest[:-1], rest[-1]

    def scale(i, carry):
        v = dy[chunk(i), :].astype(F32) * mlp[chunk(i), :]
        sums[chunk(i), 0:1] = jnp.sum(v, axis=1, keepdims=True)
        return carry

    passes(dy.shape[0], scale, 0)
    vec_o[...] = vec[...]
    vec_o[5:6, :] = sums[...].T[0:1, :]
    if len(grads) == 1:
        at = 0
        for a, b in ((h2, dup), (gm, act), (ga, att)):
            grads[0][:, at : at + b.shape[0]] = nt(a[...], b[...]).astype(BF16)
            at += b.shape[0]
        return
    x, y = (place[1] >> 1) & 1, (place[1] >> 2) & 1
    a_sent, a_kept, b_sent, b_kept = grads
    n, half = a_sent.shape[0] // 4, a_sent.shape[1]

    def put(p, left, low, high):
        block = [p[i * n : (i + 1) * n, low:high] for i in range(8)]
        first = left + low < half
        at = left + low - (0 if first else half)
        cols = slice(at, at + high - low)
        for i in range(4):
            out = slice(i * n, (i + 1) * n)
            if first:
                zero, one = 4 * (i // 2) + i % 2, 4 * (i // 2) + 2 + i % 2
                a_sent[out, cols] = pick(x, block[one], block[zero])
                a_kept[out, cols] = pick(x, block[zero], block[one])
            else:
                b_sent[out, cols] = pick(y, block[4 + i], block[i])
                b_kept[out, cols] = pick(y, block[i], block[4 + i])

    left = 0
    for a, b in ((h2, dup), (gm, act), (ga, att)):
        p = nt(a[...], b[...]).astype(BF16)
        n_cols = p.shape[1]
        cut = min(max(half - left, 0), n_cols)
        if cut > 0:
            put(p, left, 0, cut)
        if cut < n_cols:
            put(p, left, cut, n_cols)
        left += n_cols


def put_halves(m, ref, own, next_to, sent):
    rows, width = own.shape[1], own.shape[0]

    def of(k):
        return ref[:, pl.ds(pl.multiple_of((m ^ k) * rows, rows), rows)]

    own[...], next_to[...] = of(0), of(2)
    sent[0:width, :] = of(1).astype(BF16)
    sent[width:, :] = of(3).astype(BF16)


def halve_kernel(own, next_to, recv, own_o, sent):
    width = own.shape[0]
    own_o[...] = own[...] + recv[0:width, :].astype(F32)
    sent[...] = (next_to[...] + recv[width:, :].astype(F32)).astype(BF16)


def put_blocks(parts, here, grads):
    at = 0
    for p in parts:
        cols = slice(at, at + p.shape[1])
        at += p.shape[1]
        if len(grads) == 1:
            grads[0][:, cols] = p
            continue
        sent, kept = grads
        n = kept.shape[0] // 4
        for b in range(4):
            even, odd = p[2 * b * n : (2 * b + 1) * n], p[(2 * b + 1) * n : (2 * b + 2) * n]
            sent[b * n : (b + 1) * n, cols] = pick(here, odd, even)
            kept[b * n : (b + 1) * n, cols] = pick(here, even, odd)


def pick(bit, a, b):
    return jnp.where(bit == 0, a, b)


def back_kernel(
    place, lengths, d0, d1, d2, d3, qkv, pt, xt, stat, nb, cols, wq_t, vec,
    p0, p2, p13, dqkv_o, vec_o,
    score, ds, acc, buckets_of, wide, sums,
):
    m = place[0]
    channels, tokens = d0.shape
    heads = channels // HEAD_DIM
    width = xt.shape[0]
    rows = p0.shape[1]
    blk = 128
    n_blk = tokens // blk
    n_rows = buckets_of.shape[0]
    buckets = n_rows // heads
    half = buckets // 2
    live = (page_ids(lengths, (1, tokens), 1, -1) >= 0).astype(F32)
    off = lax.broadcasted_iota(jnp.int32, (blk, blk), 1) - lax.broadcasted_iota(
        jnp.int32, (blk, blk), 0
    )

    def one_head(h, carry):
        def rows_of(which):
            return pl.ds(pl.multiple_of(which * channels + h * HEAD_DIM, HEAD_DIM), HEAD_DIM)

        q, k, v = qkv[rows_of(0), :], qkv[rows_of(1), :], qkv[rows_of(2), :]
        mine = rows_of(0)
        d_att = (
            d0[mine, :].astype(F32) + d1[mine, :].astype(F32)
            + d2[mine, :].astype(F32) + d3[mine, :].astype(F32)
        )
        d_att = (d_att.astype(BF16).astype(F32) * live).astype(BF16)
        dqkv_o[rows_of(2), :] = nt(d_att, pt[h]).astype(BF16)
        score[...] = nn(v.T, d_att)
        acc[...] = jnp.zeros(acc.shape, F32)
        for i in range(n_blk):
            lanes = slice(i * blk, (i + 1) * blk)
            total = jnp.zeros((8, blk), F32)
            for j in range(n_blk):
                at = slice(j * blk, (j + 1) * blk)
                prod = score[at, lanes] * pt[h, at, lanes].astype(F32)
                score[at, lanes] = prod
                total = total + fold(prod)
            total = across(total)
            for j in range(n_blk):
                at = slice(j * blk, (j + 1) * blk)
                g = score[at, lanes] - pt[h, at, lanes].astype(F32) * total
                g = g.astype(BF16)
                ds[at, lanes] = g
                slot = max(min(i - j, 2), -2) + 2
                acc[slot] = acc[slot] + g.astype(F32)
        dqkv_o[rows_of(0), :] = (nn(k, ds[...]) * HEAD_DIM**-0.5).astype(BF16)
        dqkv_o[rows_of(1), :] = nt(q, ds[...]).astype(BF16)
        near, before, after = acc[2], acc[1], acc[3]
        corner_b, off_b = before[0:16, :], off[0:16, :] - blk
        corner_a, off_a = after[blk - 16 : blk, :], off[blk - 16 : blk, :] + blk
        first = h * buckets
        for b in range(buckets):
            if b == 0:
                v = fold(acc[0]) + fold(jnp.where(off - blk <= -half, before, 0.0))
                v = v + fold(jnp.where(off <= -half, near, 0.0))
            elif b == buckets - 1:
                v = fold(acc[4]) + fold(jnp.where(off + blk >= half - 1, after, 0.0))
                v = v + fold(jnp.where(off >= half - 1, near, 0.0))
            else:
                v = fold(jnp.where(off == b - half, near, 0.0))
                if b < half:
                    v = v + fold(jnp.where(off_b == b - half, corner_b, 0.0))
                elif b > half:
                    v = v + fold(jnp.where(off_a == b - half, corner_a, 0.0))
            buckets_of[pl.ds(first + b, 1), :] = across(v)
        return carry

    lax.fori_loop(0, heads, one_head, 0, unroll=True)
    wide[...] = nn(wq_t[...], dqkv_o[...])
    mean, rstd = stat[0:1, :], stat[1:2, :]
    zero = jnp.zeros((8, tokens), F32)

    def gather(i, part):
        d = wide[chunk(i), :]
        hat = (xt[chunk(i), :].astype(F32) - mean) * rstd
        u = d * cols[chunk(i), :][:, GAIN0 : GAIN0 + 1]
        sums[chunk(i), 0:1] = jnp.sum(d * hat, axis=1, keepdims=True)
        sums[chunk(i), 1:2] = jnp.sum(d, axis=1, keepdims=True)
        return part[0] + fold(u), part[1] + fold(u * hat)

    first, second = passes(width, gather, (zero, zero))
    first, second = across(first) / width, across(second) / width

    def back(i, carry):
        hat = (xt[chunk(i), :].astype(F32) - mean) * rstd
        u = wide[chunk(i), :] * cols[chunk(i), :][:, GAIN0 : GAIN0 + 1]
        wide[chunk(i), :] = nb[chunk(i), :] + rstd * (u - first - hat * second)
        return carry

    passes(width, back, 0)
    put_halves(m, wide, p0, p2, p13)
    turned = sums[...].T
    vec_o[...] = vec[...]
    vec_o[0:1, :] = turned[0:1, :]
    vec_o[2:3, :] = turned[1:2, :]
    each = jnp.sum(buckets_of[...], axis=1, keepdims=True)
    shape = (n_rows, width)
    lane = lax.broadcasted_iota(jnp.int32, shape, 1)
    row = lax.broadcasted_iota(jnp.int32, shape, 0)
    vec_o[6:7, :] = across(jnp.where(lane == row + m * n_rows, each, 0.0))


def qkv_grad_kernel(place, h1, dqkv, vec, *grads):
    put_blocks([nt(h1[...], dqkv[...]).astype(BF16)], place[1] & 1, grads)
    if len(grads) > 1:
        put_vec(vec[...], grads[0])


def put_vec(vec, ref):
    half = vec.shape[1] // 2
    v = jnp.concatenate([vec[:, :half], vec[:, half:]])
    high = v.astype(BF16)
    n, rows = ref.shape[0], v.shape[0]
    ref[n - 2 * rows : n - rows, :half] = high
    ref[n - rows :, :half] = (v - high.astype(F32)).astype(BF16)


def get_vec(ref, width):
    n, rows, half = ref.shape[0], 16, width // 2
    v = ref[n - 2 * rows : n - rows, :half].astype(F32) + ref[n - rows :, :half].astype(F32)
    return jnp.concatenate([v[:8], v[8:]], axis=1)


def grads_second_kernel(place, a_keep, a_recv, b_keep, b_recv, sent, kept):
    core = place[1] & 1
    half, n = a_keep.shape[1], kept.shape[0] // 2
    for at, keep, recv in ((0, a_keep, a_recv), (half, b_keep, b_recv)):
        cols = slice(at, at + half)
        for i in range(2):
            rows = pl.ds(pl.multiple_of(2 * i * n, 2 * n), 2 * n)
            out = slice(i * n, (i + 1) * n)
            halve_rows(core, keep.at[rows], recv.at[rows], sent.at[out, cols], kept.at[out, cols])


def grads_third_kernel(place, keep, recv, a_sent, a_kept, b_sent, b_kept):
    x, y = (place[1] >> 1) & 1, (place[1] >> 2) & 1
    half = a_kept.shape[1]
    halve_rows(y, keep.at[:, :half], recv.at[:, :half], a_sent, a_kept)
    halve_rows(x, keep.at[:, half:], recv.at[:, half:], b_sent, b_kept)


def halve_rows(bit, keep, recv, sent, kept):
    n = kept.shape[0]
    for ref, b in ((sent, 1 - bit), (kept, bit)):
        rows = pl.ds(pl.multiple_of(b * n, n), n)
        total = keep[rows, :].astype(F32) + recv[rows, :].astype(F32)
        ref[0:n, :] = total.astype(ref.dtype)


def qkv_second_kernel(place, vec, keep, recv, sent, kept, vec_o):
    x = (place[1] >> 1) & 1
    n = kept.shape[0] // 2
    for i in range(2):
        for ref, b in ((sent, 1 - x), (kept, x)):
            rows = pl.ds(pl.multiple_of((2 * i + b) * n, n), n)
            total = keep[rows, :].astype(F32) + recv[rows, :].astype(F32)
            ref[i * n : (i + 1) * n, :] = total.astype(ref.dtype)
    vec_o[...] = vec[...] + get_vec(recv, vec.shape[1])
    put_vec(vec_o[...], sent)


def qkv_third_kernel(place, vec, keep, recv, sent, kept, vec_o):
    halve_rows((place[1] >> 2) & 1, keep, recv, sent, kept)
    vec_o[...] = vec[...] + get_vec(recv, vec.shape[1])
    put_vec(vec_o[...], sent)


def last_kernel(
    place, vec, a_keep, a_recv, b_keep, b_recv, q_keep, q_recv,
    up_o, down_o, qkv_o, vec_o, o0, o1, o2, o3, turned,
):
    m = place[0]
    hidden = up_o.shape[1]
    channels = o0.shape[0]
    a = a_keep[...] + a_recv[...].astype(F32)
    b = b_keep[...] + b_recv[...].astype(F32)
    share, half = a.shape
    up_o[...] = a[:, :hidden]
    down_o[:, : half - hidden] = a[:, hidden:]
    down_o[:, half - hidden :] = b[:, : 2 * hidden - half]
    turned[...] = b[:, 2 * hidden - half :].T
    v = vec[...] + get_vec(q_recv, vec.shape[1])
    vec_o[...] = v
    tiles = v.shape[1] // 128
    high = v.astype(BF16)
    low = (v - high.astype(F32)).astype(BF16)
    both = jnp.concatenate([high.astype(F32), low.astype(F32)]).astype(BF16)
    for k, ref in enumerate((o0, o1, o2, o3)):
        t = turned[pl.ds(pl.multiple_of((m ^ k) * channels, channels), channels), :]
        ref[0:channels, 0:share] = t.astype(ref.dtype)
        if k:
            for i in range(tiles):
                at = channels + 16 * i
                ref[at : at + 16, :] = both[:, 128 * i : 128 * (i + 1)]
    q = q_keep[...] + q_recv[0:share, :].astype(F32)
    for i in range(3):
        qkv_o[i] = q[:, i * channels : (i + 1) * channels]


def small_kernel(vec, o0, o1, o2, o3, out, gains, biases, scales, table):
    channels, share = out.shape
    others = (o1, o2, o3)
    total = o0[...]
    v = vec[...]
    for ref in others:
        total = total + ref[0:channels, 0:share].astype(F32)
        parts = []
        for i in range(v.shape[1] // 128):
            at = channels + 16 * i
            both = ref[at : at + 16, :].astype(F32)
            parts.append(both[:8] + both[8:])
        v = v + jnp.concatenate(parts, axis=1)
    out[...] = total
    gains[...] = v[0:2]
    biases[...] = v[2:4]
    scales[...] = v[4:6]
    n = table.shape[1]
    for h in range(table.shape[0]):
        table[h : h + 1, :] = v[6:7, h * n : (h + 1) * n]


def input_kernel(own, recv, dy, out):
    total = own[...] + recv[...].astype(F32)
    out[...] = (dy[...].astype(F32) + total.T).astype(BF16)


def output_kernel(own, recv, mid, cols, out):
    total = own[...] + recv[...].astype(F32)
    out[...] = (mid[...] + cols[:, SCALE1 : SCALE1 + 1] * total).T.astype(BF16)


def body(
    tokens,
    page_lengths,
    norm_gains,
    norm_biases,
    layer_scales,
    w_qkv,
    rel_table,
    w_out,
    w_up,
    w_down,
    cotangent,
):
    mp, dp = lax.axis_size("mp"), lax.axis_size("dp")
    rows, width = tokens.shape
    group = rows * mp
    channels = w_qkv.shape[2]
    hidden = w_up.shape[1]
    heads = channels // HEAD_DIM
    buckets = rel_table.shape[0]
    m, d = lax.axis_index("mp"), lax.axis_index("dp")
    place = jnp.stack([m, d]).astype(jnp.int32)

    def swap(v, k, axis="mp", name="rows"):
        n = mp if axis == "mp" else dp
        with jax.named_scope(name):
            return lax.ppermute(v, axis, [(i, i ^ k) for i in range(n)])

    def after(v, *seen):
        return lax.optimization_barrier((v,) + seen)[0]

    fast = dp == 8 and (width // dp) % 16 == 0 and hidden == width

    cols = jnp.concatenate(
        [norm_gains[0:1], norm_biases[0:1], norm_gains[1:2], norm_biases[1:2], layer_scales]
    ).T
    wq = jnp.transpose(w_qkv, (1, 2, 0)).reshape(3 * channels, width)

    piece = channels // 4
    sent = jnp.concatenate([tokens, lax.dynamic_slice_in_dim(w_out, (d & 3) * piece, piece, 0)])
    x = [sent] + [swap(sent, k, name="x") for k in (1, 2, 3)]
    dy1 = swap(cotangent, 1, name="dy")
    wq_t, w_up_t, w_down_t = call(
        turn_kernel,
        [like((width, 3 * channels), BF16), like((hidden, width), BF16), like((width, hidden), BF16)],
        [wq, w_up, w_down],
    )
    x[1:] = lax.optimization_barrier((x[1:], wq_t))[0]
    (part,) = call(pieces_kernel, [like((4, piece, width), BF16)], x)
    part_x = swap(part, 2, "dp", name="w")
    dy2 = swap(after(cotangent, *x[1:]), 2, name="dy")
    wq_now = after(wq, wq_t, w_up_t, w_down_t, dy1)
    xt, h1, stat, qkv, pt, att = call(
        head_kernel,
        [
            like((width, group), BF16),
            like((width, group), BF16),
            like((8, group), F32),
            like((3 * channels, group), BF16),
            like((heads, group, group), BF16),
            like((channels, group), BF16),
        ],
        [place, page_lengths, rel_table] + x + [cols, wq_now],
        n_smem=3,
        scratch=[
            pltpu.VMEM((group, group), F32),
            pltpu.VMEM((group, 128), jnp.int32),
            pltpu.VMEM((3, 128, 128), F32),
        ],
        us=10,
    )
    (parts,) = call(pair_kernel, [like((8, piece, width), BF16)], [part, after(part_x, att, dy2)])
    att_sent = after(att, parts)
    atts = [att] + [swap(att_sent, k, name="att") for k in (1, 2, 3)]
    dy = [cotangent, dy1, dy2, swap(after(dy2, *atts[1:]), 1, name="dy")]
    w_pieces = [parts, swap(parts, 1, "dp", name="w")]
    w_out_full, w_out_t = call(
        out_weight_kernel, [like((width, width), BF16)] * 2, [place] + w_pieces, n_smem=1
    )
    act_like = like((width, group), BF16)
    hid_like = like((hidden, group), BF16)
    wide_like = like((width, group), F32)
    block = like((width, rows), F32)
    blocks = [block, block, like((2 * width, rows), BF16)]
    att_all, attn, hat, rstd, h2, act, slope, mid, mlp_part, m0, m2, m13 = call(
        up_kernel,
        [act_like, wide_like, wide_like, like((8, group), F32), act_like, hid_like]
        + [like((hidden, group), F32), block, wide_like]
        + blocks,
        [place] + atts + [xt, cols, w_out_t, w_up_t, w_down_t],
        n_smem=1,
        scratch=[pltpu.VMEM((hidden, group), F32)],
        us=10,
    )
    m_recv = swap(m13, 1, name="mlp")
    d0, d1, d2, d3, nb, dup, gm, ga, dy_t, vec = call(
        down_kernel,
        [like((channels, group), BF16)] * 4
        + [wide_like, hid_like, act_like, act_like, act_like, like((8, width), F32)],
        [place] + dy + [cols, attn, hat, rstd, slope, w_out_full, w_up, w_down],
        n_smem=1,
        scratch=[pltpu.VMEM((max(width, hidden), group), F32), pltpu.VMEM((width, 128), F32)],
        us=10,
    )
    d_att = [d0] + [swap(v, k, name="d_att") for k, v in ((1, d1), (2, d2), (3, d3))]
    grad_cols = 2 * hidden + width
    share = width // dp
    half = grad_cols // 2
    if fast:
        grad_like = [like((width // 2, half), BF16)] * 4
    else:
        grad_like = [like((width, grad_cols), BF16)]
    vec, *grads = call(
        mlp_grad_kernel,
        [like((8, width), F32)] + grad_like,
        [place, vec, mlp_part, act, dup, gm, ga, att_all, h2, dy_t],
        n_smem=1,
        scratch=[pltpu.VMEM((width, 128), F32)],
    )
    if fast:
        a_sent, a_kept, b_sent, b_kept = grads
        a_recv = swap(a_sent, 2, "dp", name="grads_a")
        b_recv = swap(b_sent, 4, "dp", name="grads_b")

    def halved(own, next_to, recv, name, us=0.01, seen=()):
        half_like = [block, like((width, rows), BF16)]
        own, sent = call(halve_kernel, half_like, [own, next_to, recv], us=us)
        return [own, swap(after(sent, *seen), 2, name=name)]

    mlp = halved(m0, m2, m_recv, "mlp", seen=d_att[1:])

    p0, p2, p13, dqkv, vec = call(
        back_kernel,
        blocks + [like((3 * channels, group), BF16), like((8, width), F32)],
        [place, page_lengths] + d_att + [qkv, pt, xt, stat, nb, cols, wq_t, vec],
        n_smem=2,
        scratch=[
            pltpu.VMEM((group, group), F32),
            pltpu.VMEM((group, group), BF16),
            pltpu.VMEM((5, 128, 128), F32),
            pltpu.VMEM((heads * buckets, 128), F32),
            pltpu.VMEM((width, group), F32),
            pltpu.VMEM((width, 128), F32),
        ],
        us=10,
    )
    p_recv = swap(after(p13, mlp[1]), 1, name="back")
    back = halved(p0, p2, p_recv, "back", us=10)
    n = 3 * channels
    extra = 4 * vec.shape[0]
    if fast:
        grad_like = [like((width // 2 + extra, n), BF16), like((width // 2, n), BF16)]
    else:
        grad_like = [like((width, n), BF16)]
    qkv_grads = call(qkv_grad_kernel, grad_like, [place, h1, dqkv, vec], n_smem=1)

    def reduced(g):
        g = g.reshape(dp, width // dp, g.shape[1])
        bit = 1
        while bit < dp:
            g = g.reshape(g.shape[0] // 2, 2, width // dp, g.shape[-1])
            here = (d & bit) // bit
            sent = lax.dynamic_index_in_dim(g, 1 - here, 1, keepdims=False)
            kept = lax.dynamic_index_in_dim(g, here, 1, keepdims=False)
            g = kept.astype(F32) + swap(sent, bit, "dp").astype(F32)
            bit *= 2
            if bit < dp:
                g = g.astype(BF16)
        return g[0]

    if fast:
        q_recv = swap(after(qkv_grads[0], mlp[1]), 1, "dp", name="qkv_core")
        g_sent, g_kept = call(
            grads_second_kernel,
            [like((2 * share, grad_cols), BF16)] * 2,
            [place, after(a_kept, q_recv), a_recv, b_kept, b_recv],
            n_smem=1,
        )
        g_recv = swap(g_sent, 1, "dp", name="grads_core")
        vec_like = [like(vec.shape, F32)]
        sent, kept, vec = call(
            qkv_second_kernel,
            [like((2 * share + extra, n), BF16), like((2 * share, n), F32)] + vec_like,
            [place, vec, qkv_grads[1], q_recv],
            n_smem=1,
        )
        recv = swap(sent, 2, "dp", name="qkv_x")
        a_sent, a_kept, b_sent, b_kept = call(
            grads_third_kernel,
            [like((share, half), BF16), like((share, half), F32)] * 2,
            [place, g_kept, g_recv],
            n_smem=1,
        )
        a_recv = swap(a_sent, 4, "dp", name="grads_a")
        b_recv = swap(b_sent, 2, "dp", name="grads_b")
        sent, kept, vec = call(
            qkv_third_kernel,
            [like((share + extra, n), BF16), like((share, n), F32)] + vec_like,
            [place, after(vec, a_kept, back[0]), kept, recv],
            n_smem=1,
        )
        recv = swap(sent, 4, "dp", name="qkv_y")
        message = like((channels + 2 * vec.size // 128, 128), BF16)
        grad_up, grad_down, grad_qkv, vec, o0, o1, o2, o3 = call(
            last_kernel,
            [like((share, hidden), F32)] * 2
            + [like((3, share, channels), F32), like(vec.shape, F32)]
            + [like((channels, share), F32)]
            + [message] * 3,
            [place, vec, a_kept, a_recv, b_kept, b_recv, kept, recv],
            n_smem=1,
            scratch=[pltpu.VMEM((width, share), F32)],
        )
        o1, o2, o3 = (swap(v, k, name="out") for k, v in ((1, o1), (2, o2), (3, o3)))
        grad_out, gains, biases, scales, grad_table = call(
            small_kernel,
            [like((channels, share), F32)]
            + [like((2, width), F32)] * 3
            + [like((heads * mp, buckets), F32)],
            [vec, o0, o1, o2, o3],
        )
        grad_qkv = jnp.transpose(grad_qkv, (1, 0, 2))
    else:
        summed = reduced(grads[0])
        grad_qkv = reduced(qkv_grads[0]).reshape(share, 3, channels)
        grad_up, grad_down = summed[:, :hidden], summed[:, hidden : 2 * hidden]
        turned = summed[:, 2 * hidden :].T

        def out_part(k):
            return lax.dynamic_slice_in_dim(turned, (m ^ k) * channels, channels, 0)

        grad_out = out_part(0)
        for k in range(1, mp):
            grad_out = grad_out + swap(out_part(k).astype(BF16), k).astype(F32)
        bit = 1
        while bit < dp:
            vec = vec + swap(vec, bit, "dp", name="vec")
            bit *= 2
        for k in (1, 2):
            vec = vec + swap(vec, k, name="vec")
        gains, biases, scales = vec[0:2], vec[2:4], vec[4:6]
        grad_table = vec[6, : heads * mp * buckets].reshape(heads * mp, buckets)

    (output,) = call(output_kernel, [like((rows, width), BF16)], mlp + [mid, cols])
    (grad_input,) = call(input_kernel, [like((rows, width), BF16)], back + [cotangent])
    return (
        output,
        grad_input,
        gains,
        biases,
        scales,
        grad_qkv,
        grad_table.T,
        grad_out,
        grad_up,
        grad_down.T,
    )


def solution(mesh):
    placed = (
        P(("dp", "mp"), None),
        P("dp", None),
        P(),
        P(),
        P(),
        P(None, None, "mp"),
        P(),
        P("mp", None),
        P(None, "mp"),
        P("mp", None),
        P(("dp", "mp"), None),
    )
    return jax.shard_map(
        body,
        mesh=mesh,
        in_specs=placed,
        out_specs=(
            P(("dp", "mp"), None),
            P(("dp", "mp"), None),
            P(),
            P(),
            P(),
            P("dp", None, "mp"),
            P(),
            P("mp", "dp"),
            P("dp", "mp"),
            P("mp", "dp"),
        ),
        check_vma=False,
    )
```

```python
import jax
import jax.numpy as jnp
from jax import lax
from jax.experimental import pallas as pl
from jax.experimental.pallas import tpu as pltpu
from jax.sharding import PartitionSpec as P

HEAD_DIM = 64
SPEED = 1.15e9
norm_eps = 1e-06
masked_score = -1000000000.0
F32 = jnp.float32
BF16 = jnp.bfloat16
SMEM = pl.BlockSpec(memory_space=pltpu.SMEM)
VMEM = pl.BlockSpec(memory_space=pltpu.VMEM)
CHUNK = 64
GAIN0, BIAS0, GAIN1, BIAS1, SCALE0, SCALE1 = range(6)


def call(kernel, outs, args, n_smem=0, scratch=(), us=0.01, limit=8):
    return pl.pallas_call(
        kernel,
        out_shape=tuple(outs),
        in_specs=[SMEM] * n_smem + [VMEM] * (len(args) - n_smem),
        out_specs=tuple([VMEM] * len(outs)),
        scratch_shapes=list(scratch),
        compiler_params=pltpu.CompilerParams(vmem_limit_bytes=limit << 20),
        name=kernel.__name__,
        cost_estimate=pl.CostEstimate(flops=int(us * SPEED), bytes_accessed=8, transcendentals=0),
    )(*args)


def like(shape, dtype):
    return jax.ShapeDtypeStruct(shape, dtype)


def nn(a, b):
    return lax.dot_general(a, b, (((1,), (0,)), ((), ())), preferred_element_type=F32)


def nt(a, b):
    return lax.dot_general(a, b, (((1,), (1,)), ((), ())), preferred_element_type=F32)


def fold(v):
    return jnp.sum(v.reshape(v.shape[0] // 8, 8, v.shape[1]), axis=0)


def across(v):
    return jnp.sum(v, axis=0, keepdims=True)


def passes(rows, step, start):
    return lax.fori_loop(0, rows // CHUNK, step, start, unroll=True)


def chunk(i):
    return pl.ds(pl.multiple_of(i * CHUNK, CHUNK), CHUNK)


def page_ids(lengths, shape, axis, dead):
    at = lax.broadcasted_iota(jnp.int32, shape, axis)
    page = jnp.zeros(shape, jnp.int32)
    end = jnp.int32(0)
    pages = lengths.shape[1]
    for p in range(pages):
        end = end + lengths[0, p]
        page = page + (at >= end).astype(jnp.int32)
    return jnp.where(page < pages - 1, page, dead)


def turn_kernel(wq, wu, wd, wq_o, wu_o, wd_o):
    wq_o[...] = wq[...].T
    wu_o[...] = wu[...].T
    wd_o[...] = wd[...].T


def pieces_kernel(x0, x1, x2, x3, out):
    n = out.shape[1]
    for k, ref in enumerate((x0, x1, x2, x3)):
        out[k] = ref[ref.shape[0] - n :, :]


def pair_kernel(a, b, out):
    out[0:4] = a[...]
    out[4:8] = b[...]


def out_weight_kernel(place, here, there, w_o, wt_o):
    m, d = place[0], place[1]
    rows = here.shape[1]
    for c, ref in enumerate((here, there)):
        for b in range(2):
            part = (d & 3) ^ (c + 2 * b)
            for k in range(4):
                at = pl.multiple_of((m ^ k) * 4 * rows + part * rows, rows)
                w_o[pl.ds(at, rows), :] = ref[4 * b + k]
    wt_o[...] = w_o[...].T


def head_kernel(
    place, lengths, table, x0, x1, x2, x3, cols, wq,
    xt_o, h1_o, stat_o, qkv_o, pt_o, att_o,
    score, ids, pattern,
):
    m = place[0]
    width, tokens = xt_o.shape
    rows = tokens // 4
    channels = att_o.shape[0]
    heads = channels // HEAD_DIM
    buckets = table.shape[0]
    half = buckets // 2
    for k, ref in enumerate((x0, x1, x2, x3)):
        at = pl.multiple_of((m ^ k) * rows, rows)
        xt_o[:, pl.ds(at, rows)] = ref[0:rows, :].T

    def add(i, acc):
        return acc + fold(xt_o[chunk(i), :].astype(F32))

    zero = jnp.zeros((8, tokens), F32)
    mean = across(passes(width, add, zero)) / width

    def spread(i, acc):
        v = xt_o[chunk(i), :].astype(F32) - mean
        return acc + fold(v * v)

    rstd = lax.rsqrt(across(passes(width, spread, zero)) / width + norm_eps)
    stat_o[0:1, :] = mean
    stat_o[1:2, :] = rstd

    def norm(i, carry):
        v = (xt_o[chunk(i), :].astype(F32) - mean) * rstd
        w = cols[chunk(i), :]
        h1_o[chunk(i), :] = (v * w[:, GAIN0 : GAIN0 + 1] + w[:, BIAS0 : BIAS0 + 1]).astype(BF16)
        return carry

    passes(width, norm, 0)
    qkv_o[...] = nn(wq[...], h1_o[...]).astype(BF16)
    qkv_o[0:channels, :] = qkv_o[0:channels, :] * BF16(HEAD_DIM**-0.5)

    ids[...] = page_ids(lengths, ids.shape, 0, -2)
    own_ids = page_ids(lengths, (1, tokens), 1, -1)
    live = (own_ids >= 0).astype(F32)
    blk = 128
    n_blk = tokens // blk
    off = lax.broadcasted_iota(jnp.int32, (blk, blk), 1) - lax.broadcasted_iota(
        jnp.int32, (blk, blk), 0
    )

    def one_head(h, carry):
        col = m * heads + h
        low, high = table[0, col], table[buckets - 1, col]
        near = jnp.where(off >= half - 1, high, low)
        for b in range(1, buckets - 1):
            near = jnp.where(off == b - half, table[b, col], near)
        pattern[1] = near
        before = jnp.full((blk, blk), low, F32)
        for b in range(1, half):
            before = jnp.where(off - blk == b - half, table[b, col], before)
        pattern[0] = before
        after = jnp.full((blk, blk), high, F32)
        for b in range(half + 1, buckets - 1):
            after = jnp.where(off + blk == b - half, table[b, col], after)
        pattern[2] = after

        def rows_of(which):
            return pl.ds(pl.multiple_of(which * channels + h * HEAD_DIM, HEAD_DIM), HEAD_DIM)

        q, k, v = qkv_o[rows_of(0), :], qkv_o[rows_of(1), :], qkv_o[rows_of(2), :]
        score[...] = nn(k.T, q)
        for i in range(n_blk):
            lanes = slice(i * blk, (i + 1) * blk)
            query_id = own_ids[:, lanes]
            top = jnp.full((8, blk), -3e38, F32)
            for j in range(n_blk):
                at = slice(j * blk, (j + 1) * blk)
                if abs(i - j) <= 1:
                    bias = pattern[i - j + 1]
                else:
                    bias = low if i < j else high
                s = jnp.where(ids[at, :] == query_id, score[at, lanes] + bias, masked_score)
                score[at, lanes] = s
                top = jnp.maximum(top, jnp.max(s.reshape(blk // 8, 8, blk), axis=0))
            top = jnp.max(top, axis=0, keepdims=True)
            total = jnp.zeros((8, blk), F32)
            for j in range(n_blk):
                at = slice(j * blk, (j + 1) * blk)
                e = jnp.exp(score[at, lanes] - top)
                score[at, lanes] = e
                total = total + fold(e)
            scale = 1.0 / across(total)
            for j in range(n_blk):
                at = slice(j * blk, (j + 1) * blk)
                pt_o[h, at, lanes] = (score[at, lanes] * scale).astype(BF16)
        mixed = nn(v, pt_o[h]) * live
        att_o[pl.ds(pl.multiple_of(h * HEAD_DIM, HEAD_DIM), HEAD_DIM), :] = mixed.astype(BF16)
        return carry

    lax.fori_loop(0, heads, one_head, 0, unroll=True)


def up_kernel(
    place, a0, a1, a2, a3, xt, cols, w_out_t, w_up_t, w_down_t,
    at_o, attn_o, hat_o, rstd_o, h2_o, act_o, slope_o, mid_o, mlp_o, m0, m2, m13,
    wide,
):
    m = place[0]
    rows = mid_o.shape[1]
    channels = a0.shape[0]
    width, tokens = xt.shape
    hidden = act_o.shape[0]
    for k, a in enumerate((a0, a1, a2, a3)):
        at_o[pl.ds(pl.multiple_of((m ^ k) * channels, channels), channels), :] = a[...]
    attn_o[...] = nn(w_out_t[...], at_o[...])
    zero = jnp.zeros((8, tokens), F32)

    def residual(i, acc):
        scale = cols[chunk(i), :][:, SCALE0 : SCALE0 + 1]
        v = xt[chunk(i), :].astype(F32) + scale * attn_o[chunk(i), :]
        hat_o[chunk(i), :] = v
        return acc + fold(v)

    mean = across(passes(width, residual, zero)) / width
    mid_o[...] = hat_o[:, pl.ds(pl.multiple_of(m * rows, rows), rows)]

    def spread(i, acc):
        v = hat_o[chunk(i), :] - mean
        return acc + fold(v * v)

    rstd = lax.rsqrt(across(passes(width, spread, zero)) / width + norm_eps)
    rstd_o[0:1, :] = rstd

    def norm(i, carry):
        w = cols[chunk(i), :]
        v = (hat_o[chunk(i), :] - mean) * rstd
        hat_o[chunk(i), :] = v
        h2_o[chunk(i), :] = (v * w[:, GAIN1 : GAIN1 + 1] + w[:, BIAS1 : BIAS1 + 1]).astype(BF16)
        return carry

    passes(width, norm, 0)
    wide[...] = nn(w_up_t[...], h2_o[...])

    def gelu(i, carry):
        u = wide[chunk(i), :]
        cdf = 0.5 + 0.5 * lax.erf(u * (0.5**0.5))
        act_o[chunk(i), :] = (u * cdf).astype(BF16)
        slope_o[chunk(i), :] = cdf + u * (jnp.exp(-0.5 * u * u) * 0.3989422804014327)
        return carry

    passes(hidden, gelu, 0)
    mlp_o[...] = nn(w_down_t[...], act_o[...])
    put_halves(m, mlp_o, m0, m2, m13)


def down_kernel(
    place, c0, c1, c2, c3, cols, attn, hat, rstd, slope, w_out, w_up, w_down,
    d0, d1, d2, d3, nb_o, dup_o, gm_o, ga_o, dy_o, vec_o,
    wide, sums,
):
    m = place[0]
    rows = c0.shape[0]
    channels = d0.shape[0]
    width, tokens = hat.shape
    hidden = slope.shape[0]
    for k, c in enumerate((c0, c1, c2, c3)):
        at = pl.ds(pl.multiple_of((m ^ k) * rows, rows), rows)
        turned = c[...].T
        dy_o[:, at] = turned
        scale = cols[:, SCALE1 : SCALE1 + 1]
        gm_o[:, at] = (turned.astype(F32) * scale).astype(BF16)
    wide[...] = nn(w_down[...], gm_o[...])

    def d_up(i, carry):
        dup_o[chunk(i), :] = (slope[chunk(i), :] * wide[chunk(i), :]).astype(BF16)
        return carry

    passes(hidden, d_up, 0)
    wide[...] = nn(w_up[...], dup_o[...])
    zero = jnp.zeros((8, tokens), F32)

    def gather(i, acc):
        d = wide[chunk(i), :]
        u = d * cols[chunk(i), :][:, GAIN1 : GAIN1 + 1]
        return acc[0] + fold(u), acc[1] + fold(u * hat[chunk(i), :])

    first, second = passes(width, gather, (zero, zero))
    first, second = across(first) / width, across(second) / width
    lane = lax.broadcasted_iota(jnp.int32, (1, tokens), 1)
    mine = ((lane >= m * rows) & (lane < (m + 1) * rows)).astype(F32)
    rstd = rstd[0:1, :]

    def back(i, carry):
        w = cols[chunk(i), :]
        d = wide[chunk(i), :]
        h = hat[chunk(i), :]
        v = rstd * (d * w[:, GAIN1 : GAIN1 + 1] - first - h * second)
        nb_o[chunk(i), :] = v
        v = v + mine * dy_o[chunk(i), :].astype(F32)
        ga_o[chunk(i), :] = (v * w[:, SCALE0 : SCALE0 + 1]).astype(BF16)
        sums[chunk(i), 0:1] = jnp.sum(d * h, axis=1, keepdims=True)
        sums[chunk(i), 1:2] = jnp.sum(d, axis=1, keepdims=True)
        sums[chunk(i), 2:3] = jnp.sum(v * attn[chunk(i), :], axis=1, keepdims=True)
        return carry

    passes(width, back, 0)
    wide[...] = nn(w_out[...], ga_o[...])
    for k, ref in enumerate((d0, d1, d2, d3)):
        at = pl.ds(pl.multiple_of((m ^ k) * channels, channels), channels)
        ref[...] = wide[at, :].astype(BF16)
    turned = sums[...].T
    vec_o[...] = jnp.zeros(vec_o.shape, F32)
    vec_o[1:2, :] = turned[0:1, :]
    vec_o[3:4, :] = turned[1:2, :]
    vec_o[4:5, :] = turned[2:3, :]


def mlp_grad_kernel(place, vec, mlp, act, dup, gm, ga, att, h2, dy, vec_o, *rest):
    grads, sums = rest[:-1], rest[-1]

    def scale(i, carry):
        v = dy[chunk(i), :].astype(F32) * mlp[chunk(i), :]
        sums[chunk(i), 0:1] = jnp.sum(v, axis=1, keepdims=True)
        return carry

    passes(dy.shape[0], scale, 0)
    vec_o[...] = vec[...]
    vec_o[5:6, :] = sums[...].T[0:1, :]
    if len(grads) == 1:
        at = 0
        for a, b in ((h2, dup), (gm, act), (ga, att)):
            grads[0][:, at : at + b.shape[0]] = nt(a[...], b[...]).astype(BF16)
            at += b.shape[0]
        return
    x, y = (place[1] >> 1) & 1, (place[1] >> 2) & 1
    a_sent, a_kept, b_sent, b_kept = grads
    n, half = a_sent.shape[0] // 4, a_sent.shape[1]

    def put(p, left, low, high):
        block = [p[i * n : (i + 1) * n, low:high] for i in range(8)]
        first = left + low < half
        at = left + low - (0 if first else half)
        cols = slice(at, at + high - low)
        for i in range(4):
            out = slice(i * n, (i + 1) * n)
            if first:
                zero, one = 4 * (i // 2) + i % 2, 4 * (i // 2) + 2 + i % 2
                a_sent[out, cols] = pick(x, block[one], block[zero])
                a_kept[out, cols] = pick(x, block[zero], block[one])
            else:
                b_sent[out, cols] = pick(y, block[4 + i], block[i])
                b_kept[out, cols] = pick(y, block[i], block[4 + i])

    left = 0
    for a, b in ((h2, dup), (gm, act), (ga, att)):
        p = nt(a[...], b[...]).astype(BF16)
        n_cols = p.shape[1]
        cut = min(max(half - left, 0), n_cols)
        if cut > 0:
            put(p, left, 0, cut)
        if cut < n_cols:
            put(p, left, cut, n_cols)
        left += n_cols


def put_halves(m, ref, own, next_to, sent):
    rows, width = own.shape[1], own.shape[0]

    def of(k):
        return ref[:, pl.ds(pl.multiple_of((m ^ k) * rows, rows), rows)]

    own[...], next_to[...] = of(0), of(2)
    sent[0:width, :] = of(1).astype(BF16)
    sent[width:, :] = of(3).astype(BF16)


def halve_kernel(own, next_to, recv, own_o, sent):
    width = own.shape[0]
    own_o[...] = own[...] + recv[0:width, :].astype(F32)
    sent[...] = (next_to[...] + recv[width:, :].astype(F32)).astype(BF16)


def put_blocks(parts, here, grads):
    at = 0
    for p in parts:
        cols = slice(at, at + p.shape[1])
        at += p.shape[1]
        if len(grads) == 1:
            grads[0][:, cols] = p
            continue
        sent, kept = grads
        n = kept.shape[0] // 4
        for b in range(4):
            even, odd = p[2 * b * n : (2 * b + 1) * n], p[(2 * b + 1) * n : (2 * b + 2) * n]
            sent[b * n : (b + 1) * n, cols] = pick(here, odd, even)
            kept[b * n : (b + 1) * n, cols] = pick(here, even, odd)


def pick(bit, a, b):
    return jnp.where(bit == 0, a, b)


def back_kernel(
    place, lengths, d0, d1, d2, d3, qkv, pt, xt, stat, nb, cols, wq_t, vec,
    p0, p2, p13, dqkv_o, vec_o,
    score, ds, acc, buckets_of, wide, sums,
):
    m = place[0]
    channels, tokens = d0.shape
    heads = channels // HEAD_DIM
    width = xt.shape[0]
    rows = p0.shape[1]
    blk = 128
    n_blk = tokens // blk
    n_rows = buckets_of.shape[0]
    buckets = n_rows // heads
    half = buckets // 2
    live = (page_ids(lengths, (1, tokens), 1, -1) >= 0).astype(F32)
    off = lax.broadcasted_iota(jnp.int32, (blk, blk), 1) - lax.broadcasted_iota(
        jnp.int32, (blk, blk), 0
    )

    def one_head(h, carry):
        def rows_of(which):
            return pl.ds(pl.multiple_of(which * channels + h * HEAD_DIM, HEAD_DIM), HEAD_DIM)

        q, k, v = qkv[rows_of(0), :], qkv[rows_of(1), :], qkv[rows_of(2), :]
        mine = rows_of(0)
        d_att = (
            d0[mine, :].astype(F32) + d1[mine, :].astype(F32)
            + d2[mine, :].astype(F32) + d3[mine, :].astype(F32)
        )
        d_att = (d_att.astype(BF16).astype(F32) * live).astype(BF16)
        dqkv_o[rows_of(2), :] = nt(d_att, pt[h]).astype(BF16)
        score[...] = nn(v.T, d_att)
        acc[...] = jnp.zeros(acc.shape, F32)
        for i in range(n_blk):
            lanes = slice(i * blk, (i + 1) * blk)
            total = jnp.zeros((8, blk), F32)
            for j in range(n_blk):
                at = slice(j * blk, (j + 1) * blk)
                prod = score[at, lanes] * pt[h, at, lanes].astype(F32)
                score[at, lanes] = prod
                total = total + fold(prod)
            total = across(total)
            for j in range(n_blk):
                at = slice(j * blk, (j + 1) * blk)
                g = score[at, lanes] - pt[h, at, lanes].astype(F32) * total
                g = g.astype(BF16)
                ds[at, lanes] = g
                slot = max(min(i - j, 2), -2) + 2
                acc[slot] = acc[slot] + g.astype(F32)
        dqkv_o[rows_of(0), :] = (nn(k, ds[...]) * HEAD_DIM**-0.5).astype(BF16)
        dqkv_o[rows_of(1), :] = nt(q, ds[...]).astype(BF16)
        near, before, after = acc[2], acc[1], acc[3]
        corner_b, off_b = before[0:16, :], off[0:16, :] - blk
        corner_a, off_a = after[blk - 16 : blk, :], off[blk - 16 : blk, :] + blk
        first = h * buckets
        for b in range(buckets):
            if b == 0:
                v = fold(acc[0]) + fold(jnp.where(off - blk <= -half, before, 0.0))
                v = v + fold(jnp.where(off <= -half, near, 0.0))
            elif b == buckets - 1:
                v = fold(acc[4]) + fold(jnp.where(off + blk >= half - 1, after, 0.0))
                v = v + fold(jnp.where(off >= half - 1, near, 0.0))
            else:
                v = fold(jnp.where(off == b - half, near, 0.0))
                if b < half:
                    v = v + fold(jnp.where(off_b == b - half, corner_b, 0.0))
                elif b > half:
                    v = v + fold(jnp.where(off_a == b - half, corner_a, 0.0))
            buckets_of[pl.ds(first + b, 1), :] = across(v)
        return carry

    lax.fori_loop(0, heads, one_head, 0, unroll=True)
    wide[...] = nn(wq_t[...], dqkv_o[...])
    mean, rstd = stat[0:1, :], stat[1:2, :]
    zero = jnp.zeros((8, tokens), F32)

    def gather(i, part):
        d = wide[chunk(i), :]
        hat = (xt[chunk(i), :].astype(F32) - mean) * rstd
        u = d * cols[chunk(i), :][:, GAIN0 : GAIN0 + 1]
        sums[chunk(i), 0:1] = jnp.sum(d * hat, axis=1, keepdims=True)
        sums[chunk(i), 1:2] = jnp.sum(d, axis=1, keepdims=True)
        return part[0] + fold(u), part[1] + fold(u * hat)

    first, second = passes(width, gather, (zero, zero))
    first, second = across(first) / width, across(second) / width

    def back(i, carry):
        hat = (xt[chunk(i), :].astype(F32) - mean) * rstd
        u = wide[chunk(i), :] * cols[chunk(i), :][:, GAIN0 : GAIN0 + 1]
        wide[chunk(i), :] = nb[chunk(i), :] + rstd * (u - first - hat * second)
        return carry

    passes(width, back, 0)
    put_halves(m, wide, p0, p2, p13)
    turned = sums[...].T
    vec_o[...] = vec[...]
    vec_o[0:1, :] = turned[0:1, :]
    vec_o[2:3, :] = turned[1:2, :]
    each = jnp.sum(buckets_of[...], axis=1, keepdims=True)
    shape = (n_rows, width)
    lane = lax.broadcasted_iota(jnp.int32, shape, 1)
    row = lax.broadcasted_iota(jnp.int32, shape, 0)
    vec_o[6:7, :] = across(jnp.where(lane == row + m * n_rows, each, 0.0))


def qkv_grad_kernel(place, h1, dqkv, vec, *grads):
    put_blocks([nt(h1[...], dqkv[...]).astype(BF16)], place[1] & 1, grads)
    if len(grads) > 1:
        put_vec(vec[...], grads[0])


def put_vec(vec, ref):
    half = vec.shape[1] // 2
    v = jnp.concatenate([vec[:, :half], vec[:, half:]])
    high = v.astype(BF16)
    n, rows = ref.shape[0], v.shape[0]
    ref[n - 2 * rows : n - rows, :half] = high
    ref[n - rows :, :half] = (v - high.astype(F32)).astype(BF16)


def get_vec(ref, width):
    n, rows, half = ref.shape[0], 16, width // 2
    v = ref[n - 2 * rows : n - rows, :half].astype(F32) + ref[n - rows :, :half].astype(F32)
    return jnp.concatenate([v[:8], v[8:]], axis=1)


def grads_second_kernel(place, a_keep, a_recv, b_keep, b_recv, s0, s1, s2, kept):
    core = place[1] & 1
    half, n, third = a_keep.shape[1], kept.shape[0] // 2, s0.shape[1]
    for j, sent in enumerate((s0, s1, s2)):
        for keep, recv, low, high in (
            (a_keep, a_recv, j * third, min((j + 1) * third, half)),
            (b_keep, b_recv, max(j * third, half) - half, (j + 1) * third - half),
        ):
            if low >= high:
                continue
            at = low + (half if keep is b_keep else 0)
            from_, to = slice(low, high), slice(at - j * third, at - j * third + high - low)
            for i in range(2):
                rows = pl.ds(pl.multiple_of(2 * i * n, 2 * n), 2 * n)
                out = slice(i * n, (i + 1) * n)
                halve_rows(
                    core, keep.at[rows, from_], recv.at[rows, from_],
                    sent.at[out, to], kept.at[out, at : at + high - low],
                )


def grads_third_kernel(place, keep, r0, r1, r2, a_sent, a_kept, b_sent, b_kept):
    x, y = (place[1] >> 1) & 1, (place[1] >> 2) & 1
    half, third = a_kept.shape[1], r0.shape[1]
    for j, recv in enumerate((r0, r1, r2)):
        low, high = j * third, (j + 1) * third
        for bit, sent, kept, first, start, stop in (
            (y, a_sent, a_kept, 0, low, min(high, half)),
            (x, b_sent, b_kept, half, max(low, half), high),
        ):
            if start >= stop:
                continue
            out = slice(start - first, stop - first)
            halve_rows(
                bit, keep.at[:, start:stop], recv.at[:, start - low : stop - low],
                sent.at[:, out], kept.at[:, out],
            )


def halve_rows(bit, keep, recv, sent, kept):
    n = kept.shape[0]
    for ref, b in ((sent, 1 - bit), (kept, bit)):
        rows = pl.ds(pl.multiple_of(b * n, n), n)
        total = keep[rows, :].astype(F32) + recv[rows, :].astype(F32)
        ref[0:n, :] = total.astype(ref.dtype)


def qkv_second_kernel(place, vec, keep, recv, sent, kept, vec_o):
    x = (place[1] >> 1) & 1
    n = kept.shape[0] // 2
    for i in range(2):
        for ref, b in ((sent, 1 - x), (kept, x)):
            rows = pl.ds(pl.multiple_of((2 * i + b) * n, n), n)
            total = keep[rows, :].astype(F32) + recv[rows, :].astype(F32)
            ref[i * n : (i + 1) * n, :] = total.astype(ref.dtype)
    vec_o[...] = vec[...] + get_vec(recv, vec.shape[1])
    put_vec(vec_o[...], sent)


def qkv_third_kernel(place, vec, keep, recv, sent, kept, vec_o):
    halve_rows((place[1] >> 2) & 1, keep, recv, sent, kept)
    vec_o[...] = vec[...] + get_vec(recv, vec.shape[1])
    put_vec(vec_o[...], sent)


def message_kernel(place, vec, b_keep, b_recv, q_recv, vec_o, o0, o1, o2, o3, turned):
    m = place[0]
    channels = o0.shape[0]
    width, share = turned.shape
    cols = slice(b_keep.shape[1] - width, b_keep.shape[1])
    turned[...] = (b_keep[:, cols] + b_recv[:, cols].astype(F32)).T
    v = vec[...] + get_vec(q_recv, vec.shape[1])
    vec_o[...] = v
    tiles = v.shape[1] // 128
    high = v.astype(BF16)
    low = (v - high.astype(F32)).astype(BF16)
    both = jnp.concatenate([high.astype(F32), low.astype(F32)]).astype(BF16)
    for k, ref in enumerate((o0, o1, o2, o3)):
        t = turned[pl.ds(pl.multiple_of((m ^ k) * channels, channels), channels), :]
        ref[0:channels, 0:share] = t.astype(ref.dtype)
        if k:
            for i in range(tiles):
                at = channels + 16 * i
                ref[at : at + 16, :] = both[:, 128 * i : 128 * (i + 1)]


def last_kernel(a_keep, a_recv, b_keep, b_recv, q_keep, q_recv, up_o, down_o, qkv_o):
    hidden = up_o.shape[1]
    channels = qkv_o.shape[2]
    a = a_keep[...] + a_recv[...].astype(F32)
    share, half = a.shape
    rest = slice(0, 2 * hidden - half)
    up_o[...] = a[:, :hidden]
    down_o[:, : half - hidden] = a[:, hidden:]
    down_o[:, half - hidden :] = b_keep[:, rest] + b_recv[:, rest].astype(F32)
    q = q_keep[...] + q_recv[0:share, :].astype(F32)
    for i in range(3):
        qkv_o[i] = q[:, i * channels : (i + 1) * channels]


def small_kernel(vec, o0, o1, o2, o3, out, gains, biases, scales, table):
    channels, share = out.shape
    others = (o1, o2, o3)
    total = o0[...]
    v = vec[...]
    for ref in others:
        total = total + ref[0:channels, 0:share].astype(F32)
        parts = []
        for i in range(v.shape[1] // 128):
            at = channels + 16 * i
            both = ref[at : at + 16, :].astype(F32)
            parts.append(both[:8] + both[8:])
        v = v + jnp.concatenate(parts, axis=1)
    out[...] = total
    gains[...] = v[0:2]
    biases[...] = v[2:4]
    scales[...] = v[4:6]
    n = table.shape[1]
    for h in range(table.shape[0]):
        table[h : h + 1, :] = v[6:7, h * n : (h + 1) * n]


def input_kernel(own, recv, dy, out):
    total = own[...] + recv[...].astype(F32)
    out[...] = (dy[...].astype(F32) + total.T).astype(BF16)


def output_kernel(own, recv, mid, cols, out):
    total = own[...] + recv[...].astype(F32)
    out[...] = (mid[...] + cols[:, SCALE1 : SCALE1 + 1] * total).T.astype(BF16)


def body(
    tokens,
    page_lengths,
    norm_gains,
    norm_biases,
    layer_scales,
    w_qkv,
    rel_table,
    w_out,
    w_up,
    w_down,
    cotangent,
):
    mp, dp = lax.axis_size("mp"), lax.axis_size("dp")
    rows, width = tokens.shape
    group = rows * mp
    channels = w_qkv.shape[2]
    hidden = w_up.shape[1]
    heads = channels // HEAD_DIM
    buckets = rel_table.shape[0]
    m, d = lax.axis_index("mp"), lax.axis_index("dp")
    place = jnp.stack([m, d]).astype(jnp.int32)

    def swap(v, k, axis="mp", name="rows"):
        n = mp if axis == "mp" else dp
        with jax.named_scope(name):
            return lax.ppermute(v, axis, [(i, i ^ k) for i in range(n)])

    def after(v, *seen):
        return lax.optimization_barrier((v,) + seen)[0]

    fast = dp == 8 and (width // dp) % 16 == 0 and hidden == width

    cols = jnp.concatenate(
        [norm_gains[0:1], norm_biases[0:1], norm_gains[1:2], norm_biases[1:2], layer_scales]
    ).T
    wq = jnp.transpose(w_qkv, (1, 2, 0)).reshape(3 * channels, width)

    piece = channels // 4
    sent = jnp.concatenate([tokens, lax.dynamic_slice_in_dim(w_out, (d & 3) * piece, piece, 0)])
    x1, x2 = swap(sent, 1, name="x"), swap(sent, 2, name="x")
    x = [sent, x1, x2, swap(after(x2, x1), 1, name="x")]
    dy2 = swap(after(cotangent, x1, x2), 2, name="dy")
    wq_t, w_up_t, w_down_t = call(
        turn_kernel,
        [like((width, 3 * channels), BF16), like((hidden, width), BF16), like((width, hidden), BF16)],
        [wq, w_up, w_down],
    )
    x[1:] = lax.optimization_barrier((x[1:], wq_t))[0]
    (part,) = call(pieces_kernel, [like((4, piece, width), BF16)], x)
    part_x = swap(part, 2, "dp", name="w")
    wq_now = after(wq, wq_t, w_up_t, w_down_t, dy2)
    xt, h1, stat, qkv, pt, att = call(
        head_kernel,
        [
            like((width, group), BF16),
            like((width, group), BF16),
            like((8, group), F32),
            like((3 * channels, group), BF16),
            like((heads, group, group), BF16),
            like((channels, group), BF16),
        ],
        [place, page_lengths, rel_table] + x + [cols, wq_now],
        n_smem=3,
        scratch=[
            pltpu.VMEM((group, group), F32),
            pltpu.VMEM((group, 128), jnp.int32),
            pltpu.VMEM((3, 128, 128), F32),
        ],
        us=10,
    )
    (parts,) = call(pair_kernel, [like((8, piece, width), BF16)], [part, after(part_x, att)])
    att_sent = after(att, parts)
    dy1 = swap(after(cotangent, parts), 1, name="dy")
    atts = [att] + [swap(att_sent, k, name="att") for k in (1, 2, 3)]
    dy = [cotangent, dy1, dy2, swap(after(dy2, parts), 1, name="dy")]
    w_pieces = [parts, swap(parts, 1, "dp", name="w")]
    w_out_full, w_out_t = call(
        out_weight_kernel, [like((width, width), BF16)] * 2, [place] + w_pieces, n_smem=1
    )
    act_like = like((width, group), BF16)
    hid_like = like((hidden, group), BF16)
    wide_like = like((width, group), F32)
    block = like((width, rows), F32)
    blocks = [block, block, like((2 * width, rows), BF16)]
    att_all, attn, hat, rstd, h2, act, slope, mid, mlp_part, m0, m2, m13 = call(
        up_kernel,
        [act_like, wide_like, wide_like, like((8, group), F32), act_like, hid_like]
        + [like((hidden, group), F32), block, wide_like]
        + blocks,
        [place] + atts + [after(xt, dy1), cols, w_out_t, w_up_t, w_down_t],
        n_smem=1,
        scratch=[pltpu.VMEM((hidden, group), F32)],
        us=10,
    )
    m_recv = swap(m13, 1, name="mlp")
    d0, d1, d2, d3, nb, dup, gm, ga, dy_t, vec = call(
        down_kernel,
        [like((channels, group), BF16)] * 4
        + [wide_like, hid_like, act_like, act_like, act_like, like((8, width), F32)],
        [place] + dy + [cols, attn, hat, rstd, slope, w_out_full, w_up, w_down],
        n_smem=1,
        scratch=[pltpu.VMEM((max(width, hidden), group), F32), pltpu.VMEM((width, 128), F32)],
        us=10,
    )
    d_att = [d0] + [swap(v, k, name="d_att") for k, v in ((1, d1), (2, d2), (3, d3))]
    grad_cols = 2 * hidden + width
    share = width // dp
    half = grad_cols // 2
    if fast:
        grad_like = [like((width // 2, half), BF16)] * 4
    else:
        grad_like = [like((width, grad_cols), BF16)]
    vec, *grads = call(
        mlp_grad_kernel,
        [like((8, width), F32)] + grad_like,
        [place, vec, mlp_part, act, dup, gm, ga, att_all, h2, dy_t],
        n_smem=1,
        scratch=[pltpu.VMEM((width, 128), F32)],
    )
    if fast:
        a_sent, a_kept, b_sent, b_kept = grads
        a_recv = swap(a_sent, 2, "dp", name="grads_a")
        b_recv = swap(b_sent, 4, "dp", name="grads_b")

    def halved(own, next_to, recv, name, us=0.01, seen=()):
        half_like = [block, like((width, rows), BF16)]
        own, sent = call(halve_kernel, half_like, [own, next_to, recv], us=us)
        return [own, swap(after(sent, *seen), 2, name=name)]

    mlp = halved(m0, m2, m_recv, "mlp", seen=d_att[1:])

    p0, p2, p13, dqkv, vec = call(
        back_kernel,
        blocks + [like((3 * channels, group), BF16), like((8, width), F32)],
        [place, page_lengths] + d_att + [qkv, pt, xt, stat, nb, cols, wq_t, vec],
        n_smem=2,
        scratch=[
            pltpu.VMEM((group, group), F32),
            pltpu.VMEM((group, group), BF16),
            pltpu.VMEM((5, 128, 128), F32),
            pltpu.VMEM((heads * buckets, 128), F32),
            pltpu.VMEM((width, group), F32),
            pltpu.VMEM((width, 128), F32),
        ],
        us=10,
    )
    p_recv = swap(after(p13, mlp[1]), 1, name="back")
    back = halved(p0, p2, p_recv, "back", us=10)
    n = 3 * channels
    extra = 4 * vec.shape[0]
    if fast:
        grad_like = [like((width // 2 + extra, n), BF16), like((width // 2, n), BF16)]
    else:
        grad_like = [like((width, n), BF16)]
    qkv_grads = call(qkv_grad_kernel, grad_like, [place, h1, dqkv, vec], n_smem=1)

    def reduced(g):
        g = g.reshape(dp, width // dp, g.shape[1])
        bit = 1
        while bit < dp:
            g = g.reshape(g.shape[0] // 2, 2, width // dp, g.shape[-1])
            here = (d & bit) // bit
            sent = lax.dynamic_index_in_dim(g, 1 - here, 1, keepdims=False)
            kept = lax.dynamic_index_in_dim(g, here, 1, keepdims=False)
            g = kept.astype(F32) + swap(sent, bit, "dp").astype(F32)
            bit *= 2
            if bit < dp:
                g = g.astype(BF16)
        return g[0]

    if fast:
        q_recv = swap(after(qkv_grads[0], mlp[1]), 1, "dp", name="qkv_core")
        vec_like = [like(vec.shape, F32)]
        sent, kept, vec = call(
            qkv_second_kernel,
            [like((2 * share + extra, n), BF16), like((2 * share, n), F32)] + vec_like,
            [place, vec, qkv_grads[1], q_recv],
            n_smem=1,
        )
        recv = swap(sent, 2, "dp", name="qkv_x")
        g0, g1, g2, g_kept = call(
            grads_second_kernel,
            [like((2 * share, grad_cols // 3), BF16)] * 3 + [like((2 * share, grad_cols), BF16)],
            [place, after(a_kept, vec), a_recv, b_kept, b_recv],
            n_smem=1,
        )
        g_recv = [swap(g, 1, "dp", name="grads_core") for g in (g0, g1, g2)]
        a_sent, a_kept, b_sent, b_kept = call(
            grads_third_kernel,
            [like((share, half), BF16), like((share, half), F32)] * 2,
            [place, g_kept] + g_recv,
            n_smem=1,
        )
        a_recv = swap(a_sent, 4, "dp", name="grads_a")
        b_recv = swap(b_sent, 2, "dp", name="grads_b")
        sent, kept, vec = call(
            qkv_third_kernel,
            [like((share + extra, n), BF16), like((share, n), F32)] + vec_like,
            [place, after(vec, a_kept, back[0]), kept, recv],
            n_smem=1,
        )
        recv = swap(sent, 4, "dp", name="qkv_y")
        message = like((channels + 2 * vec.size // 128, 128), BF16)
        vec, o0, o1, o2, o3 = call(
            message_kernel,
            vec_like + [like((channels, share), F32)] + [message] * 3,
            [place, vec, b_kept, b_recv, recv],
            n_smem=1,
            scratch=[pltpu.VMEM((width, share), F32)],
        )
        grad_up, grad_down, grad_qkv = call(
            last_kernel,
            [like((share, hidden), F32)] * 2 + [like((3, share, channels), F32)],
            [a_kept, a_recv, b_kept, b_recv, after(kept, o1), recv],
        )
        o1, o2, o3 = (swap(v, k, name="out") for k, v in ((1, o1), (2, o2), (3, o3)))
        grad_out, gains, biases, scales, grad_table = call(
            small_kernel,
            [like((channels, share), F32)]
            + [like((2, width), F32)] * 3
            + [like((heads * mp, buckets), F32)],
            [vec, o0, o1, o2, o3],
        )
        grad_qkv = jnp.transpose(grad_qkv, (1, 0, 2))
    else:
        summed = reduced(grads[0])
        grad_qkv = reduced(qkv_grads[0]).reshape(share, 3, channels)
        grad_up, grad_down = summed[:, :hidden], summed[:, hidden : 2 * hidden]
        turned = summed[:, 2 * hidden :].T

        def out_part(k):
            return lax.dynamic_slice_in_dim(turned, (m ^ k) * channels, channels, 0)

        grad_out = out_part(0)
        for k in range(1, mp):
            grad_out = grad_out + swap(out_part(k).astype(BF16), k).astype(F32)
        bit = 1
        while bit < dp:
            vec = vec + swap(vec, bit, "dp", name="vec")
            bit *= 2
        for k in (1, 2):
            vec = vec + swap(vec, k, name="vec")
        gains, biases, scales = vec[0:2], vec[2:4], vec[4:6]
        grad_table = vec[6, : heads * mp * buckets].reshape(heads * mp, buckets)

    (output,) = call(output_kernel, [like((rows, width), BF16)], mlp + [mid, cols])
    (grad_input,) = call(input_kernel, [like((rows, width), BF16)], back + [cotangent], us=10)
    return (
        output,
        grad_input,
        gains,
        biases,
        scales,
        grad_qkv,
        grad_table.T,
        grad_out,
        grad_up,
        grad_down.T,
    )


def solution(mesh):
    placed = (
        P(("dp", "mp"), None),
        P("dp", None),
        P(),
        P(),
        P(),
        P(None, None, "mp"),
        P(),
        P("mp", None),
        P(None, "mp"),
        P("mp", None),
        P(("dp", "mp"), None),
    )
    return jax.shard_map(
        body,
        mesh=mesh,
        in_specs=placed,
        out_specs=(
            P(("dp", "mp"), None),
            P(("dp", "mp"), None),
            P(),
            P(),
            P(),
            P("dp", None, "mp"),
            P(),
            P("mp", "dp"),
            P("dp", "mp"),
            P("mp", "dp"),
        ),
        check_vma=False,
    )
```

```python
import jax
import jax.numpy as jnp
from jax import lax
from jax.experimental import pallas as pl
from jax.experimental.pallas import tpu as pltpu
from jax.sharding import PartitionSpec as P

HEAD_DIM = 64
SPEED = 1.15e9
norm_eps = 1e-06
masked_score = -1000000000.0
F32 = jnp.float32
BF16 = jnp.bfloat16
SMEM = pl.BlockSpec(memory_space=pltpu.SMEM)
VMEM = pl.BlockSpec(memory_space=pltpu.VMEM)
CHUNK = 64
GAIN0, BIAS0, GAIN1, BIAS1, SCALE0, SCALE1 = range(6)


def call(kernel, outs, args, n_smem=0, scratch=(), us=0.01, limit=8):
    return pl.pallas_call(
        kernel,
        out_shape=tuple(outs),
        in_specs=[SMEM] * n_smem + [VMEM] * (len(args) - n_smem),
        out_specs=tuple([VMEM] * len(outs)),
        scratch_shapes=list(scratch),
        compiler_params=pltpu.CompilerParams(vmem_limit_bytes=limit << 20),
        name=kernel.__name__,
        cost_estimate=pl.CostEstimate(flops=int(us * SPEED), bytes_accessed=8, transcendentals=0),
    )(*args)


def like(shape, dtype):
    return jax.ShapeDtypeStruct(shape, dtype)


def nn(a, b):
    return lax.dot_general(a, b, (((1,), (0,)), ((), ())), preferred_element_type=F32)


def nt(a, b):
    return lax.dot_general(a, b, (((1,), (1,)), ((), ())), preferred_element_type=F32)


def fold(v):
    return jnp.sum(v.reshape(v.shape[0] // 8, 8, v.shape[1]), axis=0)


def across(v):
    return jnp.sum(v, axis=0, keepdims=True)


def passes(rows, step, start):
    return lax.fori_loop(0, rows // CHUNK, step, start, unroll=True)


def chunk(i):
    return pl.ds(pl.multiple_of(i * CHUNK, CHUNK), CHUNK)


def page_ids(lengths, shape, axis, dead):
    at = lax.broadcasted_iota(jnp.int32, shape, axis)
    page = jnp.zeros(shape, jnp.int32)
    end = jnp.int32(0)
    pages = lengths.shape[1]
    for p in range(pages):
        end = end + lengths[0, p]
        page = page + (at >= end).astype(jnp.int32)
    return jnp.where(page < pages - 1, page, dead)


def turn_kernel(wq, wu, wd, wq_o, wu_o, wd_o):
    wq_o[...] = wq[...].T
    wu_o[...] = wu[...].T
    wd_o[...] = wd[...].T


def pieces_kernel(x0, x1, x2, x3, out):
    n = out.shape[1]
    for k, ref in enumerate((x0, x1, x2, x3)):
        out[k] = ref[ref.shape[0] - n :, :]


def pair_kernel(a, b, out):
    out[0:4] = a[...]
    out[4:8] = b[...]


def out_weight_kernel(place, here, there, w_o, wt_o):
    m, d = place[0], place[1]
    rows = here.shape[1]
    for c, ref in enumerate((here, there)):
        for b in range(2):
            part = (d & 3) ^ (c + 2 * b)
            for k in range(4):
                at = pl.multiple_of((m ^ k) * 4 * rows + part * rows, rows)
                w_o[pl.ds(at, rows), :] = ref[4 * b + k]
    wt_o[...] = w_o[...].T


def head_kernel(
    place, lengths, table, x0, x1, x2, x3, cols, wq,
    xt_o, h1_o, stat_o, qkv_o, pt_o, att_o,
    score, ids, pattern,
):
    m = place[0]
    width, tokens = xt_o.shape
    rows = tokens // 4
    channels = att_o.shape[0]
    heads = channels // HEAD_DIM
    buckets = table.shape[0]
    half = buckets // 2
    for k, ref in enumerate((x0, x1, x2, x3)):
        at = pl.multiple_of((m ^ k) * rows, rows)
        xt_o[:, pl.ds(at, rows)] = ref[0:rows, :].T

    def add(i, acc):
        return acc + fold(xt_o[chunk(i), :].astype(F32))

    zero = jnp.zeros((8, tokens), F32)
    mean = across(passes(width, add, zero)) / width

    def spread(i, acc):
        v = xt_o[chunk(i), :].astype(F32) - mean
        return acc + fold(v * v)

    rstd = lax.rsqrt(across(passes(width, spread, zero)) / width + norm_eps)
    stat_o[0:1, :] = mean
    stat_o[1:2, :] = rstd

    def norm(i, carry):
        v = (xt_o[chunk(i), :].astype(F32) - mean) * rstd
        w = cols[chunk(i), :]
        h1_o[chunk(i), :] = (v * w[:, GAIN0 : GAIN0 + 1] + w[:, BIAS0 : BIAS0 + 1]).astype(BF16)
        return carry

    passes(width, norm, 0)
    qkv_o[...] = nn(wq[...], h1_o[...]).astype(BF16)
    qkv_o[0:channels, :] = qkv_o[0:channels, :] * BF16(HEAD_DIM**-0.5)

    ids[...] = page_ids(lengths, ids.shape, 0, -2)
    own_ids = page_ids(lengths, (1, tokens), 1, -1)
    live = (own_ids >= 0).astype(F32)
    blk = 128
    n_blk = tokens // blk
    off = lax.broadcasted_iota(jnp.int32, (blk, blk), 1) - lax.broadcasted_iota(
        jnp.int32, (blk, blk), 0
    )

    def one_head(h, carry):
        col = m * heads + h
        low, high = table[0, col], table[buckets - 1, col]
        near = jnp.where(off >= half - 1, high, low)
        for b in range(1, buckets - 1):
            near = jnp.where(off == b - half, table[b, col], near)
        pattern[1] = near
        before = jnp.full((blk, blk), low, F32)
        for b in range(1, half):
            before = jnp.where(off - blk == b - half, table[b, col], before)
        pattern[0] = before
        after = jnp.full((blk, blk), high, F32)
        for b in range(half + 1, buckets - 1):
            after = jnp.where(off + blk == b - half, table[b, col], after)
        pattern[2] = after

        def rows_of(which):
            return pl.ds(pl.multiple_of(which * channels + h * HEAD_DIM, HEAD_DIM), HEAD_DIM)

        q, k, v = qkv_o[rows_of(0), :], qkv_o[rows_of(1), :], qkv_o[rows_of(2), :]
        score[...] = nn(k.T, q)
        for i in range(n_blk):
            lanes = slice(i * blk, (i + 1) * blk)
            query_id = own_ids[:, lanes]
            top = jnp.full((8, blk), -3e38, F32)
            for j in range(n_blk):
                at = slice(j * blk, (j + 1) * blk)
                if abs(i - j) <= 1:
                    bias = pattern[i - j + 1]
                else:
                    bias = low if i < j else high
                s = jnp.where(ids[at, :] == query_id, score[at, lanes] + bias, masked_score)
                score[at, lanes] = s
                top = jnp.maximum(top, jnp.max(s.reshape(blk // 8, 8, blk), axis=0))
            top = jnp.max(top, axis=0, keepdims=True)
            total = jnp.zeros((8, blk), F32)
            for j in range(n_blk):
                at = slice(j * blk, (j + 1) * blk)
                e = jnp.exp(score[at, lanes] - top)
                score[at, lanes] = e
                total = total + fold(e)
            scale = 1.0 / across(total)
            for j in range(n_blk):
                at = slice(j * blk, (j + 1) * blk)
                pt_o[h, at, lanes] = (score[at, lanes] * scale).astype(BF16)
        mixed = nn(v, pt_o[h]) * live
        att_o[pl.ds(pl.multiple_of(h * HEAD_DIM, HEAD_DIM), HEAD_DIM), :] = mixed.astype(BF16)
        return carry

    lax.fori_loop(0, heads, one_head, 0, unroll=True)


def up_kernel(
    place, a0, a1, a2, a3, xt, cols, w_out_t, w_up_t, w_down_t,
    at_o, attn_o, hat_o, rstd_o, h2_o, act_o, slope_o, mid_o, mlp_o, m0, m2, m13,
    wide,
):
    m = place[0]
    rows = mid_o.shape[1]
    channels = a0.shape[0]
    width, tokens = xt.shape
    hidden = act_o.shape[0]
    for k, a in enumerate((a0, a1, a2, a3)):
        at_o[pl.ds(pl.multiple_of((m ^ k) * channels, channels), channels), :] = a[...]
    attn_o[...] = nn(w_out_t[...], at_o[...])
    zero = jnp.zeros((8, tokens), F32)

    def residual(i, acc):
        scale = cols[chunk(i), :][:, SCALE0 : SCALE0 + 1]
        v = xt[chunk(i), :].astype(F32) + scale * attn_o[chunk(i), :]
        hat_o[chunk(i), :] = v
        return acc + fold(v)

    mean = across(passes(width, residual, zero)) / width
    mid_o[...] = hat_o[:, pl.ds(pl.multiple_of(m * rows, rows), rows)]

    def spread(i, acc):
        v = hat_o[chunk(i), :] - mean
        return acc + fold(v * v)

    rstd = lax.rsqrt(across(passes(width, spread, zero)) / width + norm_eps)
    rstd_o[0:1, :] = rstd

    def norm(i, carry):
        w = cols[chunk(i), :]
        v = (hat_o[chunk(i), :] - mean) * rstd
        hat_o[chunk(i), :] = v
        h2_o[chunk(i), :] = (v * w[:, GAIN1 : GAIN1 + 1] + w[:, BIAS1 : BIAS1 + 1]).astype(BF16)
        return carry

    passes(width, norm, 0)
    wide[...] = nn(w_up_t[...], h2_o[...])

    def gelu(i, carry):
        u = wide[chunk(i), :]
        cdf = 0.5 + 0.5 * lax.erf(u * (0.5**0.5))
        act_o[chunk(i), :] = (u * cdf).astype(BF16)
        slope_o[chunk(i), :] = cdf + u * (jnp.exp(-0.5 * u * u) * 0.3989422804014327)
        return carry

    passes(hidden, gelu, 0)
    mlp_o[...] = nn(w_down_t[...], act_o[...])
    put_halves(m, mlp_o, m0, m2, m13)


def down_kernel(
    place, c0, c1, c2, c3, cols, attn, hat, rstd, slope, w_out, w_up, w_down,
    d0, d1, d2, d3, nb_o, dup_o, gm_o, ga_o, dy_o, vec_o,
    wide, sums,
):
    m = place[0]
    rows = c0.shape[0]
    channels = d0.shape[0]
    width, tokens = hat.shape
    hidden = slope.shape[0]
    for k, c in enumerate((c0, c1, c2, c3)):
        at = pl.ds(pl.multiple_of((m ^ k) * rows, rows), rows)
        turned = c[...].T
        dy_o[:, at] = turned
        scale = cols[:, SCALE1 : SCALE1 + 1]
        gm_o[:, at] = (turned.astype(F32) * scale).astype(BF16)
    wide[...] = nn(w_down[...], gm_o[...])

    def d_up(i, carry):
        dup_o[chunk(i), :] = (slope[chunk(i), :] * wide[chunk(i), :]).astype(BF16)
        return carry

    passes(hidden, d_up, 0)
    wide[...] = nn(w_up[...], dup_o[...])
    zero = jnp.zeros((8, tokens), F32)

    def gather(i, acc):
        d = wide[chunk(i), :]
        u = d * cols[chunk(i), :][:, GAIN1 : GAIN1 + 1]
        return acc[0] + fold(u), acc[1] + fold(u * hat[chunk(i), :])

    first, second = passes(width, gather, (zero, zero))
    first, second = across(first) / width, across(second) / width
    lane = lax.broadcasted_iota(jnp.int32, (1, tokens), 1)
    mine = ((lane >= m * rows) & (lane < (m + 1) * rows)).astype(F32)
    rstd = rstd[0:1, :]

    def back(i, carry):
        w = cols[chunk(i), :]
        d = wide[chunk(i), :]
        h = hat[chunk(i), :]
        v = rstd * (d * w[:, GAIN1 : GAIN1 + 1] - first - h * second)
        nb_o[chunk(i), :] = v
        v = v + mine * dy_o[chunk(i), :].astype(F32)
        ga_o[chunk(i), :] = (v * w[:, SCALE0 : SCALE0 + 1]).astype(BF16)
        sums[chunk(i), 0:1] = jnp.sum(d * h, axis=1, keepdims=True)
        sums[chunk(i), 1:2] = jnp.sum(d, axis=1, keepdims=True)
        sums[chunk(i), 2:3] = jnp.sum(v * attn[chunk(i), :], axis=1, keepdims=True)
        return carry

    passes(width, back, 0)
    wide[...] = nn(w_out[...], ga_o[...])
    for k, ref in enumerate((d0, d1, d2, d3)):
        at = pl.ds(pl.multiple_of((m ^ k) * channels, channels), channels)
        ref[...] = wide[at, :].astype(BF16)
    turned = sums[...].T
    vec_o[...] = jnp.zeros(vec_o.shape, F32)
    vec_o[1:2, :] = turned[0:1, :]
    vec_o[3:4, :] = turned[1:2, :]
    vec_o[4:5, :] = turned[2:3, :]


def mlp_grad_kernel(place, vec, mlp, act, dup, gm, ga, att, h2, dy, vec_o, *rest):
    grads, sums = rest[:-1], rest[-1]

    def scale(i, carry):
        v = dy[chunk(i), :].astype(F32) * mlp[chunk(i), :]
        sums[chunk(i), 0:1] = jnp.sum(v, axis=1, keepdims=True)
        return carry

    passes(dy.shape[0], scale, 0)
    vec_o[...] = vec[...]
    vec_o[5:6, :] = sums[...].T[0:1, :]
    if len(grads) == 1:
        at = 0
        for a, b in ((h2, dup), (gm, act), (ga, att)):
            grads[0][:, at : at + b.shape[0]] = nt(a[...], b[...]).astype(BF16)
            at += b.shape[0]
        return
    x, y = (place[1] >> 1) & 1, (place[1] >> 2) & 1
    a_sent, a_kept, b_sent, b_kept = grads
    n, half = a_sent.shape[0] // 4, a_sent.shape[1]

    def put(p, left, low, high):
        block = [p[i * n : (i + 1) * n, low:high] for i in range(8)]
        first = left + low < half
        at = left + low - (0 if first else half)
        cols = slice(at, at + high - low)
        for i in range(4):
            out = slice(i * n, (i + 1) * n)
            if first:
                zero, one = 4 * (i // 2) + i % 2, 4 * (i // 2) + 2 + i % 2
                a_sent[out, cols] = pick(x, block[one], block[zero])
                a_kept[out, cols] = pick(x, block[zero], block[one])
            else:
                b_sent[out, cols] = pick(y, block[4 + i], block[i])
                b_kept[out, cols] = pick(y, block[i], block[4 + i])

    left = 0
    for a, b in ((h2, dup), (gm, act), (ga, att)):
        p = nt(a[...], b[...]).astype(BF16)
        n_cols = p.shape[1]
        cut = min(max(half - left, 0), n_cols)
        if cut > 0:
            put(p, left, 0, cut)
        if cut < n_cols:
            put(p, left, cut, n_cols)
        left += n_cols


def put_halves(m, ref, own, next_to, sent):
    rows, width = own.shape[1], own.shape[0]

    def of(k):
        return ref[:, pl.ds(pl.multiple_of((m ^ k) * rows, rows), rows)]

    own[...], next_to[...] = of(0), of(2)
    sent[0:width, :] = of(1).astype(BF16)
    sent[width:, :] = of(3).astype(BF16)


def halve_kernel(own, next_to, recv, own_o, sent):
    width = own.shape[0]
    own_o[...] = own[...] + recv[0:width, :].astype(F32)
    sent[...] = (next_to[...] + recv[width:, :].astype(F32)).astype(BF16)


def put_blocks(parts, here, grads):
    at = 0
    for p in parts:
        cols = slice(at, at + p.shape[1])
        at += p.shape[1]
        if len(grads) == 1:
            grads[0][:, cols] = p
            continue
        sent, kept = grads
        n = kept.shape[0] // 4
        for b in range(4):
            even, odd = p[2 * b * n : (2 * b + 1) * n], p[(2 * b + 1) * n : (2 * b + 2) * n]
            sent[b * n : (b + 1) * n, cols] = pick(here, odd, even)
            kept[b * n : (b + 1) * n, cols] = pick(here, even, odd)


def pick(bit, a, b):
    return jnp.where(bit == 0, a, b)


def back_kernel(
    place, lengths, d0, d1, d2, d3, qkv, pt, xt, h1, stat, nb, cols, wq_t, vec,
    p0, p2, p13, vec_o, *rest,
):
    grads, (dqkv_o, score, ds, acc, buckets_of, wide, sums) = rest[:-7], rest[-7:]
    m = place[0]
    channels, tokens = d0.shape
    heads = channels // HEAD_DIM
    width = xt.shape[0]
    rows = p0.shape[1]
    blk = 128
    n_blk = tokens // blk
    n_rows = buckets_of.shape[0]
    buckets = n_rows // heads
    half = buckets // 2
    live = (page_ids(lengths, (1, tokens), 1, -1) >= 0).astype(F32)
    off = lax.broadcasted_iota(jnp.int32, (blk, blk), 1) - lax.broadcasted_iota(
        jnp.int32, (blk, blk), 0
    )

    def one_head(h, carry):
        def rows_of(which):
            return pl.ds(pl.multiple_of(which * channels + h * HEAD_DIM, HEAD_DIM), HEAD_DIM)

        q, k, v = qkv[rows_of(0), :], qkv[rows_of(1), :], qkv[rows_of(2), :]
        mine = rows_of(0)
        d_att = (
            d0[mine, :].astype(F32) + d1[mine, :].astype(F32)
            + d2[mine, :].astype(F32) + d3[mine, :].astype(F32)
        )
        d_att = (d_att.astype(BF16).astype(F32) * live).astype(BF16)
        dqkv_o[rows_of(2), :] = nt(d_att, pt[h]).astype(BF16)
        score[...] = nn(v.T, d_att)
        acc[...] = jnp.zeros(acc.shape, F32)
        for i in range(n_blk):
            lanes = slice(i * blk, (i + 1) * blk)
            total = jnp.zeros((8, blk), F32)
            for j in range(n_blk):
                at = slice(j * blk, (j + 1) * blk)
                prod = score[at, lanes] * pt[h, at, lanes].astype(F32)
                score[at, lanes] = prod
                total = total + fold(prod)
            total = across(total)
            for j in range(n_blk):
                at = slice(j * blk, (j + 1) * blk)
                g = score[at, lanes] - pt[h, at, lanes].astype(F32) * total
                g = g.astype(BF16)
                ds[at, lanes] = g
                slot = max(min(i - j, 2), -2) + 2
                acc[slot] = acc[slot] + g.astype(F32)
        dqkv_o[rows_of(0), :] = (nn(k, ds[...]) * HEAD_DIM**-0.5).astype(BF16)
        dqkv_o[rows_of(1), :] = nt(q, ds[...]).astype(BF16)
        near, before, after = acc[2], acc[1], acc[3]
        corner_b, off_b = before[0:16, :], off[0:16, :] - blk
        corner_a, off_a = after[blk - 16 : blk, :], off[blk - 16 : blk, :] + blk
        first = h * buckets
        for b in range(buckets):
            if b == 0:
                v = fold(acc[0]) + fold(jnp.where(off - blk <= -half, before, 0.0))
                v = v + fold(jnp.where(off <= -half, near, 0.0))
            elif b == buckets - 1:
                v = fold(acc[4]) + fold(jnp.where(off + blk >= half - 1, after, 0.0))
                v = v + fold(jnp.where(off >= half - 1, near, 0.0))
            else:
                v = fold(jnp.where(off == b - half, near, 0.0))
                if b < half:
                    v = v + fold(jnp.where(off_b == b - half, corner_b, 0.0))
                elif b > half:
                    v = v + fold(jnp.where(off_a == b - half, corner_a, 0.0))
            buckets_of[pl.ds(first + b, 1), :] = across(v)
        return carry

    lax.fori_loop(0, heads, one_head, 0, unroll=True)
    wide[...] = nn(wq_t[...], dqkv_o[...])
    weight_grad = nt(h1[...], dqkv_o[...]).astype(BF16)
    mean, rstd = stat[0:1, :], stat[1:2, :]
    zero = jnp.zeros((8, tokens), F32)

    def gather(i, part):
        d = wide[chunk(i), :]
        hat = (xt[chunk(i), :].astype(F32) - mean) * rstd
        u = d * cols[chunk(i), :][:, GAIN0 : GAIN0 + 1]
        sums[chunk(i), 0:1] = jnp.sum(d * hat, axis=1, keepdims=True)
        sums[chunk(i), 1:2] = jnp.sum(d, axis=1, keepdims=True)
        return part[0] + fold(u), part[1] + fold(u * hat)

    first, second = passes(width, gather, (zero, zero))
    first, second = across(first) / width, across(second) / width

    def back(i, carry):
        hat = (xt[chunk(i), :].astype(F32) - mean) * rstd
        u = wide[chunk(i), :] * cols[chunk(i), :][:, GAIN0 : GAIN0 + 1]
        wide[chunk(i), :] = nb[chunk(i), :] + rstd * (u - first - hat * second)
        return carry

    passes(width, back, 0)
    put_halves(m, wide, p0, p2, p13)
    turned = sums[...].T
    vec_o[...] = vec[...]
    vec_o[0:1, :] = turned[0:1, :]
    vec_o[2:3, :] = turned[1:2, :]
    each = jnp.sum(buckets_of[...], axis=1, keepdims=True)
    shape = (n_rows, width)
    lane = lax.broadcasted_iota(jnp.int32, shape, 1)
    row = lax.broadcasted_iota(jnp.int32, shape, 0)
    vec_o[6:7, :] = across(jnp.where(lane == row + m * n_rows, each, 0.0))
    put_blocks([weight_grad], place[1] & 1, grads)
    if len(grads) > 1:
        put_vec(vec_o[...], grads[0])


def put_vec(vec, ref):
    half = vec.shape[1] // 2
    v = jnp.concatenate([vec[:, :half], vec[:, half:]])
    high = v.astype(BF16)
    n, rows = ref.shape[0], v.shape[0]
    ref[n - 2 * rows : n - rows, :half] = high
    ref[n - rows :, :half] = (v - high.astype(F32)).astype(BF16)


def get_vec(ref, width):
    n, rows, half = ref.shape[0], 16, width // 2
    v = ref[n - 2 * rows : n - rows, :half].astype(F32) + ref[n - rows :, :half].astype(F32)
    return jnp.concatenate([v[:8], v[8:]], axis=1)


def grads_second_kernel(place, a_keep, a_recv, b_keep, b_recv, s0, s1, s2, kept):
    core = place[1] & 1
    half, n, third = a_keep.shape[1], kept.shape[0] // 2, s0.shape[1]
    for j, sent in enumerate((s0, s1, s2)):
        for keep, recv, low, high in (
            (a_keep, a_recv, j * third, min((j + 1) * third, half)),
            (b_keep, b_recv, max(j * third, half) - half, (j + 1) * third - half),
        ):
            if low >= high:
                continue
            at = low + (half if keep is b_keep else 0)
            from_, to = slice(low, high), slice(at - j * third, at - j * third + high - low)
            for i in range(2):
                rows = pl.ds(pl.multiple_of(2 * i * n, 2 * n), 2 * n)
                out = slice(i * n, (i + 1) * n)
                halve_rows(
                    core, keep.at[rows, from_], recv.at[rows, from_],
                    sent.at[out, to], kept.at[out, at : at + high - low],
                )


def grads_third_kernel(place, keep, r0, r1, r2, a_sent, a_kept, b_sent, b_kept):
    x, y = (place[1] >> 1) & 1, (place[1] >> 2) & 1
    half, third = a_kept.shape[1], r0.shape[1]
    for j, recv in enumerate((r0, r1, r2)):
        low, high = j * third, (j + 1) * third
        for bit, sent, kept, first, start, stop in (
            (y, a_sent, a_kept, 0, low, min(high, half)),
            (x, b_sent, b_kept, half, max(low, half), high),
        ):
            if start >= stop:
                continue
            out = slice(start - first, stop - first)
            halve_rows(
                bit, keep.at[:, start:stop], recv.at[:, start - low : stop - low],
                sent.at[:, out], kept.at[:, out],
            )


def halve_rows(bit, keep, recv, sent, kept):
    n = kept.shape[0]
    for ref, b in ((sent, 1 - bit), (kept, bit)):
        rows = pl.ds(pl.multiple_of(b * n, n), n)
        total = keep[rows, :].astype(F32) + recv[rows, :].astype(F32)
        ref[0:n, :] = total.astype(ref.dtype)


def qkv_second_kernel(place, vec, keep, recv, sent, kept, vec_o):
    x = (place[1] >> 1) & 1
    n = kept.shape[0] // 2
    for i in range(2):
        for ref, b in ((sent, 1 - x), (kept, x)):
            rows = pl.ds(pl.multiple_of((2 * i + b) * n, n), n)
            total = keep[rows, :].astype(F32) + recv[rows, :].astype(F32)
            ref[i * n : (i + 1) * n, :] = total.astype(ref.dtype)
    vec_o[...] = vec[...] + get_vec(recv, vec.shape[1])
    put_vec(vec_o[...], sent)


def qkv_third_kernel(place, vec, keep, recv, sent, kept, vec_o):
    halve_rows((place[1] >> 2) & 1, keep, recv, sent, kept)
    vec_o[...] = vec[...] + get_vec(recv, vec.shape[1])
    put_vec(vec_o[...], sent)


def message_kernel(place, vec, b_keep, b_recv, q_recv, vec_o, o0, o1, o2, o3, turned):
    m = place[0]
    channels = o0.shape[0]
    width, share = turned.shape
    cols = slice(b_keep.shape[1] - width, b_keep.shape[1])
    turned[...] = (b_keep[:, cols] + b_recv[:, cols].astype(F32)).T
    v = vec[...] + get_vec(q_recv, vec.shape[1])
    vec_o[...] = v
    tiles = v.shape[1] // 128
    high = v.astype(BF16)
    low = (v - high.astype(F32)).astype(BF16)
    both = jnp.concatenate([high.astype(F32), low.astype(F32)]).astype(BF16)
    for k, ref in enumerate((o0, o1, o2, o3)):
        t = turned[pl.ds(pl.multiple_of((m ^ k) * channels, channels), channels), :]
        ref[0:channels, 0:share] = t.astype(ref.dtype)
        if k:
            for i in range(tiles):
                at = channels + 16 * i
                ref[at : at + 16, :] = both[:, 128 * i : 128 * (i + 1)]


def last_kernel(a_keep, a_recv, b_keep, b_recv, q_keep, q_recv, up_o, down_o, qkv_o):
    hidden = up_o.shape[1]
    channels = qkv_o.shape[2]
    a = a_keep[...] + a_recv[...].astype(F32)
    share, half = a.shape
    rest = slice(0, 2 * hidden - half)
    up_o[...] = a[:, :hidden]
    down_o[:, : half - hidden] = a[:, hidden:]
    down_o[:, half - hidden :] = b_keep[:, rest] + b_recv[:, rest].astype(F32)
    q = q_keep[...] + q_recv[0:share, :].astype(F32)
    for i in range(3):
        qkv_o[i] = q[:, i * channels : (i + 1) * channels]


def small_kernel(vec, o0, o1, o2, o3, out, gains, biases, scales, table):
    channels, share = out.shape
    others = (o1, o2, o3)
    total = o0[...]
    v = vec[...]
    for ref in others:
        total = total + ref[0:channels, 0:share].astype(F32)
        parts = []
        for i in range(v.shape[1] // 128):
            at = channels + 16 * i
            both = ref[at : at + 16, :].astype(F32)
            parts.append(both[:8] + both[8:])
        v = v + jnp.concatenate(parts, axis=1)
    out[...] = total
    gains[...] = v[0:2]
    biases[...] = v[2:4]
    scales[...] = v[4:6]
    n = table.shape[1]
    for h in range(table.shape[0]):
        table[h : h + 1, :] = v[6:7, h * n : (h + 1) * n]


def input_kernel(own, recv, dy, out):
    total = own[...] + recv[...].astype(F32)
    out[...] = (dy[...].astype(F32) + total.T).astype(BF16)


def output_kernel(own, recv, mid, cols, out):
    total = own[...] + recv[...].astype(F32)
    out[...] = (mid[...] + cols[:, SCALE1 : SCALE1 + 1] * total).T.astype(BF16)


def body(
    tokens,
    page_lengths,
    norm_gains,
    norm_biases,
    layer_scales,
    w_qkv,
    rel_table,
    w_out,
    w_up,
    w_down,
    cotangent,
):
    mp, dp = lax.axis_size("mp"), lax.axis_size("dp")
    rows, width = tokens.shape
    group = rows * mp
    channels = w_qkv.shape[2]
    hidden = w_up.shape[1]
    heads = channels // HEAD_DIM
    buckets = rel_table.shape[0]
    m, d = lax.axis_index("mp"), lax.axis_index("dp")
    place = jnp.stack([m, d]).astype(jnp.int32)

    def swap(v, k, axis="mp", name="rows"):
        n = mp if axis == "mp" else dp
        with jax.named_scope(name):
            return lax.ppermute(v, axis, [(i, i ^ k) for i in range(n)])

    def after(v, *seen):
        return lax.optimization_barrier((v,) + seen)[0]

    fast = dp == 8 and (width // dp) % 16 == 0 and hidden == width

    cols = jnp.concatenate(
        [norm_gains[0:1], norm_biases[0:1], norm_gains[1:2], norm_biases[1:2], layer_scales]
    ).T
    wq = jnp.transpose(w_qkv, (1, 2, 0)).reshape(3 * channels, width)

    piece = channels // 4
    sent = jnp.concatenate([tokens, lax.dynamic_slice_in_dim(w_out, (d & 3) * piece, piece, 0)])
    x1, x2 = swap(sent, 1, name="x"), swap(sent, 2, name="x")
    x = [sent, x1, x2, swap(after(x2, x1), 1, name="x")]
    dy2 = swap(after(cotangent, *x[1:]), 2, name="dy")
    wq_t, w_up_t, w_down_t = call(
        turn_kernel,
        [like((width, 3 * channels), BF16), like((hidden, width), BF16), like((width, hidden), BF16)],
        [wq, w_up, w_down],
    )
    x[1:] = lax.optimization_barrier((x[1:], wq_t))[0]
    (part,) = call(pieces_kernel, [like((4, piece, width), BF16)], x)
    part_x = swap(part, 2, "dp", name="w")
    wq_now = after(wq, wq_t, w_up_t, w_down_t)
    xt, h1, stat, qkv, pt, att = call(
        head_kernel,
        [
            like((width, group), BF16),
            like((width, group), BF16),
            like((8, group), F32),
            like((3 * channels, group), BF16),
            like((heads, group, group), BF16),
            like((channels, group), BF16),
        ],
        [place, page_lengths, rel_table] + x + [cols, wq_now],
        n_smem=3,
        scratch=[
            pltpu.VMEM((group, group), F32),
            pltpu.VMEM((group, 128), jnp.int32),
            pltpu.VMEM((3, 128, 128), F32),
        ],
        us=10,
    )
    (parts,) = call(pair_kernel, [like((8, piece, width), BF16)], [part, after(part_x, att, dy2)])
    att_sent = after(att, parts)
    dy1 = swap(after(cotangent, parts), 1, name="dy")
    atts = [att] + [swap(att_sent, k, name="att") for k in (1, 2, 3)]
    dy = [cotangent, dy1, dy2, swap(after(dy2, parts), 1, name="dy")]
    w_pieces = [parts, swap(parts, 1, "dp", name="w")]
    w_out_full, w_out_t = call(
        out_weight_kernel, [like((width, width), BF16)] * 2, [place] + w_pieces, n_smem=1
    )
    act_like = like((width, group), BF16)
    hid_like = like((hidden, group), BF16)
    wide_like = like((width, group), F32)
    block = like((width, rows), F32)
    blocks = [block, block, like((2 * width, rows), BF16)]
    att_all, attn, hat, rstd, h2, act, slope, mid, mlp_part, m0, m2, m13 = call(
        up_kernel,
        [act_like, wide_like, wide_like, like((8, group), F32), act_like, hid_like]
        + [like((hidden, group), F32), block, wide_like]
        + blocks,
        [place] + atts + [after(xt, dy1), cols, w_out_t, w_up_t, w_down_t],
        n_smem=1,
        scratch=[pltpu.VMEM((hidden, group), F32)],
        us=10,
    )
    m_recv = swap(m13, 1, name="mlp")
    d0, d1, d2, d3, nb, dup, gm, ga, dy_t, vec = call(
        down_kernel,
        [like((channels, group), BF16)] * 4
        + [wide_like, hid_like, act_like, act_like, act_like, like((8, width), F32)],
        [place] + dy + [cols, attn, hat, rstd, slope, w_out_full, w_up, w_down],
        n_smem=1,
        scratch=[pltpu.VMEM((max(width, hidden), group), F32), pltpu.VMEM((width, 128), F32)],
        us=10,
    )
    d_att = [d0] + [swap(v, k, name="d_att") for k, v in ((1, d1), (2, d2), (3, d3))]
    grad_cols = 2 * hidden + width
    share = width // dp
    half = grad_cols // 2
    if fast:
        grad_like = [like((width // 2, half), BF16)] * 4
    else:
        grad_like = [like((width, grad_cols), BF16)]
    vec, *grads = call(
        mlp_grad_kernel,
        [like((8, width), F32)] + grad_like,
        [place, vec, mlp_part, act, dup, gm, ga, att_all, h2, dy_t],
        n_smem=1,
        scratch=[pltpu.VMEM((width, 128), F32)],
    )
    if fast:
        a_sent, a_kept, b_sent, b_kept = grads
        a_recv = swap(a_sent, 2, "dp", name="grads_a")
        b_recv = swap(b_sent, 4, "dp", name="grads_b")

    def halved(own, next_to, recv, name, us=0.01, seen=()):
        half_like = [block, like((width, rows), BF16)]
        own, sent = call(halve_kernel, half_like, [own, next_to, recv], us=us)
        return [own, swap(after(sent, *seen), 2, name=name)]

    mlp = halved(m0, m2, m_recv, "mlp", seen=d_att[1:])

    n = 3 * channels
    extra = 4 * vec.shape[0]
    if fast:
        grad_like = [like((width // 2 + extra, n), BF16), like((width // 2, n), BF16)]
    else:
        grad_like = [like((width, n), BF16)]
    p0, p2, p13, vec, *qkv_grads = call(
        back_kernel,
        blocks + [like((8, width), F32)] + grad_like,
        [place, page_lengths] + d_att + [qkv, pt, xt, h1, stat, nb, cols, wq_t, vec],
        n_smem=2,
        scratch=[
            pltpu.VMEM((n, group), BF16),
            pltpu.VMEM((group, group), F32),
            pltpu.VMEM((group, group), BF16),
            pltpu.VMEM((5, 128, 128), F32),
            pltpu.VMEM((heads * buckets, 128), F32),
            pltpu.VMEM((width, group), F32),
            pltpu.VMEM((width, 128), F32),
        ],
        us=10,
    )
    p_recv = swap(after(p13, mlp[1]), 1, name="back")
    back = halved(p0, p2, p_recv, "back", us=10)

    def reduced(g):
        g = g.reshape(dp, width // dp, g.shape[1])
        bit = 1
        while bit < dp:
            g = g.reshape(g.shape[0] // 2, 2, width // dp, g.shape[-1])
            here = (d & bit) // bit
            sent = lax.dynamic_index_in_dim(g, 1 - here, 1, keepdims=False)
            kept = lax.dynamic_index_in_dim(g, here, 1, keepdims=False)
            g = kept.astype(F32) + swap(sent, bit, "dp").astype(F32)
            bit *= 2
            if bit < dp:
                g = g.astype(BF16)
        return g[0]

    if fast:
        q_recv = swap(after(qkv_grads[0], mlp[1]), 1, "dp", name="qkv_core")
        vec_like = [like(vec.shape, F32)]
        sent, kept, vec = call(
            qkv_second_kernel,
            [like((2 * share + extra, n), BF16), like((2 * share, n), F32)] + vec_like,
            [place, vec, qkv_grads[1], q_recv],
            n_smem=1,
        )
        recv = swap(sent, 2, "dp", name="qkv_x")
        g0, g1, g2, g_kept = call(
            grads_second_kernel,
            [like((2 * share, grad_cols // 3), BF16)] * 3 + [like((2 * share, grad_cols), BF16)],
            [place, after(a_kept, vec), a_recv, b_kept, b_recv],
            n_smem=1,
        )
        g_recv = [swap(g, 1, "dp", name="grads_core") for g in (g0, g1, g2)]
        a_sent, a_kept, b_sent, b_kept = call(
            grads_third_kernel,
            [like((share, half), BF16), like((share, half), F32)] * 2,
            [place, g_kept] + g_recv,
            n_smem=1,
        )
        a_recv = swap(a_sent, 4, "dp", name="grads_a")
        b_recv = swap(b_sent, 2, "dp", name="grads_b")
        sent, kept, vec = call(
            qkv_third_kernel,
            [like((share + extra, n), BF16), like((share, n), F32)] + vec_like,
            [place, after(vec, a_kept, back[0]), kept, recv],
            n_smem=1,
        )
        recv = swap(sent, 4, "dp", name="qkv_y")
        message = like((channels + 2 * vec.size // 128, 128), BF16)
        vec, o0, o1, o2, o3 = call(
            message_kernel,
            vec_like + [like((channels, share), F32)] + [message] * 3,
            [place, vec, b_kept, b_recv, recv],
            n_smem=1,
            scratch=[pltpu.VMEM((width, share), F32)],
        )
        grad_up, grad_down, grad_qkv = call(
            last_kernel,
            [like((share, hidden), F32)] * 2 + [like((3, share, channels), F32)],
            [a_kept, a_recv, b_kept, b_recv, after(kept, o1), recv],
        )
        o1, o2, o3 = (swap(v, k, name="out") for k, v in ((1, o1), (2, o2), (3, o3)))
        grad_out, gains, biases, scales, grad_table = call(
            small_kernel,
            [like((channels, share), F32)]
            + [like((2, width), F32)] * 3
            + [like((heads * mp, buckets), F32)],
            [vec, o0, o1, o2, o3],
        )
        grad_qkv = jnp.transpose(grad_qkv, (1, 0, 2))
    else:
        summed = reduced(grads[0])
        grad_qkv = reduced(qkv_grads[0]).reshape(share, 3, channels)
        grad_up, grad_down = summed[:, :hidden], summed[:, hidden : 2 * hidden]
        turned = summed[:, 2 * hidden :].T

        def out_part(k):
            return lax.dynamic_slice_in_dim(turned, (m ^ k) * channels, channels, 0)

        grad_out = out_part(0)
        for k in range(1, mp):
            grad_out = grad_out + swap(out_part(k).astype(BF16), k).astype(F32)
        bit = 1
        while bit < dp:
            vec = vec + swap(vec, bit, "dp", name="vec")
            bit *= 2
        for k in (1, 2):
            vec = vec + swap(vec, k, name="vec")
        gains, biases, scales = vec[0:2], vec[2:4], vec[4:6]
        grad_table = vec[6, : heads * mp * buckets].reshape(heads * mp, buckets)

    (output,) = call(output_kernel, [like((rows, width), BF16)], mlp + [mid, cols])
    (grad_input,) = call(input_kernel, [like((rows, width), BF16)], back + [cotangent], us=10)
    return (
        output,
        grad_input,
        gains,
        biases,
        scales,
        grad_qkv,
        grad_table.T,
        grad_out,
        grad_up,
        grad_down.T,
    )


def solution(mesh):
    placed = (
        P(("dp", "mp"), None),
        P("dp", None),
        P(),
        P(),
        P(),
        P(None, None, "mp"),
        P(),
        P("mp", None),
        P(None, "mp"),
        P("mp", None),
        P(("dp", "mp"), None),
    )
    return jax.shard_map(
        body,
        mesh=mesh,
        in_specs=placed,
        out_specs=(
            P(("dp", "mp"), None),
            P(("dp", "mp"), None),
            P(),
            P(),
            P(),
            P("dp", None, "mp"),
            P(),
            P("mp", "dp"),
            P("dp", "mp"),
            P("mp", "dp"),
        ),
        check_vma=False,
    )
```

```python
import jax
import jax.numpy as jnp
from jax import lax
from jax.experimental import pallas as pl
from jax.experimental.pallas import tpu as pltpu
from jax.sharding import PartitionSpec as P

HEAD_DIM = 64
SPEED = 1.15e9
norm_eps = 1e-06
masked_score = -1000000000.0
F32 = jnp.float32
BF16 = jnp.bfloat16
SMEM = pl.BlockSpec(memory_space=pltpu.SMEM)
VMEM = pl.BlockSpec(memory_space=pltpu.VMEM)
CHUNK = 64
GAIN0, BIAS0, GAIN1, BIAS1, SCALE0, SCALE1 = range(6)


def call(kernel, outs, args, n_smem=0, scratch=(), us=0.01, limit=8):
    return pl.pallas_call(
        kernel,
        out_shape=tuple(outs),
        in_specs=[SMEM] * n_smem + [VMEM] * (len(args) - n_smem),
        out_specs=tuple([VMEM] * len(outs)),
        scratch_shapes=list(scratch),
        compiler_params=pltpu.CompilerParams(vmem_limit_bytes=limit << 20),
        name=kernel.__name__,
        cost_estimate=pl.CostEstimate(flops=int(us * SPEED), bytes_accessed=8, transcendentals=0),
    )(*args)


def like(shape, dtype):
    return jax.ShapeDtypeStruct(shape, dtype)


def nn(a, b):
    return lax.dot_general(a, b, (((1,), (0,)), ((), ())), preferred_element_type=F32)


def nt(a, b):
    return lax.dot_general(a, b, (((1,), (1,)), ((), ())), preferred_element_type=F32)


def fold(v):
    return jnp.sum(v.reshape(v.shape[0] // 8, 8, v.shape[1]), axis=0)


def across(v):
    return jnp.sum(v, axis=0, keepdims=True)


def passes(rows, step, start):
    return lax.fori_loop(0, rows // CHUNK, step, start, unroll=True)


def chunk(i):
    return pl.ds(pl.multiple_of(i * CHUNK, CHUNK), CHUNK)


def page_ids(lengths, shape, axis, dead):
    at = lax.broadcasted_iota(jnp.int32, shape, axis)
    page = jnp.zeros(shape, jnp.int32)
    end = jnp.int32(0)
    pages = lengths.shape[1]
    for p in range(pages):
        end = end + lengths[0, p]
        page = page + (at >= end).astype(jnp.int32)
    return jnp.where(page < pages - 1, page, dead)


def turn_kernel(wq, wu, wd, wq_o, wu_o, wd_o):
    wq_o[...] = wq[...].T
    wu_o[...] = wu[...].T
    wd_o[...] = wd[...].T


def pieces_kernel(x0, x1, x2, x3, out):
    n = out.shape[1]
    for k, ref in enumerate((x0, x1, x2, x3)):
        out[k] = ref[ref.shape[0] - n :, :]


def pair_kernel(a, b, out):
    out[0:4] = a[...]
    out[4:8] = b[...]


def out_weight_kernel(place, here, there, w_o, wt_o):
    m, d = place[0], place[1]
    rows = here.shape[1]
    for c, ref in enumerate((here, there)):
        for b in range(2):
            part = (d & 3) ^ (c + 2 * b)
            for k in range(4):
                at = pl.multiple_of((m ^ k) * 4 * rows + part * rows, rows)
                w_o[pl.ds(at, rows), :] = ref[4 * b + k]
    wt_o[...] = w_o[...].T


def head_kernel(
    place, lengths, table, x0, x1, x2, x3, cols, wq,
    xt_o, h1_o, stat_o, qkv_o, pt_o, att_o, top_o, low_o,
    score, ids, pattern,
):
    m = place[0]
    width, tokens = xt_o.shape
    rows = tokens // 4
    channels = att_o.shape[0]
    heads = channels // HEAD_DIM
    buckets = table.shape[0]
    half = buckets // 2
    for k, ref in enumerate((x0, x1, x2, x3)):
        at = pl.multiple_of((m ^ k) * rows, rows)
        xt_o[:, pl.ds(at, rows)] = ref[0:rows, :].T

    def add(i, acc):
        return acc + fold(xt_o[chunk(i), :].astype(F32))

    zero = jnp.zeros((8, tokens), F32)
    mean = across(passes(width, add, zero)) / width

    def spread(i, acc):
        v = xt_o[chunk(i), :].astype(F32) - mean
        return acc + fold(v * v)

    rstd = lax.rsqrt(across(passes(width, spread, zero)) / width + norm_eps)
    stat_o[0:1, :] = mean
    stat_o[1:2, :] = rstd

    def norm(i, carry):
        v = (xt_o[chunk(i), :].astype(F32) - mean) * rstd
        w = cols[chunk(i), :]
        h1_o[chunk(i), :] = (v * w[:, GAIN0 : GAIN0 + 1] + w[:, BIAS0 : BIAS0 + 1]).astype(BF16)
        return carry

    passes(width, norm, 0)
    qkv_o[...] = nn(wq[...], h1_o[...]).astype(BF16)
    qkv_o[0:channels, :] = qkv_o[0:channels, :] * BF16(HEAD_DIM**-0.5)

    ids[...] = page_ids(lengths, ids.shape, 0, -2)
    own_ids = page_ids(lengths, (1, tokens), 1, -1)
    live = (own_ids >= 0).astype(F32)
    blk = 128
    n_blk = tokens // blk
    off = lax.broadcasted_iota(jnp.int32, (blk, blk), 1) - lax.broadcasted_iota(
        jnp.int32, (blk, blk), 0
    )

    def one_head(h, carry):
        col = m * heads + h
        low, high = table[0, col], table[buckets - 1, col]
        near = jnp.where(off >= half - 1, high, low)
        for b in range(1, buckets - 1):
            near = jnp.where(off == b - half, table[b, col], near)
        pattern[1] = near
        before = jnp.full((blk, blk), low, F32)
        for b in range(1, half):
            before = jnp.where(off - blk == b - half, table[b, col], before)
        pattern[0] = before
        after = jnp.full((blk, blk), high, F32)
        for b in range(half + 1, buckets - 1):
            after = jnp.where(off + blk == b - half, table[b, col], after)
        pattern[2] = after

        def rows_of(which):
            return pl.ds(pl.multiple_of(which * channels + h * HEAD_DIM, HEAD_DIM), HEAD_DIM)

        q, k, v = qkv_o[rows_of(0), :], qkv_o[rows_of(1), :], qkv_o[rows_of(2), :]
        score[...] = nn(k.T, q)
        for i in range(n_blk):
            lanes = slice(i * blk, (i + 1) * blk)
            query_id = own_ids[:, lanes]
            top = jnp.full((8, blk), -3e38, F32)
            for j in range(n_blk):
                at = slice(j * blk, (j + 1) * blk)
                if abs(i - j) <= 1:
                    bias = pattern[i - j + 1]
                else:
                    bias = low if i < j else high
                s = jnp.where(ids[at, :] == query_id, score[at, lanes] + bias, masked_score)
                score[at, lanes] = s
                top = jnp.maximum(top, jnp.max(s.reshape(blk // 8, 8, blk), axis=0))
            top = jnp.max(top, axis=0, keepdims=True)
            total = jnp.zeros((8, blk), F32)
            for j in range(n_blk):
                at = slice(j * blk, (j + 1) * blk)
                e = jnp.exp(score[at, lanes] - top)
                score[at, lanes] = e
                total = total + fold(e)
            scale = 1.0 / across(total)
            for j in range(n_blk):
                at = slice(j * blk, (j + 1) * blk)
                pt_o[h, at, lanes] = (score[at, lanes] * scale).astype(BF16)
        mixed = nn(v, pt_o[h]) * live
        att_o[pl.ds(pl.multiple_of(h * HEAD_DIM, HEAD_DIM), HEAD_DIM), :] = mixed.astype(BF16)
        return carry

    lax.fori_loop(0, heads, one_head, 0, unroll=True)
    half_rows = channels // 2
    top_o[...], low_o[...] = att_o[0:half_rows, :], att_o[half_rows:, :]


def up_kernel(
    place, a0, a1, a2t, a2b, a3t, a3b, xt, cols, w_out_t, w_up_t, w_down_t,
    at_o, attn_o, hat_o, rstd_o, h2_o, act_o, slope_o, mid_o, mlp_o, m0, m2, m13,
    wide,
):
    m = place[0]
    rows = mid_o.shape[1]
    channels = a0.shape[0]
    width, tokens = xt.shape
    hidden = act_o.shape[0]
    top = channels // 2
    for k, first, a in ((0, 0, a0), (1, 0, a1), (2, 0, a2t), (2, top, a2b), (3, 0, a3t), (3, top, a3b)):
        at = pl.multiple_of((m ^ k) * channels + first, top)
        at_o[pl.ds(at, a.shape[0]), :] = a[...]
    attn_o[...] = nn(w_out_t[...], at_o[...])
    zero = jnp.zeros((8, tokens), F32)

    def residual(i, acc):
        scale = cols[chunk(i), :][:, SCALE0 : SCALE0 + 1]
        v = xt[chunk(i), :].astype(F32) + scale * attn_o[chunk(i), :]
        hat_o[chunk(i), :] = v
        return acc + fold(v)

    mean = across(passes(width, residual, zero)) / width
    mid_o[...] = hat_o[:, pl.ds(pl.multiple_of(m * rows, rows), rows)]

    def spread(i, acc):
        v = hat_o[chunk(i), :] - mean
        return acc + fold(v * v)

    rstd = lax.rsqrt(across(passes(width, spread, zero)) / width + norm_eps)
    rstd_o[0:1, :] = rstd

    def norm(i, carry):
        w = cols[chunk(i), :]
        v = (hat_o[chunk(i), :] - mean) * rstd
        hat_o[chunk(i), :] = v
        h2_o[chunk(i), :] = (v * w[:, GAIN1 : GAIN1 + 1] + w[:, BIAS1 : BIAS1 + 1]).astype(BF16)
        return carry

    passes(width, norm, 0)
    wide[...] = nn(w_up_t[...], h2_o[...])

    def gelu(i, carry):
        u = wide[chunk(i), :]
        cdf = 0.5 + 0.5 * lax.erf(u * (0.5**0.5))
        act_o[chunk(i), :] = (u * cdf).astype(BF16)
        slope_o[chunk(i), :] = cdf + u * (jnp.exp(-0.5 * u * u) * 0.3989422804014327)
        return carry

    passes(hidden, gelu, 0)
    mlp_o[...] = nn(w_down_t[...], act_o[...])
    put_halves(m, mlp_o, m0, m2, m13)


def down_kernel(
    place, c0, c1, c2, c3, cols, attn, hat, rstd, slope, w_out, w_up, w_down,
    d0, d1, d2, d3, nb_o, dup_o, gm_o, ga_o, dy_o, vec_o,
    wide, sums,
):
    m = place[0]
    rows = c0.shape[0]
    channels = d0.shape[0]
    width, tokens = hat.shape
    hidden = slope.shape[0]
    for k, c in enumerate((c0, c1, c2, c3)):
        at = pl.ds(pl.multiple_of((m ^ k) * rows, rows), rows)
        turned = c[...].T
        dy_o[:, at] = turned
        scale = cols[:, SCALE1 : SCALE1 + 1]
        gm_o[:, at] = (turned.astype(F32) * scale).astype(BF16)
    wide[...] = nn(w_down[...], gm_o[...])

    def d_up(i, carry):
        dup_o[chunk(i), :] = (slope[chunk(i), :] * wide[chunk(i), :]).astype(BF16)
        return carry

    passes(hidden, d_up, 0)
    wide[...] = nn(w_up[...], dup_o[...])
    zero = jnp.zeros((8, tokens), F32)

    def gather(i, acc):
        d = wide[chunk(i), :]
        u = d * cols[chunk(i), :][:, GAIN1 : GAIN1 + 1]
        return acc[0] + fold(u), acc[1] + fold(u * hat[chunk(i), :])

    first, second = passes(width, gather, (zero, zero))
    first, second = across(first) / width, across(second) / width
    lane = lax.broadcasted_iota(jnp.int32, (1, tokens), 1)
    mine = ((lane >= m * rows) & (lane < (m + 1) * rows)).astype(F32)
    rstd = rstd[0:1, :]

    def back(i, carry):
        w = cols[chunk(i), :]
        d = wide[chunk(i), :]
        h = hat[chunk(i), :]
        v = rstd * (d * w[:, GAIN1 : GAIN1 + 1] - first - h * second)
        nb_o[chunk(i), :] = v
        v = v + mine * dy_o[chunk(i), :].astype(F32)
        ga_o[chunk(i), :] = (v * w[:, SCALE0 : SCALE0 + 1]).astype(BF16)
        sums[chunk(i), 0:1] = jnp.sum(d * h, axis=1, keepdims=True)
        sums[chunk(i), 1:2] = jnp.sum(d, axis=1, keepdims=True)
        sums[chunk(i), 2:3] = jnp.sum(v * attn[chunk(i), :], axis=1, keepdims=True)
        return carry

    passes(width, back, 0)
    wide[...] = nn(w_out[...], ga_o[...])
    for k, ref in enumerate((d0, d1, d2, d3)):
        at = pl.ds(pl.multiple_of((m ^ k) * channels, channels), channels)
        ref[...] = wide[at, :].astype(BF16)
    turned = sums[...].T
    vec_o[...] = jnp.zeros(vec_o.shape, F32)
    vec_o[1:2, :] = turned[0:1, :]
    vec_o[3:4, :] = turned[1:2, :]
    vec_o[4:5, :] = turned[2:3, :]


def mlp_grad_kernel(place, vec, mlp, act, dup, gm, ga, att, h2, dy, vec_o, *rest):
    grads, sums = rest[:-1], rest[-1]

    def scale(i, carry):
        v = dy[chunk(i), :].astype(F32) * mlp[chunk(i), :]
        sums[chunk(i), 0:1] = jnp.sum(v, axis=1, keepdims=True)
        return carry

    passes(dy.shape[0], scale, 0)
    vec_o[...] = vec[...]
    vec_o[5:6, :] = sums[...].T[0:1, :]
    if len(grads) == 1:
        at = 0
        for a, b in ((h2, dup), (gm, act), (ga, att)):
            grads[0][:, at : at + b.shape[0]] = nt(a[...], b[...]).astype(BF16)
            at += b.shape[0]
        return
    x, y = (place[1] >> 1) & 1, (place[1] >> 2) & 1
    a_sent, a_kept, b_sent, b_kept = grads
    n, half = a_sent.shape[0] // 4, a_sent.shape[1]

    def put(p, left, low, high):
        block = [p[i * n : (i + 1) * n, low:high] for i in range(8)]
        first = left + low < half
        at = left + low - (0 if first else half)
        cols = slice(at, at + high - low)
        for i in range(4):
            out = slice(i * n, (i + 1) * n)
            if first:
                zero, one = 4 * (i // 2) + i % 2, 4 * (i // 2) + 2 + i % 2
                a_sent[out, cols] = pick(x, block[one], block[zero])
                a_kept[out, cols] = pick(x, block[zero], block[one])
            else:
                b_sent[out, cols] = pick(y, block[4 + i], block[i])
                b_kept[out, cols] = pick(y, block[i], block[4 + i])

    left = 0
    for a, b in ((h2, dup), (gm, act), (ga, att)):
        p = nt(a[...], b[...]).astype(BF16)
        n_cols = p.shape[1]
        cut = min(max(half - left, 0), n_cols)
        if cut > 0:
            put(p, left, 0, cut)
        if cut < n_cols:
            put(p, left, cut, n_cols)
        left += n_cols


def put_halves(m, ref, own, next_to, sent):
    rows, width = own.shape[1], own.shape[0]

    def of(k):
        return ref[:, pl.ds(pl.multiple_of((m ^ k) * rows, rows), rows)]

    own[...], next_to[...] = of(0), of(2)
    sent[0:width, :] = of(1).astype(BF16)
    sent[width:, :] = of(3).astype(BF16)


def halve_kernel(own, next_to, recv, own_o, sent):
    width = own.shape[0]
    own_o[...] = own[...] + recv[0:width, :].astype(F32)
    sent[...] = (next_to[...] + recv[width:, :].astype(F32)).astype(BF16)


def put_blocks(parts, here, grads):
    at = 0
    for p in parts:
        cols = slice(at, at + p.shape[1])
        at += p.shape[1]
        if len(grads) == 1:
            grads[0][:, cols] = p
            continue
        sent, kept = grads
        n = kept.shape[0] // 4
        for b in range(4):
            even, odd = p[2 * b * n : (2 * b + 1) * n], p[(2 * b + 1) * n : (2 * b + 2) * n]
            sent[b * n : (b + 1) * n, cols] = pick(here, odd, even)
            kept[b * n : (b + 1) * n, cols] = pick(here, even, odd)


def pick(bit, a, b):
    return jnp.where(bit == 0, a, b)


def back_kernel(
    place, lengths, d0, d1, d2, d3, qkv, pt, xt, h1, stat, nb, cols, wq_t, vec,
    p0, p2, p13, vec_o, *rest,
):
    grads, (dqkv_o, score, ds, acc, buckets_of, wide, sums) = rest[:-7], rest[-7:]
    m = place[0]
    channels, tokens = d0.shape
    heads = channels // HEAD_DIM
    width = xt.shape[0]
    rows = p0.shape[1]
    blk = 128
    n_blk = tokens // blk
    n_rows = buckets_of.shape[0]
    buckets = n_rows // heads
    half = buckets // 2
    live = (page_ids(lengths, (1, tokens), 1, -1) >= 0).astype(F32)
    off = lax.broadcasted_iota(jnp.int32, (blk, blk), 1) - lax.broadcasted_iota(
        jnp.int32, (blk, blk), 0
    )

    def one_head(h, carry):
        def rows_of(which):
            return pl.ds(pl.multiple_of(which * channels + h * HEAD_DIM, HEAD_DIM), HEAD_DIM)

        q, k, v = qkv[rows_of(0), :], qkv[rows_of(1), :], qkv[rows_of(2), :]
        mine = rows_of(0)
        d_att = (
            d0[mine, :].astype(F32) + d1[mine, :].astype(F32)
            + d2[mine, :].astype(F32) + d3[mine, :].astype(F32)
        )
        d_att = (d_att.astype(BF16).astype(F32) * live).astype(BF16)
        dqkv_o[rows_of(2), :] = nt(d_att, pt[h]).astype(BF16)
        score[...] = nn(v.T, d_att)
        acc[...] = jnp.zeros(acc.shape, F32)
        for i in range(n_blk):
            lanes = slice(i * blk, (i + 1) * blk)
            total = jnp.zeros((8, blk), F32)
            for j in range(n_blk):
                at = slice(j * blk, (j + 1) * blk)
                prod = score[at, lanes] * pt[h, at, lanes].astype(F32)
                score[at, lanes] = prod
                total = total + fold(prod)
            total = across(total)
            for j in range(n_blk):
                at = slice(j * blk, (j + 1) * blk)
                g = score[at, lanes] - pt[h, at, lanes].astype(F32) * total
                g = g.astype(BF16)
                ds[at, lanes] = g
                slot = max(min(i - j, 2), -2) + 2
                acc[slot] = acc[slot] + g.astype(F32)
        dqkv_o[rows_of(0), :] = (nn(k, ds[...]) * HEAD_DIM**-0.5).astype(BF16)
        dqkv_o[rows_of(1), :] = nt(q, ds[...]).astype(BF16)
        near, before, after = acc[2], acc[1], acc[3]
        corner_b, off_b = before[0:16, :], off[0:16, :] - blk
        corner_a, off_a = after[blk - 16 : blk, :], off[blk - 16 : blk, :] + blk
        first = h * buckets
        for b in range(buckets):
            if b == 0:
                v = fold(acc[0]) + fold(jnp.where(off - blk <= -half, before, 0.0))
                v = v + fold(jnp.where(off <= -half, near, 0.0))
            elif b == buckets - 1:
                v = fold(acc[4]) + fold(jnp.where(off + blk >= half - 1, after, 0.0))
                v = v + fold(jnp.where(off >= half - 1, near, 0.0))
            else:
                v = fold(jnp.where(off == b - half, near, 0.0))
                if b < half:
                    v = v + fold(jnp.where(off_b == b - half, corner_b, 0.0))
                elif b > half:
                    v = v + fold(jnp.where(off_a == b - half, corner_a, 0.0))
            buckets_of[pl.ds(first + b, 1), :] = across(v)
        return carry

    lax.fori_loop(0, heads, one_head, 0, unroll=True)
    wide[...] = nn(wq_t[...], dqkv_o[...])
    weight_grad = nt(h1[...], dqkv_o[...]).astype(BF16)
    mean, rstd = stat[0:1, :], stat[1:2, :]
    zero = jnp.zeros((8, tokens), F32)

    def gather(i, part):
        d = wide[chunk(i), :]
        hat = (xt[chunk(i), :].astype(F32) - mean) * rstd
        u = d * cols[chunk(i), :][:, GAIN0 : GAIN0 + 1]
        sums[chunk(i), 0:1] = jnp.sum(d * hat, axis=1, keepdims=True)
        sums[chunk(i), 1:2] = jnp.sum(d, axis=1, keepdims=True)
        return part[0] + fold(u), part[1] + fold(u * hat)

    first, second = passes(width, gather, (zero, zero))
    first, second = across(first) / width, across(second) / width

    def back(i, carry):
        hat = (xt[chunk(i), :].astype(F32) - mean) * rstd
        u = wide[chunk(i), :] * cols[chunk(i), :][:, GAIN0 : GAIN0 + 1]
        wide[chunk(i), :] = nb[chunk(i), :] + rstd * (u - first - hat * second)
        return carry

    passes(width, back, 0)
    put_halves(m, wide, p0, p2, p13)
    turned = sums[...].T
    vec_o[...] = vec[...]
    vec_o[0:1, :] = turned[0:1, :]
    vec_o[2:3, :] = turned[1:2, :]
    each = jnp.sum(buckets_of[...], axis=1, keepdims=True)
    shape = (n_rows, width)
    lane = lax.broadcasted_iota(jnp.int32, shape, 1)
    row = lax.broadcasted_iota(jnp.int32, shape, 0)
    vec_o[6:7, :] = across(jnp.where(lane == row + m * n_rows, each, 0.0))
    put_blocks([weight_grad], place[1] & 1, grads)
    if len(grads) > 1:
        put_vec(vec_o[...], grads[0])


def put_vec(vec, ref):
    half = vec.shape[1] // 2
    v = jnp.concatenate([vec[:, :half], vec[:, half:]])
    high = v.astype(BF16)
    n, rows = ref.shape[0], v.shape[0]
    ref[n - 2 * rows : n - rows, :half] = high
    ref[n - rows :, :half] = (v - high.astype(F32)).astype(BF16)


def get_vec(ref, width):
    n, rows, half = ref.shape[0], 16, width // 2
    v = ref[n - 2 * rows : n - rows, :half].astype(F32) + ref[n - rows :, :half].astype(F32)
    return jnp.concatenate([v[:8], v[8:]], axis=1)


def grads_second_kernel(place, a_keep, a_recv, b_keep, b_recv, s0, s1, s2, kept):
    core = place[1] & 1
    half, n, third = a_keep.shape[1], kept.shape[0] // 2, s0.shape[1]
    for j, sent in enumerate((s0, s1, s2)):
        for keep, recv, low, high in (
            (a_keep, a_recv, j * third, min((j + 1) * third, half)),
            (b_keep, b_recv, max(j * third, half) - half, (j + 1) * third - half),
        ):
            if low >= high:
                continue
            at = low + (half if keep is b_keep else 0)
            from_, to = slice(low, high), slice(at - j * third, at - j * third + high - low)
            for i in range(2):
                rows = pl.ds(pl.multiple_of(2 * i * n, 2 * n), 2 * n)
                out = slice(i * n, (i + 1) * n)
                halve_rows(
                    core, keep.at[rows, from_], recv.at[rows, from_],
                    sent.at[out, to], kept.at[out, at : at + high - low],
                )


def grads_third_kernel(place, keep, r0, r1, r2, a_sent, a_kept, b_sent, b_kept):
    x, y = (place[1] >> 1) & 1, (place[1] >> 2) & 1
    half, third = a_kept.shape[1], r0.shape[1]
    for j, recv in enumerate((r0, r1, r2)):
        low, high = j * third, (j + 1) * third
        for bit, sent, kept, first, start, stop in (
            (y, a_sent, a_kept, 0, low, min(high, half)),
            (x, b_sent, b_kept, half, max(low, half), high),
        ):
            if start >= stop:
                continue
            out = slice(start - first, stop - first)
            halve_rows(
                bit, keep.at[:, start:stop], recv.at[:, start - low : stop - low],
                sent.at[:, out], kept.at[:, out],
            )


def halve_rows(bit, keep, recv, sent, kept):
    n = kept.shape[0]
    for ref, b in ((sent, 1 - bit), (kept, bit)):
        rows = pl.ds(pl.multiple_of(b * n, n), n)
        total = keep[rows, :].astype(F32) + recv[rows, :].astype(F32)
        ref[0:n, :] = total.astype(ref.dtype)


def qkv_second_kernel(place, vec, keep, recv, sent, kept, vec_o):
    x = (place[1] >> 1) & 1
    n = kept.shape[0] // 2
    for i in range(2):
        for ref, b in ((sent, 1 - x), (kept, x)):
            rows = pl.ds(pl.multiple_of((2 * i + b) * n, n), n)
            total = keep[rows, :].astype(F32) + recv[rows, :].astype(F32)
            ref[i * n : (i + 1) * n, :] = total.astype(ref.dtype)
    vec_o[...] = vec[...] + get_vec(recv, vec.shape[1])
    put_vec(vec_o[...], sent)


def qkv_third_kernel(place, vec, keep, recv, sent, kept, vec_o):
    halve_rows((place[1] >> 2) & 1, keep, recv, sent, kept)
    vec_o[...] = vec[...] + get_vec(recv, vec.shape[1])
    put_vec(vec_o[...], sent)


def message_kernel(place, vec, b_keep, b_recv, q_recv, vec_o, o0, o1, o2, o3, turned):
    m = place[0]
    channels = o0.shape[0]
    width, share = turned.shape
    cols = slice(b_keep.shape[1] - width, b_keep.shape[1])
    turned[...] = (b_keep[:, cols] + b_recv[:, cols].astype(F32)).T
    v = vec[...] + get_vec(q_recv, vec.shape[1])
    vec_o[...] = v
    tiles = v.shape[1] // 128
    high = v.astype(BF16)
    low = (v - high.astype(F32)).astype(BF16)
    both = jnp.concatenate([high.astype(F32), low.astype(F32)]).astype(BF16)
    for k, ref in enumerate((o0, o1, o2, o3)):
        t = turned[pl.ds(pl.multiple_of((m ^ k) * channels, channels), channels), :]
        ref[0:channels, 0:share] = t.astype(ref.dtype)
        if k:
            for i in range(tiles):
                at = channels + 16 * i
                ref[at : at + 16, :] = both[:, 128 * i : 128 * (i + 1)]


def last_kernel(a_keep, a_recv, b_keep, b_recv, q_keep, q_recv, up_o, down_o, qkv_o):
    hidden = up_o.shape[1]
    channels = qkv_o.shape[2]
    a = a_keep[...] + a_recv[...].astype(F32)
    share, half = a.shape
    rest = slice(0, 2 * hidden - half)
    up_o[...] = a[:, :hidden]
    down_o[:, : half - hidden] = a[:, hidden:]
    down_o[:, half - hidden :] = b_keep[:, rest] + b_recv[:, rest].astype(F32)
    q = q_keep[...] + q_recv[0:share, :].astype(F32)
    for i in range(3):
        qkv_o[i] = q[:, i * channels : (i + 1) * channels]


def small_kernel(vec, o0, o1, o2, o3, out, gains, biases, scales, table):
    channels, share = out.shape
    others = (o1, o2, o3)
    total = o0[...]
    v = vec[...]
    for ref in others:
        total = total + ref[0:channels, 0:share].astype(F32)
        parts = []
        for i in range(v.shape[1] // 128):
            at = channels + 16 * i
            both = ref[at : at + 16, :].astype(F32)
            parts.append(both[:8] + both[8:])
        v = v + jnp.concatenate(parts, axis=1)
    out[...] = total
    gains[...] = v[0:2]
    biases[...] = v[2:4]
    scales[...] = v[4:6]
    n = table.shape[1]
    for h in range(table.shape[0]):
        table[h : h + 1, :] = v[6:7, h * n : (h + 1) * n]


def input_kernel(own, recv, dy, out):
    total = own[...] + recv[...].astype(F32)
    out[...] = (dy[...].astype(F32) + total.T).astype(BF16)


def output_kernel(own, recv, mid, cols, out):
    total = own[...] + recv[...].astype(F32)
    out[...] = (mid[...] + cols[:, SCALE1 : SCALE1 + 1] * total).T.astype(BF16)


def body(
    tokens,
    page_lengths,
    norm_gains,
    norm_biases,
    layer_scales,
    w_qkv,
    rel_table,
    w_out,
    w_up,
    w_down,
    cotangent,
):
    mp, dp = lax.axis_size("mp"), lax.axis_size("dp")
    rows, width = tokens.shape
    group = rows * mp
    channels = w_qkv.shape[2]
    hidden = w_up.shape[1]
    heads = channels // HEAD_DIM
    buckets = rel_table.shape[0]
    m, d = lax.axis_index("mp"), lax.axis_index("dp")
    place = jnp.stack([m, d]).astype(jnp.int32)

    def swap(v, k, axis="mp", name="rows"):
        n = mp if axis == "mp" else dp
        with jax.named_scope(name):
            return lax.ppermute(v, axis, [(i, i ^ k) for i in range(n)])

    def after(v, *seen):
        return lax.optimization_barrier((v,) + seen)[0]

    fast = dp == 8 and (width // dp) % 16 == 0 and hidden == width

    cols = jnp.concatenate(
        [norm_gains[0:1], norm_biases[0:1], norm_gains[1:2], norm_biases[1:2], layer_scales]
    ).T
    wq = jnp.transpose(w_qkv, (1, 2, 0)).reshape(3 * channels, width)

    piece = channels // 4
    sent = jnp.concatenate([tokens, lax.dynamic_slice_in_dim(w_out, (d & 3) * piece, piece, 0)])
    x1, x2 = swap(sent, 1, name="x"), swap(sent, 2, name="x")
    x = [sent, x1, x2, swap(after(x2, x1), 1, name="x")]
    dy2 = swap(after(cotangent, *x[1:]), 2, name="dy")
    dy1 = swap(after(cotangent, *x[1:]), 1, name="dy")
    wq_t, w_up_t, w_down_t = call(
        turn_kernel,
        [like((width, 3 * channels), BF16), like((hidden, width), BF16), like((width, hidden), BF16)],
        [wq, w_up, w_down],
    )
    x[1:] = lax.optimization_barrier((x[1:], wq_t))[0]
    (part,) = call(pieces_kernel, [like((4, piece, width), BF16)], x)
    part_x = swap(part, 2, "dp", name="w")
    wq_now = after(wq, wq_t, w_up_t, w_down_t)
    xt, h1, stat, qkv, pt, att, att_top, att_low = call(
        head_kernel,
        [
            like((width, group), BF16),
            like((width, group), BF16),
            like((8, group), F32),
            like((3 * channels, group), BF16),
            like((heads, group, group), BF16),
            like((channels, group), BF16),
            like((channels // 2, group), BF16),
            like((channels // 2, group), BF16),
        ],
        [place, page_lengths, rel_table] + x + [cols, wq_now],
        n_smem=3,
        scratch=[
            pltpu.VMEM((group, group), F32),
            pltpu.VMEM((group, 128), jnp.int32),
            pltpu.VMEM((3, 128, 128), F32),
        ],
        us=10,
    )
    (parts,) = call(
        pair_kernel, [like((8, piece, width), BF16)], [part, after(part_x, att, dy1, dy2)]
    )
    att_top, att_low, att_sent = after(att_top, parts), after(att_low, parts), after(att, parts)
    a2t, a2b = swap(att_top, 2, name="att"), swap(att_low, 2, name="att")
    a3b, a1 = swap(att_low, 3, name="att"), swap(att_sent, 1, name="att")
    atts = [att, a1, a2t, a2b, swap(a2t, 1, name="att"), a3b]
    dy = [cotangent, dy1, dy2, swap(after(dy2, parts), 1, name="dy")]
    w_pieces = [parts, swap(parts, 1, "dp", name="w")]
    w_out_full, w_out_t = call(
        out_weight_kernel, [like((width, width), BF16)] * 2, [place] + w_pieces, n_smem=1
    )
    act_like = like((width, group), BF16)
    hid_like = like((hidden, group), BF16)
    wide_like = like((width, group), F32)
    block = like((width, rows), F32)
    blocks = [block, block, like((2 * width, rows), BF16)]
    att_all, attn, hat, rstd, h2, act, slope, mid, mlp_part, m0, m2, m13 = call(
        up_kernel,
        [act_like, wide_like, wide_like, like((8, group), F32), act_like, hid_like]
        + [like((hidden, group), F32), block, wide_like]
        + blocks,
        [place] + atts + [after(xt, dy1), cols, w_out_t, w_up_t, w_down_t],
        n_smem=1,
        scratch=[pltpu.VMEM((hidden, group), F32)],
        us=10,
    )
    m_recv = swap(m13, 1, name="mlp")
    d0, d1, d2, d3, nb, dup, gm, ga, dy_t, vec = call(
        down_kernel,
        [like((channels, group), BF16)] * 4
        + [wide_like, hid_like, act_like, act_like, act_like, like((8, width), F32)],
        [place] + dy + [cols, attn, hat, rstd, slope, w_out_full, w_up, w_down],
        n_smem=1,
        scratch=[pltpu.VMEM((max(width, hidden), group), F32), pltpu.VMEM((width, 128), F32)],
        us=10,
    )
    d_att = [d0] + [swap(v, k, name="d_att") for k, v in ((1, d1), (2, d2), (3, d3))]
    grad_cols = 2 * hidden + width
    share = width // dp
    half = grad_cols // 2
    if fast:
        grad_like = [like((width // 2, half), BF16)] * 4
    else:
        grad_like = [like((width, grad_cols), BF16)]
    vec, *grads = call(
        mlp_grad_kernel,
        [like((8, width), F32)] + grad_like,
        [place, vec, mlp_part, act, dup, gm, ga, att_all, h2, dy_t],
        n_smem=1,
        scratch=[pltpu.VMEM((width, 128), F32)],
    )
    if fast:
        a_sent, a_kept, b_sent, b_kept = grads
        a_recv = swap(a_sent, 2, "dp", name="grads_a")
        b_recv = swap(b_sent, 4, "dp", name="grads_b")

    def halved(own, next_to, recv, name, us=0.01, seen=()):
        half_like = [block, like((width, rows), BF16)]
        own, sent = call(halve_kernel, half_like, [own, next_to, recv], us=us)
        return [own, swap(after(sent, *seen), 2, name=name)]

    mlp = halved(m0, m2, m_recv, "mlp", seen=d_att[1:])

    n = 3 * channels
    extra = 4 * vec.shape[0]
    if fast:
        grad_like = [like((width // 2 + extra, n), BF16), like((width // 2, n), BF16)]
    else:
        grad_like = [like((width, n), BF16)]
    p0, p2, p13, vec, *qkv_grads = call(
        back_kernel,
        blocks + [like((8, width), F32)] + grad_like,
        [place, page_lengths] + d_att + [qkv, pt, xt, h1, stat, nb, cols, wq_t, vec],
        n_smem=2,
        scratch=[
            pltpu.VMEM((n, group), BF16),
            pltpu.VMEM((group, group), F32),
            pltpu.VMEM((group, group), BF16),
            pltpu.VMEM((5, 128, 128), F32),
            pltpu.VMEM((heads * buckets, 128), F32),
            pltpu.VMEM((width, group), F32),
            pltpu.VMEM((width, 128), F32),
        ],
        us=10,
    )
    p_recv = swap(after(p13, mlp[1]), 1, name="back")
    back = halved(p0, p2, p_recv, "back", us=10)

    def reduced(g):
        g = g.reshape(dp, width // dp, g.shape[1])
        bit = 1
        while bit < dp:
            g = g.reshape(g.shape[0] // 2, 2, width // dp, g.shape[-1])
            here = (d & bit) // bit
            sent = lax.dynamic_index_in_dim(g, 1 - here, 1, keepdims=False)
            kept = lax.dynamic_index_in_dim(g, here, 1, keepdims=False)
            g = kept.astype(F32) + swap(sent, bit, "dp").astype(F32)
            bit *= 2
            if bit < dp:
                g = g.astype(BF16)
        return g[0]

    if fast:
        q_recv = swap(after(qkv_grads[0], mlp[1]), 1, "dp", name="qkv_core")
        vec_like = [like(vec.shape, F32)]
        sent, kept, vec = call(
            qkv_second_kernel,
            [like((2 * share + extra, n), BF16), like((2 * share, n), F32)] + vec_like,
            [place, vec, qkv_grads[1], q_recv],
            n_smem=1,
        )
        recv = swap(sent, 2, "dp", name="qkv_x")
        g0, g1, g2, g_kept = call(
            grads_second_kernel,
            [like((2 * share, grad_cols // 3), BF16)] * 3 + [like((2 * share, grad_cols), BF16)],
            [place, after(a_kept, vec), a_recv, b_kept, b_recv],
            n_smem=1,
        )
        g_recv = [swap(g, 1, "dp", name="grads_core") for g in (g0, g1, g2)]
        a_sent, a_kept, b_sent, b_kept = call(
            grads_third_kernel,
            [like((share, half), BF16), like((share, half), F32)] * 2,
            [place, g_kept] + g_recv,
            n_smem=1,
        )
        a_recv = swap(a_sent, 4, "dp", name="grads_a")
        b_recv = swap(b_sent, 2, "dp", name="grads_b")
        sent, kept, vec = call(
            qkv_third_kernel,
            [like((share + extra, n), BF16), like((share, n), F32)] + vec_like,
            [place, after(vec, a_kept, back[0]), kept, recv],
            n_smem=1,
        )
        recv = swap(sent, 4, "dp", name="qkv_y")
        message = like((channels + 2 * vec.size // 128, 128), BF16)
        vec, o0, o1, o2, o3 = call(
            message_kernel,
            vec_like + [like((channels, share), F32)] + [message] * 3,
            [place, vec, b_kept, b_recv, recv],
            n_smem=1,
            scratch=[pltpu.VMEM((width, share), F32)],
        )
        grad_up, grad_down, grad_qkv = call(
            last_kernel,
            [like((share, hidden), F32)] * 2 + [like((3, share, channels), F32)],
            [a_kept, a_recv, b_kept, b_recv, after(kept, o1), recv],
        )
        o1, o2, o3 = (swap(v, k, name="out") for k, v in ((1, o1), (2, o2), (3, o3)))
        grad_out, gains, biases, scales, grad_table = call(
            small_kernel,
            [like((channels, share), F32)]
            + [like((2, width), F32)] * 3
            + [like((heads * mp, buckets), F32)],
            [vec, o0, o1, o2, o3],
        )
        grad_qkv = jnp.transpose(grad_qkv, (1, 0, 2))
    else:
        summed = reduced(grads[0])
        grad_qkv = reduced(qkv_grads[0]).reshape(share, 3, channels)
        grad_up, grad_down = summed[:, :hidden], summed[:, hidden : 2 * hidden]
        turned = summed[:, 2 * hidden :].T

        def out_part(k):
            return lax.dynamic_slice_in_dim(turned, (m ^ k) * channels, channels, 0)

        grad_out = out_part(0)
        for k in range(1, mp):
            grad_out = grad_out + swap(out_part(k).astype(BF16), k).astype(F32)
        bit = 1
        while bit < dp:
            vec = vec + swap(vec, bit, "dp", name="vec")
            bit *= 2
        for k in (1, 2):
            vec = vec + swap(vec, k, name="vec")
        gains, biases, scales = vec[0:2], vec[2:4], vec[4:6]
        grad_table = vec[6, : heads * mp * buckets].reshape(heads * mp, buckets)

    (output,) = call(output_kernel, [like((rows, width), BF16)], mlp + [mid, cols])
    (grad_input,) = call(input_kernel, [like((rows, width), BF16)], back + [cotangent], us=10)
    return (
        output,
        grad_input,
        gains,
        biases,
        scales,
        grad_qkv,
        grad_table.T,
        grad_out,
        grad_up,
        grad_down.T,
    )


def solution(mesh):
    placed = (
        P(("dp", "mp"), None),
        P("dp", None),
        P(),
        P(),
        P(),
        P(None, None, "mp"),
        P(),
        P("mp", None),
        P(None, "mp"),
        P("mp", None),
        P(("dp", "mp"), None),
    )
    return jax.shard_map(
        body,
        mesh=mesh,
        in_specs=placed,
        out_specs=(
            P(("dp", "mp"), None),
            P(("dp", "mp"), None),
            P(),
            P(),
            P(),
            P("dp", None, "mp"),
            P(),
            P("mp", "dp"),
            P("dp", "mp"),
            P("mp", "dp"),
        ),
        check_vma=False,
    )
```

```python
import jax
import jax.numpy as jnp
from jax import lax
from jax.experimental import pallas as pl
from jax.experimental.pallas import tpu as pltpu
from jax.sharding import PartitionSpec as P

HEAD_DIM = 64
SPEED = 1.15e9
norm_eps = 1e-06
masked_score = -1000000000.0
F32 = jnp.float32
BF16 = jnp.bfloat16
SMEM = pl.BlockSpec(memory_space=pltpu.SMEM)
VMEM = pl.BlockSpec(memory_space=pltpu.VMEM)
CHUNK = 64
GAIN0, BIAS0, GAIN1, BIAS1, SCALE0, SCALE1 = range(6)


def call(kernel, outs, args, n_smem=0, scratch=(), us=0.01, limit=8):
    return pl.pallas_call(
        kernel,
        out_shape=tuple(outs),
        in_specs=[SMEM] * n_smem + [VMEM] * (len(args) - n_smem),
        out_specs=tuple([VMEM] * len(outs)),
        scratch_shapes=list(scratch),
        compiler_params=pltpu.CompilerParams(vmem_limit_bytes=limit << 20),
        name=kernel.__name__,
        cost_estimate=pl.CostEstimate(flops=int(us * SPEED), bytes_accessed=8, transcendentals=0),
    )(*args)


def like(shape, dtype):
    return jax.ShapeDtypeStruct(shape, dtype)


def nn(a, b):
    return lax.dot_general(a, b, (((1,), (0,)), ((), ())), preferred_element_type=F32)


def nt(a, b):
    return lax.dot_general(a, b, (((1,), (1,)), ((), ())), preferred_element_type=F32)


def fold(v):
    return jnp.sum(v.reshape(v.shape[0] // 8, 8, v.shape[1]), axis=0)


def across(v):
    return jnp.sum(v, axis=0, keepdims=True)


def passes(rows, step, start):
    return lax.fori_loop(0, rows // CHUNK, step, start, unroll=True)


def chunk(i):
    return pl.ds(pl.multiple_of(i * CHUNK, CHUNK), CHUNK)


def page_ids(lengths, shape, axis, dead):
    at = lax.broadcasted_iota(jnp.int32, shape, axis)
    page = jnp.zeros(shape, jnp.int32)
    end = jnp.int32(0)
    pages = lengths.shape[1]
    for p in range(pages):
        end = end + lengths[0, p]
        page = page + (at >= end).astype(jnp.int32)
    return jnp.where(page < pages - 1, page, dead)


def turn_kernel(wq, wu, wd, wq_o, wu_o, wd_o):
    wq_o[...] = wq[...].T
    wu_o[...] = wu[...].T
    wd_o[...] = wd[...].T


def pieces_kernel(x0, x1, x2, x3, out):
    n = out.shape[1]
    for k, ref in enumerate((x0, x1, x2, x3)):
        out[k] = ref[ref.shape[0] - n :, :]


def pair_kernel(a, b, out):
    out[0:4] = a[...]
    out[4:8] = b[...]


def out_weight_kernel(place, here, there, w_o, wt_o):
    m, d = place[0], place[1]
    rows = here.shape[1]
    for c, ref in enumerate((here, there)):
        for b in range(2):
            part = (d & 3) ^ (c + 2 * b)
            for k in range(4):
                at = pl.multiple_of((m ^ k) * 4 * rows + part * rows, rows)
                w_o[pl.ds(at, rows), :] = ref[4 * b + k]
    wt_o[...] = w_o[...].T


def bias_kernel(place, lengths, table, pattern, ids):
    buckets = table.shape[0]
    half = buckets // 2
    heads, _, blk, _ = pattern.shape
    ids[...] = page_ids(lengths, ids.shape, 0, -2)
    off = lax.broadcasted_iota(jnp.int32, (blk, blk), 1) - lax.broadcasted_iota(
        jnp.int32, (blk, blk), 0
    )
    for h in range(heads):
        col = place[0] * heads + h
        low, high = table[0, col], table[buckets - 1, col]
        near = jnp.where(off >= half - 1, high, low)
        for b in range(1, buckets - 1):
            near = jnp.where(off == b - half, table[b, col], near)
        before = jnp.full((blk, blk), low, F32)
        for b in range(1, half):
            before = jnp.where(off - blk == b - half, table[b, col], before)
        after = jnp.full((blk, blk), high, F32)
        for b in range(half + 1, buckets - 1):
            after = jnp.where(off + blk == b - half, table[b, col], after)
        pattern[h, 0], pattern[h, 1], pattern[h, 2] = before, near, after


def head_kernel(
    place, lengths, table, x0, x1, x2, x3, pattern, ids, cols, wq,
    xt_o, h1_o, stat_o, qkv_o, pt_o, att_o, top_o, low_o,
    score,
):
    m = place[0]
    width, tokens = xt_o.shape
    rows = tokens // 4
    channels = att_o.shape[0]
    heads = channels // HEAD_DIM
    buckets = table.shape[0]
    for k, ref in enumerate((x0, x1, x2, x3)):
        at = pl.multiple_of((m ^ k) * rows, rows)
        xt_o[:, pl.ds(at, rows)] = ref[0:rows, :].T

    def add(i, acc):
        return acc + fold(xt_o[chunk(i), :].astype(F32))

    zero = jnp.zeros((8, tokens), F32)
    mean = across(passes(width, add, zero)) / width

    def spread(i, acc):
        v = xt_o[chunk(i), :].astype(F32) - mean
        return acc + fold(v * v)

    rstd = lax.rsqrt(across(passes(width, spread, zero)) / width + norm_eps)
    stat_o[0:1, :] = mean
    stat_o[1:2, :] = rstd

    def norm(i, carry):
        v = (xt_o[chunk(i), :].astype(F32) - mean) * rstd
        w = cols[chunk(i), :]
        h1_o[chunk(i), :] = (v * w[:, GAIN0 : GAIN0 + 1] + w[:, BIAS0 : BIAS0 + 1]).astype(BF16)
        return carry

    passes(width, norm, 0)
    qkv_o[...] = nn(wq[...], h1_o[...]).astype(BF16)
    qkv_o[0:channels, :] = qkv_o[0:channels, :] * BF16(HEAD_DIM**-0.5)

    own_ids = page_ids(lengths, (1, tokens), 1, -1)
    live = (own_ids >= 0).astype(F32)
    blk = 128
    n_blk = tokens // blk

    def one_head(h):
        col = m * heads + h
        low, high = table[0, col], table[buckets - 1, col]

        def rows_of(which):
            return pl.ds(which * channels + h * HEAD_DIM, HEAD_DIM)

        q, k, v = qkv_o[rows_of(0), :], qkv_o[rows_of(1), :], qkv_o[rows_of(2), :]
        score[h] = nn(k.T, q)
        for i in range(n_blk):
            lanes = slice(i * blk, (i + 1) * blk)
            query_id = own_ids[:, lanes]
            top = jnp.full((8, blk), -3e38, F32)
            for j in range(n_blk):
                at = slice(j * blk, (j + 1) * blk)
                if abs(i - j) <= 1:
                    bias = pattern[h, i - j + 1]
                else:
                    bias = low if i < j else high
                s = jnp.where(ids[at, :] == query_id, score[h, at, lanes] + bias, masked_score)
                score[h, at, lanes] = s
                top = jnp.maximum(top, jnp.max(s.reshape(blk // 8, 8, blk), axis=0))
            top = jnp.max(top, axis=0, keepdims=True)
            total = jnp.zeros((8, blk), F32)
            for j in range(n_blk):
                at = slice(j * blk, (j + 1) * blk)
                e = jnp.exp(score[h, at, lanes] - top)
                score[h, at, lanes] = e
                total = total + fold(e)
            scale = 1.0 / across(total)
            for j in range(n_blk):
                at = slice(j * blk, (j + 1) * blk)
                pt_o[h, at, lanes] = (score[h, at, lanes] * scale).astype(BF16)
        mixed = nn(v, pt_o[h]) * live
        att_o[h * HEAD_DIM : (h + 1) * HEAD_DIM, :] = mixed.astype(BF16)

    for h in range(heads):
        one_head(h)
    half_rows = channels // 2
    top_o[...], low_o[...] = att_o[0:half_rows, :], att_o[half_rows:, :]


def up_kernel(
    place, a0, a1, a2t, a2b, a3t, a3b, xt, cols, w_out_t, w_up_t, w_down_t,
    at_o, attn_o, hat_o, rstd_o, h2_o, act_o, slope_o, mid_o, mlp_o, m0, m2, m13,
    wide,
):
    m = place[0]
    rows = mid_o.shape[1]
    channels = a0.shape[0]
    width, tokens = xt.shape
    hidden = act_o.shape[0]
    top = channels // 2
    for k, first, a in ((0, 0, a0), (1, 0, a1), (2, 0, a2t), (2, top, a2b), (3, 0, a3t), (3, top, a3b)):
        at = pl.multiple_of((m ^ k) * channels + first, top)
        at_o[pl.ds(at, a.shape[0]), :] = a[...]
    attn_o[...] = nn(w_out_t[...], at_o[...])
    zero = jnp.zeros((8, tokens), F32)

    def residual(i, acc):
        scale = cols[chunk(i), :][:, SCALE0 : SCALE0 + 1]
        v = xt[chunk(i), :].astype(F32) + scale * attn_o[chunk(i), :]
        hat_o[chunk(i), :] = v
        return acc + fold(v)

    mean = across(passes(width, residual, zero)) / width
    mid_o[...] = hat_o[:, pl.ds(pl.multiple_of(m * rows, rows), rows)]

    def spread(i, acc):
        v = hat_o[chunk(i), :] - mean
        return acc + fold(v * v)

    rstd = lax.rsqrt(across(passes(width, spread, zero)) / width + norm_eps)
    rstd_o[0:1, :] = rstd

    def norm(i, carry):
        w = cols[chunk(i), :]
        v = (hat_o[chunk(i), :] - mean) * rstd
        hat_o[chunk(i), :] = v
        h2_o[chunk(i), :] = (v * w[:, GAIN1 : GAIN1 + 1] + w[:, BIAS1 : BIAS1 + 1]).astype(BF16)
        return carry

    passes(width, norm, 0)
    wide[...] = nn(w_up_t[...], h2_o[...])

    def gelu(i, carry):
        u = wide[chunk(i), :]
        cdf = 0.5 + 0.5 * lax.erf(u * (0.5**0.5))
        act_o[chunk(i), :] = (u * cdf).astype(BF16)
        slope_o[chunk(i), :] = cdf + u * (jnp.exp(-0.5 * u * u) * 0.3989422804014327)
        return carry

    passes(hidden, gelu, 0)
    mlp_o[...] = nn(w_down_t[...], act_o[...])
    put_halves(m, mlp_o, m0, m2, m13)


def down_kernel(
    place, c0, c1, c2, c3, cols, attn, hat, rstd, slope, w_out, w_up, w_down,
    d0, d1, d2, d3, nb_o, dup_o, gm_o, ga_o, dy_o, vec_o,
    wide, sums,
):
    m = place[0]
    rows = c0.shape[0]
    channels = d0.shape[0]
    width, tokens = hat.shape
    hidden = slope.shape[0]
    for k, c in enumerate((c0, c1, c2, c3)):
        at = pl.ds(pl.multiple_of((m ^ k) * rows, rows), rows)
        turned = c[...].T
        dy_o[:, at] = turned
        scale = cols[:, SCALE1 : SCALE1 + 1]
        gm_o[:, at] = (turned.astype(F32) * scale).astype(BF16)
    wide[...] = nn(w_down[...], gm_o[...])

    def d_up(i, carry):
        dup_o[chunk(i), :] = (slope[chunk(i), :] * wide[chunk(i), :]).astype(BF16)
        return carry

    passes(hidden, d_up, 0)
    wide[...] = nn(w_up[...], dup_o[...])
    zero = jnp.zeros((8, tokens), F32)

    def gather(i, acc):
        d = wide[chunk(i), :]
        u = d * cols[chunk(i), :][:, GAIN1 : GAIN1 + 1]
        return acc[0] + fold(u), acc[1] + fold(u * hat[chunk(i), :])

    first, second = passes(width, gather, (zero, zero))
    first, second = across(first) / width, across(second) / width
    lane = lax.broadcasted_iota(jnp.int32, (1, tokens), 1)
    mine = ((lane >= m * rows) & (lane < (m + 1) * rows)).astype(F32)
    rstd = rstd[0:1, :]

    def back(i, carry):
        w = cols[chunk(i), :]
        d = wide[chunk(i), :]
        h = hat[chunk(i), :]
        v = rstd * (d * w[:, GAIN1 : GAIN1 + 1] - first - h * second)
        nb_o[chunk(i), :] = v
        v = v + mine * dy_o[chunk(i), :].astype(F32)
        ga_o[chunk(i), :] = (v * w[:, SCALE0 : SCALE0 + 1]).astype(BF16)
        sums[chunk(i), 0:1] = jnp.sum(d * h, axis=1, keepdims=True)
        sums[chunk(i), 1:2] = jnp.sum(d, axis=1, keepdims=True)
        sums[chunk(i), 2:3] = jnp.sum(v * attn[chunk(i), :], axis=1, keepdims=True)
        return carry

    passes(width, back, 0)
    wide[...] = nn(w_out[...], ga_o[...])
    for k, ref in enumerate((d0, d1, d2, d3)):
        at = pl.ds(pl.multiple_of((m ^ k) * channels, channels), channels)
        ref[...] = wide[at, :].astype(BF16)
    turned = sums[...].T
    vec_o[...] = jnp.zeros(vec_o.shape, F32)
    vec_o[1:2, :] = turned[0:1, :]
    vec_o[3:4, :] = turned[1:2, :]
    vec_o[4:5, :] = turned[2:3, :]


def mlp_grad_kernel(place, vec, mlp, act, dup, gm, ga, att, h2, dy, vec_o, *rest):
    grads, sums = rest[:-1], rest[-1]

    def scale(i, carry):
        v = dy[chunk(i), :].astype(F32) * mlp[chunk(i), :]
        sums[chunk(i), 0:1] = jnp.sum(v, axis=1, keepdims=True)
        return carry

    passes(dy.shape[0], scale, 0)
    vec_o[...] = vec[...]
    vec_o[5:6, :] = sums[...].T[0:1, :]
    if len(grads) == 1:
        at = 0
        for a, b in ((h2, dup), (gm, act), (ga, att)):
            grads[0][:, at : at + b.shape[0]] = nt(a[...], b[...]).astype(BF16)
            at += b.shape[0]
        return
    x, y = (place[1] >> 1) & 1, (place[1] >> 2) & 1
    a_sent, a_kept, b_sent, b_kept = grads
    n, half = a_sent.shape[0] // 4, a_sent.shape[1]

    def put(p, left, low, high):
        block = [p[i * n : (i + 1) * n, low:high] for i in range(8)]
        first = left + low < half
        at = left + low - (0 if first else half)
        cols = slice(at, at + high - low)
        for i in range(4):
            out = slice(i * n, (i + 1) * n)
            if first:
                zero, one = 4 * (i // 2) + i % 2, 4 * (i // 2) + 2 + i % 2
                a_sent[out, cols] = pick(x, block[one], block[zero])
                a_kept[out, cols] = pick(x, block[zero], block[one])
            else:
                b_sent[out, cols] = pick(y, block[4 + i], block[i])
                b_kept[out, cols] = pick(y, block[i], block[4 + i])

    left = 0
    for a, b in ((h2, dup), (gm, act), (ga, att)):
        p = nt(a[...], b[...]).astype(BF16)
        n_cols = p.shape[1]
        cut = min(max(half - left, 0), n_cols)
        if cut > 0:
            put(p, left, 0, cut)
        if cut < n_cols:
            put(p, left, cut, n_cols)
        left += n_cols


def put_halves(m, ref, own, next_to, sent):
    rows, width = own.shape[1], own.shape[0]

    def of(k):
        return ref[:, pl.ds(pl.multiple_of((m ^ k) * rows, rows), rows)]

    own[...], next_to[...] = of(0), of(2)
    sent[0:width, :] = of(1).astype(BF16)
    sent[width:, :] = of(3).astype(BF16)


def halve_kernel(own, next_to, recv, own_o, sent):
    width = own.shape[0]
    own_o[...] = own[...] + recv[0:width, :].astype(F32)
    sent[...] = (next_to[...] + recv[width:, :].astype(F32)).astype(BF16)


def put_blocks(parts, here, grads):
    at = 0
    for p in parts:
        cols = slice(at, at + p.shape[1])
        at += p.shape[1]
        if len(grads) == 1:
            grads[0][:, cols] = p
            continue
        sent, kept = grads
        n = kept.shape[0] // 4
        for b in range(4):
            even, odd = p[2 * b * n : (2 * b + 1) * n], p[(2 * b + 1) * n : (2 * b + 2) * n]
            sent[b * n : (b + 1) * n, cols] = pick(here, odd, even)
            kept[b * n : (b + 1) * n, cols] = pick(here, even, odd)


def pick(bit, a, b):
    return jnp.where(bit == 0, a, b)


def back_kernel(
    place, lengths, d0, d1, d2, d3, qkv, pt, xt, h1, stat, nb, cols, wq_t, vec,
    p0, p2, p13, vec_o, *rest,
):
    grads, (dqkv_o, score, ds, acc, buckets_of, wide, sums) = rest[:-7], rest[-7:]
    m = place[0]
    channels, tokens = d0.shape
    heads = channels // HEAD_DIM
    width = xt.shape[0]
    rows = p0.shape[1]
    blk = 128
    n_blk = tokens // blk
    n_rows = buckets_of.shape[0]
    buckets = n_rows // heads
    half = buckets // 2
    live = (page_ids(lengths, (1, tokens), 1, -1) >= 0).astype(F32)
    off = lax.broadcasted_iota(jnp.int32, (blk, blk), 1) - lax.broadcasted_iota(
        jnp.int32, (blk, blk), 0
    )

    def one_head(h):
        def rows_of(which):
            return pl.ds(which * channels + h * HEAD_DIM, HEAD_DIM)

        q, k, v = qkv[rows_of(0), :], qkv[rows_of(1), :], qkv[rows_of(2), :]
        mine = rows_of(0)
        d_att = (
            d0[mine, :].astype(F32) + d1[mine, :].astype(F32)
            + d2[mine, :].astype(F32) + d3[mine, :].astype(F32)
        )
        d_att = (d_att.astype(BF16).astype(F32) * live).astype(BF16)
        dqkv_o[rows_of(2), :] = nt(d_att, pt[h]).astype(BF16)
        score[h] = nn(v.T, d_att)
        acc[h] = jnp.zeros(acc.shape[1:], F32)
        for i in range(n_blk):
            lanes = slice(i * blk, (i + 1) * blk)
            total = jnp.zeros((8, blk), F32)
            for j in range(n_blk):
                at = slice(j * blk, (j + 1) * blk)
                prod = score[h, at, lanes] * pt[h, at, lanes].astype(F32)
                score[h, at, lanes] = prod
                total = total + fold(prod)
            total = across(total)
            for j in range(n_blk):
                at = slice(j * blk, (j + 1) * blk)
                g = score[h, at, lanes] - pt[h, at, lanes].astype(F32) * total
                g = g.astype(BF16)
                ds[h, at, lanes] = g
                slot = max(min(i - j, 2), -2) + 2
                acc[h, slot] = acc[h, slot] + g.astype(F32)
        dqkv_o[rows_of(0), :] = (nn(k, ds[h]) * HEAD_DIM**-0.5).astype(BF16)
        dqkv_o[rows_of(1), :] = nt(q, ds[h]).astype(BF16)
        near, before, after = acc[h, 2], acc[h, 1], acc[h, 3]
        corner_b, off_b = before[0:16, :], off[0:16, :] - blk
        corner_a, off_a = after[blk - 16 : blk, :], off[blk - 16 : blk, :] + blk
        first = h * buckets
        for b in range(buckets):
            if b == 0:
                v = fold(acc[h, 0]) + fold(jnp.where(off - blk <= -half, before, 0.0))
                v = v + fold(jnp.where(off <= -half, near, 0.0))
            elif b == buckets - 1:
                v = fold(acc[h, 4]) + fold(jnp.where(off + blk >= half - 1, after, 0.0))
                v = v + fold(jnp.where(off >= half - 1, near, 0.0))
            else:
                v = fold(jnp.where(off == b - half, near, 0.0))
                if b < half:
                    v = v + fold(jnp.where(off_b == b - half, corner_b, 0.0))
                elif b > half:
                    v = v + fold(jnp.where(off_a == b - half, corner_a, 0.0))
            buckets_of[first + b : first + b + 1, :] = across(v)

    for h in range(heads):
        one_head(h)
    wide[...] = nn(wq_t[...], dqkv_o[...])
    weight_grad = nt(h1[...], dqkv_o[...]).astype(BF16)
    mean, rstd = stat[0:1, :], stat[1:2, :]
    zero = jnp.zeros((8, tokens), F32)

    def gather(i, part):
        d = wide[chunk(i), :]
        hat = (xt[chunk(i), :].astype(F32) - mean) * rstd
        u = d * cols[chunk(i), :][:, GAIN0 : GAIN0 + 1]
        sums[chunk(i), 0:1] = jnp.sum(d * hat, axis=1, keepdims=True)
        sums[chunk(i), 1:2] = jnp.sum(d, axis=1, keepdims=True)
        return part[0] + fold(u), part[1] + fold(u * hat)

    first, second = passes(width, gather, (zero, zero))
    first, second = across(first) / width, across(second) / width

    def back(i, carry):
        hat = (xt[chunk(i), :].astype(F32) - mean) * rstd
        u = wide[chunk(i), :] * cols[chunk(i), :][:, GAIN0 : GAIN0 + 1]
        wide[chunk(i), :] = nb[chunk(i), :] + rstd * (u - first - hat * second)
        return carry

    passes(width, back, 0)
    put_halves(m, wide, p0, p2, p13)
    turned = sums[...].T
    vec_o[...] = vec[...]
    vec_o[0:1, :] = turned[0:1, :]
    vec_o[2:3, :] = turned[1:2, :]
    each = jnp.sum(buckets_of[...], axis=1, keepdims=True)
    shape = (n_rows, width)
    lane = lax.broadcasted_iota(jnp.int32, shape, 1)
    row = lax.broadcasted_iota(jnp.int32, shape, 0)
    vec_o[6:7, :] = across(jnp.where(lane == row + m * n_rows, each, 0.0))
    put_blocks([weight_grad], place[1] & 1, grads)
    if len(grads) > 1:
        put_vec(vec_o[...], grads[0])


def put_vec(vec, ref):
    half = vec.shape[1] // 2
    v = jnp.concatenate([vec[:, :half], vec[:, half:]])
    high = v.astype(BF16)
    n, rows = ref.shape[0], v.shape[0]
    ref[n - 2 * rows : n - rows, :half] = high
    ref[n - rows :, :half] = (v - high.astype(F32)).astype(BF16)


def get_vec(ref, width):
    n, rows, half = ref.shape[0], 16, width // 2
    v = ref[n - 2 * rows : n - rows, :half].astype(F32) + ref[n - rows :, :half].astype(F32)
    return jnp.concatenate([v[:8], v[8:]], axis=1)


def grads_second_kernel(place, a_keep, a_recv, b_keep, b_recv, s0, s1, s2, kept):
    core = place[1] & 1
    half, n, third = a_keep.shape[1], kept.shape[0] // 2, s0.shape[1]
    for j, sent in enumerate((s0, s1, s2)):
        for keep, recv, low, high in (
            (a_keep, a_recv, j * third, min((j + 1) * third, half)),
            (b_keep, b_recv, max(j * third, half) - half, (j + 1) * third - half),
        ):
            if low >= high:
                continue
            at = low + (half if keep is b_keep else 0)
            from_, to = slice(low, high), slice(at - j * third, at - j * third + high - low)
            for i in range(2):
                rows = pl.ds(pl.multiple_of(2 * i * n, 2 * n), 2 * n)
                out = slice(i * n, (i + 1) * n)
                halve_rows(
                    core, keep.at[rows, from_], recv.at[rows, from_],
                    sent.at[out, to], kept.at[out, at : at + high - low],
                )


def grads_third_kernel(place, keep, r0, r1, r2, a_sent, a_kept, b_sent, b_kept):
    x, y = (place[1] >> 1) & 1, (place[1] >> 2) & 1
    half, third = a_kept.shape[1], r0.shape[1]
    for j, recv in enumerate((r0, r1, r2)):
        low, high = j * third, (j + 1) * third
        for bit, sent, kept, first, start, stop in (
            (y, a_sent, a_kept, 0, low, min(high, half)),
            (x, b_sent, b_kept, half, max(low, half), high),
        ):
            if start >= stop:
                continue
            out = slice(start - first, stop - first)
            halve_rows(
                bit, keep.at[:, start:stop], recv.at[:, start - low : stop - low],
                sent.at[:, out], kept.at[:, out],
            )


def halve_rows(bit, keep, recv, sent, kept):
    n = kept.shape[0]
    for ref, b in ((sent, 1 - bit), (kept, bit)):
        rows = pl.ds(pl.multiple_of(b * n, n), n)
        total = keep[rows, :].astype(F32) + recv[rows, :].astype(F32)
        ref[0:n, :] = total.astype(ref.dtype)


def qkv_second_kernel(place, vec, keep, recv, sent, kept, vec_o):
    x = (place[1] >> 1) & 1
    n = kept.shape[0] // 2
    for i in range(2):
        for ref, b in ((sent, 1 - x), (kept, x)):
            rows = pl.ds(pl.multiple_of((2 * i + b) * n, n), n)
            total = keep[rows, :].astype(F32) + recv[rows, :].astype(F32)
            ref[i * n : (i + 1) * n, :] = total.astype(ref.dtype)
    vec_o[...] = vec[...] + get_vec(recv, vec.shape[1])
    put_vec(vec_o[...], sent)


def qkv_third_kernel(place, vec, keep, recv, sent, kept, vec_o):
    halve_rows((place[1] >> 2) & 1, keep, recv, sent, kept)
    vec_o[...] = vec[...] + get_vec(recv, vec.shape[1])
    put_vec(vec_o[...], sent)


def message_kernel(place, vec, b_keep, b_recv, q_recv, vec_o, o0, o1, o2, o3, turned):
    m = place[0]
    channels = o0.shape[0]
    width, share = turned.shape
    cols = slice(b_keep.shape[1] - width, b_keep.shape[1])
    turned[...] = (b_keep[:, cols] + b_recv[:, cols].astype(F32)).T
    v = vec[...] + get_vec(q_recv, vec.shape[1])
    vec_o[...] = v
    tiles = v.shape[1] // 128
    high = v.astype(BF16)
    low = (v - high.astype(F32)).astype(BF16)
    both = jnp.concatenate([high.astype(F32), low.astype(F32)]).astype(BF16)
    for k, ref in enumerate((o0, o1, o2, o3)):
        t = turned[pl.ds(pl.multiple_of((m ^ k) * channels, channels), channels), :]
        ref[0:channels, 0:share] = t.astype(ref.dtype)
        if k:
            for i in range(tiles):
                at = channels + 16 * i
                ref[at : at + 16, :] = both[:, 128 * i : 128 * (i + 1)]


def last_kernel(a_keep, a_recv, b_keep, b_recv, q_keep, q_recv, up_o, down_o, qkv_o):
    hidden = up_o.shape[1]
    channels = qkv_o.shape[2]
    a = a_keep[...] + a_recv[...].astype(F32)
    share, half = a.shape
    rest = slice(0, 2 * hidden - half)
    up_o[...] = a[:, :hidden]
    down_o[:, : half - hidden] = a[:, hidden:]
    down_o[:, half - hidden :] = b_keep[:, rest] + b_recv[:, rest].astype(F32)
    q = q_keep[...] + q_recv[0:share, :].astype(F32)
    for i in range(3):
        qkv_o[i] = q[:, i * channels : (i + 1) * channels]


def small_kernel(vec, o0, o1, o2, o3, out, gains, biases, scales, table):
    channels, share = out.shape
    others = (o1, o2, o3)
    total = o0[...]
    v = vec[...]
    for ref in others:
        total = total + ref[0:channels, 0:share].astype(F32)
        parts = []
        for i in range(v.shape[1] // 128):
            at = channels + 16 * i
            both = ref[at : at + 16, :].astype(F32)
            parts.append(both[:8] + both[8:])
        v = v + jnp.concatenate(parts, axis=1)
    out[...] = total
    gains[...] = v[0:2]
    biases[...] = v[2:4]
    scales[...] = v[4:6]
    n = table.shape[1]
    for h in range(table.shape[0]):
        table[h : h + 1, :] = v[6:7, h * n : (h + 1) * n]


def input_kernel(own, recv, dy, out):
    total = own[...] + recv[...].astype(F32)
    out[...] = (dy[...].astype(F32) + total.T).astype(BF16)


def output_kernel(own, recv, mid, cols, out):
    total = own[...] + recv[...].astype(F32)
    out[...] = (mid[...] + cols[:, SCALE1 : SCALE1 + 1] * total).T.astype(BF16)


def body(
    tokens,
    page_lengths,
    norm_gains,
    norm_biases,
    layer_scales,
    w_qkv,
    rel_table,
    w_out,
    w_up,
    w_down,
    cotangent,
):
    mp, dp = lax.axis_size("mp"), lax.axis_size("dp")
    rows, width = tokens.shape
    group = rows * mp
    channels = w_qkv.shape[2]
    hidden = w_up.shape[1]
    heads = channels // HEAD_DIM
    buckets = rel_table.shape[0]
    m, d = lax.axis_index("mp"), lax.axis_index("dp")
    place = jnp.stack([m, d]).astype(jnp.int32)

    def swap(v, k, axis="mp", name="rows"):
        n = mp if axis == "mp" else dp
        with jax.named_scope(name):
            return lax.ppermute(v, axis, [(i, i ^ k) for i in range(n)])

    def after(v, *seen):
        return lax.optimization_barrier((v,) + seen)[0]

    fast = dp == 8 and (width // dp) % 16 == 0 and hidden == width

    cols = jnp.concatenate(
        [norm_gains[0:1], norm_biases[0:1], norm_gains[1:2], norm_biases[1:2], layer_scales]
    ).T
    wq = jnp.transpose(w_qkv, (1, 2, 0)).reshape(3 * channels, width)

    piece = channels // 4
    sent = jnp.concatenate([tokens, lax.dynamic_slice_in_dim(w_out, (d & 3) * piece, piece, 0)])
    x1, x2 = swap(sent, 1, name="x"), swap(sent, 2, name="x")
    x = [sent, x1, x2, swap(after(x2, x1), 1, name="x")]
    dy2 = swap(after(cotangent, *x[1:]), 2, name="dy")
    dy1 = swap(after(cotangent, *x[1:]), 1, name="dy")
    wq_t, w_up_t, w_down_t = call(
        turn_kernel,
        [like((width, 3 * channels), BF16), like((hidden, width), BF16), like((width, hidden), BF16)],
        [wq, w_up, w_down],
    )
    pattern, ids = call(
        bias_kernel,
        [like((heads, 3, 128, 128), F32), like((group, 128), jnp.int32)],
        [place, page_lengths, rel_table],
        n_smem=3,
    )
    x[1:] = lax.optimization_barrier((x[1:], wq_t, pattern))[0]
    (part,) = call(pieces_kernel, [like((4, piece, width), BF16)], x)
    part_x = swap(part, 2, "dp", name="w")
    wq_now = after(wq, wq_t, w_up_t, w_down_t)
    xt, h1, stat, qkv, pt, att, att_top, att_low = call(
        head_kernel,
        [
            like((width, group), BF16),
            like((width, group), BF16),
            like((8, group), F32),
            like((3 * channels, group), BF16),
            like((heads, group, group), BF16),
            like((channels, group), BF16),
            like((channels // 2, group), BF16),
            like((channels // 2, group), BF16),
        ],
        [place, page_lengths, rel_table] + x + [pattern, ids, cols, wq_now],
        n_smem=3,
        scratch=[
            pltpu.VMEM((heads, group, group), F32),
        ],
        limit=24,
        us=10,
    )
    (parts,) = call(
        pair_kernel, [like((8, piece, width), BF16)], [part, after(part_x, att, dy1, dy2)]
    )
    att_top, att_low, att_sent = after(att_top, parts), after(att_low, parts), after(att, parts)
    a2t, a2b = swap(att_top, 2, name="att"), swap(att_low, 2, name="att")
    a3b, a1 = swap(att_low, 3, name="att"), swap(att_sent, 1, name="att")
    atts = [att, a1, a2t, a2b, swap(a2t, 1, name="att"), a3b]
    dy = [cotangent, dy1, dy2, swap(after(dy2, parts), 1, name="dy")]
    w_pieces = [parts, swap(parts, 1, "dp", name="w")]
    w_out_full, w_out_t = call(
        out_weight_kernel, [like((width, width), BF16)] * 2, [place] + w_pieces, n_smem=1
    )
    act_like = like((width, group), BF16)
    hid_like = like((hidden, group), BF16)
    wide_like = like((width, group), F32)
    block = like((width, rows), F32)
    blocks = [block, block, like((2 * width, rows), BF16)]
    att_all, attn, hat, rstd, h2, act, slope, mid, mlp_part, m0, m2, m13 = call(
        up_kernel,
        [act_like, wide_like, wide_like, like((8, group), F32), act_like, hid_like]
        + [like((hidden, group), F32), block, wide_like]
        + blocks,
        [place] + atts + [after(xt, dy1), cols, w_out_t, w_up_t, w_down_t],
        n_smem=1,
        scratch=[pltpu.VMEM((hidden, group), F32)],
        us=10,
    )
    m_recv = swap(m13, 1, name="mlp")
    d0, d1, d2, d3, nb, dup, gm, ga, dy_t, vec = call(
        down_kernel,
        [like((channels, group), BF16)] * 4
        + [wide_like, hid_like, act_like, act_like, act_like, like((8, width), F32)],
        [place] + dy + [cols, attn, hat, rstd, slope, w_out_full, w_up, w_down],
        n_smem=1,
        scratch=[pltpu.VMEM((max(width, hidden), group), F32), pltpu.VMEM((width, 128), F32)],
        us=10,
    )
    d_att = [d0] + [swap(v, k, name="d_att") for k, v in ((1, d1), (2, d2), (3, d3))]
    grad_cols = 2 * hidden + width
    share = width // dp
    half = grad_cols // 2
    if fast:
        grad_like = [like((width // 2, half), BF16)] * 4
    else:
        grad_like = [like((width, grad_cols), BF16)]
    vec, *grads = call(
        mlp_grad_kernel,
        [like((8, width), F32)] + grad_like,
        [place, vec, mlp_part, act, dup, gm, ga, att_all, h2, dy_t],
        n_smem=1,
        scratch=[pltpu.VMEM((width, 128), F32)],
    )
    if fast:
        a_sent, a_kept, b_sent, b_kept = grads
        a_recv = swap(a_sent, 2, "dp", name="grads_a")
        b_recv = swap(b_sent, 4, "dp", name="grads_b")

    def halved(own, next_to, recv, name, us=0.01, seen=()):
        half_like = [block, like((width, rows), BF16)]
        own, sent = call(halve_kernel, half_like, [own, next_to, recv], us=us)
        return [own, swap(after(sent, *seen), 2, name=name)]

    mlp = halved(m0, m2, m_recv, "mlp", seen=d_att[1:])

    n = 3 * channels
    extra = 4 * vec.shape[0]
    if fast:
        grad_like = [like((width // 2 + extra, n), BF16), like((width // 2, n), BF16)]
    else:
        grad_like = [like((width, n), BF16)]
    p0, p2, p13, vec, *qkv_grads = call(
        back_kernel,
        blocks + [like((8, width), F32)] + grad_like,
        [place, page_lengths] + d_att + [qkv, pt, xt, h1, stat, nb, cols, wq_t, vec],
        n_smem=2,
        scratch=[
            pltpu.VMEM((n, group), BF16),
            pltpu.VMEM((heads, group, group), F32),
            pltpu.VMEM((heads, group, group), BF16),
            pltpu.VMEM((heads, 5, 128, 128), F32),
            pltpu.VMEM((heads * buckets, 128), F32),
            pltpu.VMEM((width, group), F32),
            pltpu.VMEM((width, 128), F32),
        ],
        limit=24,
        us=10,
    )
    p_recv = swap(after(p13, mlp[1]), 1, name="back")
    back = halved(p0, p2, p_recv, "back", us=10)

    def reduced(g):
        g = g.reshape(dp, width // dp, g.shape[1])
        bit = 1
        while bit < dp:
            g = g.reshape(g.shape[0] // 2, 2, width // dp, g.shape[-1])
            here = (d & bit) // bit
            sent = lax.dynamic_index_in_dim(g, 1 - here, 1, keepdims=False)
            kept = lax.dynamic_index_in_dim(g, here, 1, keepdims=False)
            g = kept.astype(F32) + swap(sent, bit, "dp").astype(F32)
            bit *= 2
            if bit < dp:
                g = g.astype(BF16)
        return g[0]

    if fast:
        q_recv = swap(after(qkv_grads[0], mlp[1]), 1, "dp", name="qkv_core")
        vec_like = [like(vec.shape, F32)]
        sent, kept, vec = call(
            qkv_second_kernel,
            [like((2 * share + extra, n), BF16), like((2 * share, n), F32)] + vec_like,
            [place, vec, qkv_grads[1], q_recv],
            n_smem=1,
        )
        recv = swap(sent, 2, "dp", name="qkv_x")
        g0, g1, g2, g_kept = call(
            grads_second_kernel,
            [like((2 * share, grad_cols // 3), BF16)] * 3 + [like((2 * share, grad_cols), BF16)],
            [place, after(a_kept, vec), a_recv, b_kept, b_recv],
            n_smem=1,
        )
        g_recv = [swap(g, 1, "dp", name="grads_core") for g in (g0, g1, g2)]
        a_sent, a_kept, b_sent, b_kept = call(
            grads_third_kernel,
            [like((share, half), BF16), like((share, half), F32)] * 2,
            [place, g_kept] + g_recv,
            n_smem=1,
        )
        a_recv = swap(a_sent, 4, "dp", name="grads_a")
        b_recv = swap(b_sent, 2, "dp", name="grads_b")
        sent, kept, vec = call(
            qkv_third_kernel,
            [like((share + extra, n), BF16), like((share, n), F32)] + vec_like,
            [place, after(vec, a_kept, back[0]), kept, recv],
            n_smem=1,
        )
        recv = swap(sent, 4, "dp", name="qkv_y")
        message = like((channels + 2 * vec.size // 128, 128), BF16)
        vec, o0, o1, o2, o3 = call(
            message_kernel,
            vec_like + [like((channels, share), F32)] + [message] * 3,
            [place, after(vec, a_recv), b_kept, b_recv, recv],
            n_smem=1,
            scratch=[pltpu.VMEM((width, share), F32)],
        )
        grad_up, grad_down, grad_qkv = call(
            last_kernel,
            [like((share, hidden), F32)] * 2 + [like((3, share, channels), F32)],
            [a_kept, a_recv, b_kept, b_recv, after(kept, o1), recv],
        )
        o1, o2, o3 = (swap(v, k, name="out") for k, v in ((1, o1), (2, o2), (3, o3)))
        grad_out, gains, biases, scales, grad_table = call(
            small_kernel,
            [like((channels, share), F32)]
            + [like((2, width), F32)] * 3
            + [like((heads * mp, buckets), F32)],
            [vec, o0, o1, o2, o3],
        )
        grad_qkv = jnp.transpose(grad_qkv, (1, 0, 2))
    else:
        summed = reduced(grads[0])
        grad_qkv = reduced(qkv_grads[0]).reshape(share, 3, channels)
        grad_up, grad_down = summed[:, :hidden], summed[:, hidden : 2 * hidden]
        turned = summed[:, 2 * hidden :].T

        def out_part(k):
            return lax.dynamic_slice_in_dim(turned, (m ^ k) * channels, channels, 0)

        grad_out = out_part(0)
        for k in range(1, mp):
            grad_out = grad_out + swap(out_part(k).astype(BF16), k).astype(F32)
        bit = 1
        while bit < dp:
            vec = vec + swap(vec, bit, "dp", name="vec")
            bit *= 2
        for k in (1, 2):
            vec = vec + swap(vec, k, name="vec")
        gains, biases, scales = vec[0:2], vec[2:4], vec[4:6]
        grad_table = vec[6, : heads * mp * buckets].reshape(heads * mp, buckets)

    (output,) = call(output_kernel, [like((rows, width), BF16)], mlp + [mid, cols])
    (grad_input,) = call(input_kernel, [like((rows, width), BF16)], back + [cotangent], us=10)
    return (
        output,
        grad_input,
        gains,
        biases,
        scales,
        grad_qkv,
        grad_table.T,
        grad_out,
        grad_up,
        grad_down.T,
    )


def solution(mesh):
    placed = (
        P(("dp", "mp"), None),
        P("dp", None),
        P(),
        P(),
        P(),
        P(None, None, "mp"),
        P(),
        P("mp", None),
        P(None, "mp"),
        P("mp", None),
        P(("dp", "mp"), None),
    )
    return jax.shard_map(
        body,
        mesh=mesh,
        in_specs=placed,
        out_specs=(
            P(("dp", "mp"), None),
            P(("dp", "mp"), None),
            P(),
            P(),
            P(),
            P("dp", None, "mp"),
            P(),
            P("mp", "dp"),
            P("dp", "mp"),
            P("mp", "dp"),
        ),
        check_vma=False,
    )
```

```python
import jax
import jax.numpy as jnp
from jax import lax
from jax.experimental import pallas as pl
from jax.experimental.pallas import tpu as pltpu
from jax.sharding import PartitionSpec as P

HEAD_DIM = 64
SPEED = 1.15e9
norm_eps = 1e-06
masked_score = -1000000000.0
F32 = jnp.float32
BF16 = jnp.bfloat16
SMEM = pl.BlockSpec(memory_space=pltpu.SMEM)
VMEM = pl.BlockSpec(memory_space=pltpu.VMEM)
CHUNK = 64
GAIN0, BIAS0, GAIN1, BIAS1, SCALE0, SCALE1 = range(6)


def call(kernel, outs, args, n_smem=0, scratch=(), us=0.01, limit=8):
    return pl.pallas_call(
        kernel,
        out_shape=tuple(outs),
        in_specs=[SMEM] * n_smem + [VMEM] * (len(args) - n_smem),
        out_specs=tuple([VMEM] * len(outs)),
        scratch_shapes=list(scratch),
        compiler_params=pltpu.CompilerParams(vmem_limit_bytes=limit << 20),
        name=kernel.__name__,
        cost_estimate=pl.CostEstimate(flops=int(us * SPEED), bytes_accessed=8, transcendentals=0),
    )(*args)


def like(shape, dtype):
    return jax.ShapeDtypeStruct(shape, dtype)


def nn(a, b):
    return lax.dot_general(a, b, (((1,), (0,)), ((), ())), preferred_element_type=F32)


def nt(a, b):
    return lax.dot_general(a, b, (((1,), (1,)), ((), ())), preferred_element_type=F32)


def fold(v):
    return jnp.sum(v.reshape(v.shape[0] // 8, 8, v.shape[1]), axis=0)


def across(v):
    return jnp.sum(v, axis=0, keepdims=True)


def passes(rows, step, start):
    return lax.fori_loop(0, rows // CHUNK, step, start, unroll=True)


def chunk(i):
    return pl.ds(pl.multiple_of(i * CHUNK, CHUNK), CHUNK)


def page_ids(lengths, shape, axis, dead):
    at = lax.broadcasted_iota(jnp.int32, shape, axis)
    page = jnp.zeros(shape, jnp.int32)
    end = jnp.int32(0)
    pages = lengths.shape[1]
    for p in range(pages):
        end = end + lengths[0, p]
        page = page + (at >= end).astype(jnp.int32)
    return jnp.where(page < pages - 1, page, dead)


def turn_kernel(wq, wu, wd, wq_o, wu_o, wd_o):
    wq_o[...] = wq[...].T
    wu_o[...] = wu[...].T
    wd_o[...] = wd[...].T


def pieces_kernel(x0, x1, x2, x3, out):
    n = out.shape[1]
    for k, ref in enumerate((x0, x1, x2, x3)):
        out[k] = ref[ref.shape[0] - n :, :]


def pair_kernel(a, b, out):
    out[0:4] = a[...]
    out[4:8] = b[...]


def out_weight_kernel(place, here, there, w_o, wt_o):
    m, d = place[0], place[1]
    rows = here.shape[1]
    for c, ref in enumerate((here, there)):
        for b in range(2):
            part = (d & 3) ^ (c + 2 * b)
            for k in range(4):
                at = pl.multiple_of((m ^ k) * 4 * rows + part * rows, rows)
                w_o[pl.ds(at, rows), :] = ref[4 * b + k]
    wt_o[...] = w_o[...].T


def bias_kernel(place, lengths, table, pattern, ids):
    buckets = table.shape[0]
    half = buckets // 2
    heads, _, blk, _ = pattern.shape
    ids[...] = page_ids(lengths, ids.shape, 0, -2)
    off = lax.broadcasted_iota(jnp.int32, (blk, blk), 1) - lax.broadcasted_iota(
        jnp.int32, (blk, blk), 0
    )
    for h in range(heads):
        col = place[0] * heads + h
        low, high = table[0, col], table[buckets - 1, col]
        near = jnp.where(off >= half - 1, high, low)
        for b in range(1, buckets - 1):
            near = jnp.where(off == b - half, table[b, col], near)
        before = jnp.full((blk, blk), low, F32)
        for b in range(1, half):
            before = jnp.where(off - blk == b - half, table[b, col], before)
        after = jnp.full((blk, blk), high, F32)
        for b in range(half + 1, buckets - 1):
            after = jnp.where(off + blk == b - half, table[b, col], after)
        pattern[h, 0], pattern[h, 1], pattern[h, 2] = before, near, after


def head_kernel(
    place, lengths, table, x0, x1, x2, x3, pattern, ids, cols, wq,
    xt_o, h1_o, stat_o, qkv_o, pt_o, att_o, top_o, low_o,
    score,
):
    m = place[0]
    width, tokens = xt_o.shape
    rows = tokens // 4
    channels = att_o.shape[0]
    heads = channels // HEAD_DIM
    buckets = table.shape[0]
    for k, ref in enumerate((x0, x1, x2, x3)):
        at = pl.multiple_of((m ^ k) * rows, rows)
        xt_o[:, pl.ds(at, rows)] = ref[0:rows, :].T

    def add(i, acc):
        return acc + fold(xt_o[chunk(i), :].astype(F32))

    zero = jnp.zeros((8, tokens), F32)
    mean = across(passes(width, add, zero)) / width

    def spread(i, acc):
        v = xt_o[chunk(i), :].astype(F32) - mean
        return acc + fold(v * v)

    rstd = lax.rsqrt(across(passes(width, spread, zero)) / width + norm_eps)
    stat_o[0:1, :] = mean
    stat_o[1:2, :] = rstd

    def norm(i, carry):
        v = (xt_o[chunk(i), :].astype(F32) - mean) * rstd
        w = cols[chunk(i), :]
        h1_o[chunk(i), :] = (v * w[:, GAIN0 : GAIN0 + 1] + w[:, BIAS0 : BIAS0 + 1]).astype(BF16)
        return carry

    passes(width, norm, 0)
    qkv_o[...] = nn(wq[...], h1_o[...]).astype(BF16)
    qkv_o[0:channels, :] = qkv_o[0:channels, :] * BF16(HEAD_DIM**-0.5)

    own_ids = page_ids(lengths, (1, tokens), 1, -1)
    live = (own_ids >= 0).astype(F32)
    blk = 128
    n_blk = tokens // blk

    def one_head(h):
        col = m * heads + h
        low, high = table[0, col], table[buckets - 1, col]

        def rows_of(which):
            return pl.ds(which * channels + h * HEAD_DIM, HEAD_DIM)

        q, k, v = qkv_o[rows_of(0), :], qkv_o[rows_of(1), :], qkv_o[rows_of(2), :]
        score[h] = nn(k.T, q)
        for i in range(n_blk):
            lanes = slice(i * blk, (i + 1) * blk)
            query_id = own_ids[:, lanes]
            top = jnp.full((8, blk), -3e38, F32)
            for j in range(n_blk):
                at = slice(j * blk, (j + 1) * blk)
                if abs(i - j) <= 1:
                    bias = pattern[h, i - j + 1]
                else:
                    bias = low if i < j else high
                s = jnp.where(ids[at, :] == query_id, score[h, at, lanes] + bias, masked_score)
                score[h, at, lanes] = s
                top = jnp.maximum(top, jnp.max(s.reshape(blk // 8, 8, blk), axis=0))
            top = jnp.max(top, axis=0, keepdims=True)
            total = jnp.zeros((8, blk), F32)
            for j in range(n_blk):
                at = slice(j * blk, (j + 1) * blk)
                e = jnp.exp(score[h, at, lanes] - top)
                score[h, at, lanes] = e
                total = total + fold(e)
            scale = 1.0 / across(total)
            for j in range(n_blk):
                at = slice(j * blk, (j + 1) * blk)
                pt_o[h, at, lanes] = (score[h, at, lanes] * scale).astype(BF16)
        mixed = nn(v, pt_o[h]) * live
        att_o[h * HEAD_DIM : (h + 1) * HEAD_DIM, :] = mixed.astype(BF16)

    for h in range(heads):
        one_head(h)
    half_rows = channels // 2
    top_o[...], low_o[...] = att_o[0:half_rows, :], att_o[half_rows:, :]


def up_kernel(
    place, a0, a1, a2t, a2b, a3t, a3b, xt, cols, w_out_t, w_up_t, w_down_t,
    at_o, attn_o, hat_o, rstd_o, h2_o, act_o, slope_o, mid_o, mlp_o, m0, m2, m13,
    wide,
):
    m = place[0]
    rows = mid_o.shape[1]
    channels = a0.shape[0]
    width, tokens = xt.shape
    hidden = act_o.shape[0]
    top = channels // 2
    for k, first, a in ((0, 0, a0), (1, 0, a1), (2, 0, a2t), (2, top, a2b), (3, 0, a3t), (3, top, a3b)):
        at = pl.multiple_of((m ^ k) * channels + first, top)
        at_o[pl.ds(at, a.shape[0]), :] = a[...]
    attn_o[...] = nn(w_out_t[...], at_o[...])
    zero = jnp.zeros((8, tokens), F32)

    def residual(i, acc):
        scale = cols[chunk(i), :][:, SCALE0 : SCALE0 + 1]
        v = xt[chunk(i), :].astype(F32) + scale * attn_o[chunk(i), :]
        hat_o[chunk(i), :] = v
        return acc + fold(v)

    mean = across(passes(width, residual, zero)) / width
    mid_o[...] = hat_o[:, pl.ds(pl.multiple_of(m * rows, rows), rows)]

    def spread(i, acc):
        v = hat_o[chunk(i), :] - mean
        return acc + fold(v * v)

    rstd = lax.rsqrt(across(passes(width, spread, zero)) / width + norm_eps)
    rstd_o[0:1, :] = rstd

    def norm(i, carry):
        w = cols[chunk(i), :]
        v = (hat_o[chunk(i), :] - mean) * rstd
        hat_o[chunk(i), :] = v
        h2_o[chunk(i), :] = (v * w[:, GAIN1 : GAIN1 + 1] + w[:, BIAS1 : BIAS1 + 1]).astype(BF16)
        return carry

    passes(width, norm, 0)
    wide[...] = nn(w_up_t[...], h2_o[...])

    def gelu(i, carry):
        u = wide[chunk(i), :]
        cdf = 0.5 + 0.5 * lax.erf(u * (0.5**0.5))
        act_o[chunk(i), :] = (u * cdf).astype(BF16)
        slope_o[chunk(i), :] = cdf + u * (jnp.exp(-0.5 * u * u) * 0.3989422804014327)
        return carry

    passes(hidden, gelu, 0)
    mlp_o[...] = nn(w_down_t[...], act_o[...])
    put_halves(m, mlp_o, m0, m2, m13)


def down_kernel(
    place, c0, c1, c2, c3, cols, attn, hat, rstd, slope, w_out, w_up, w_down,
    d0, d1, d2, d3, nb_o, dup_o, gm_o, ga_o, dy_o, vec_o,
    wide, sums,
):
    m = place[0]
    rows = c0.shape[0]
    channels = d0.shape[0]
    width, tokens = hat.shape
    hidden = slope.shape[0]
    for k, c in enumerate((c0, c1, c2, c3)):
        at = pl.ds(pl.multiple_of((m ^ k) * rows, rows), rows)
        turned = c[...].T
        dy_o[:, at] = turned
        scale = cols[:, SCALE1 : SCALE1 + 1]
        gm_o[:, at] = (turned.astype(F32) * scale).astype(BF16)
    wide[...] = nn(w_down[...], gm_o[...])

    def d_up(i, carry):
        dup_o[chunk(i), :] = (slope[chunk(i), :] * wide[chunk(i), :]).astype(BF16)
        return carry

    passes(hidden, d_up, 0)
    wide[...] = nn(w_up[...], dup_o[...])
    zero = jnp.zeros((8, tokens), F32)

    def gather(i, acc):
        d = wide[chunk(i), :]
        u = d * cols[chunk(i), :][:, GAIN1 : GAIN1 + 1]
        return acc[0] + fold(u), acc[1] + fold(u * hat[chunk(i), :])

    first, second = passes(width, gather, (zero, zero))
    first, second = across(first) / width, across(second) / width
    lane = lax.broadcasted_iota(jnp.int32, (1, tokens), 1)
    mine = ((lane >= m * rows) & (lane < (m + 1) * rows)).astype(F32)
    rstd = rstd[0:1, :]

    def back(i, carry):
        w = cols[chunk(i), :]
        d = wide[chunk(i), :]
        h = hat[chunk(i), :]
        v = rstd * (d * w[:, GAIN1 : GAIN1 + 1] - first - h * second)
        nb_o[chunk(i), :] = v
        v = v + mine * dy_o[chunk(i), :].astype(F32)
        ga_o[chunk(i), :] = (v * w[:, SCALE0 : SCALE0 + 1]).astype(BF16)
        sums[chunk(i), 0:1] = jnp.sum(d * h, axis=1, keepdims=True)
        sums[chunk(i), 1:2] = jnp.sum(d, axis=1, keepdims=True)
        sums[chunk(i), 2:3] = jnp.sum(v * attn[chunk(i), :], axis=1, keepdims=True)
        return carry

    passes(width, back, 0)
    wide[...] = nn(w_out[...], ga_o[...])
    for k, ref in enumerate((d0, d1, d2, d3)):
        at = pl.ds(pl.multiple_of((m ^ k) * channels, channels), channels)
        ref[...] = wide[at, :].astype(BF16)
    turned = sums[...].T
    vec_o[...] = jnp.zeros(vec_o.shape, F32)
    vec_o[1:2, :] = turned[0:1, :]
    vec_o[3:4, :] = turned[1:2, :]
    vec_o[4:5, :] = turned[2:3, :]


def mlp_grad_kernel(place, vec, mlp, act, dup, gm, ga, att, h2, dy, vec_o, *rest):
    grads, sums = rest[:-1], rest[-1]

    def scale(i, carry):
        v = dy[chunk(i), :].astype(F32) * mlp[chunk(i), :]
        sums[chunk(i), 0:1] = jnp.sum(v, axis=1, keepdims=True)
        return carry

    passes(dy.shape[0], scale, 0)
    vec_o[...] = vec[...]
    vec_o[5:6, :] = sums[...].T[0:1, :]
    if len(grads) == 1:
        at = 0
        for a, b in ((h2, dup), (gm, act), (ga, att)):
            grads[0][:, at : at + b.shape[0]] = nt(a[...], b[...]).astype(BF16)
            at += b.shape[0]
        return
    x, y = (place[1] >> 1) & 1, (place[1] >> 2) & 1
    a_sent, a_kept, b_sent, b_kept = grads
    n, half = a_sent.shape[0] // 4, a_sent.shape[1]

    def put(p, left, low, high):
        block = [p[i * n : (i + 1) * n, low:high] for i in range(8)]
        first = left + low < half
        at = left + low - (0 if first else half)
        cols = slice(at, at + high - low)
        for i in range(4):
            out = slice(i * n, (i + 1) * n)
            if first:
                zero, one = 4 * (i // 2) + i % 2, 4 * (i // 2) + 2 + i % 2
                a_sent[out, cols] = pick(x, block[one], block[zero])
                a_kept[out, cols] = pick(x, block[zero], block[one])
            else:
                b_sent[out, cols] = pick(y, block[4 + i], block[i])
                b_kept[out, cols] = pick(y, block[i], block[4 + i])

    left = 0
    for a, b in ((h2, dup), (gm, act), (ga, att)):
        p = nt(a[...], b[...]).astype(BF16)
        n_cols = p.shape[1]
        cut = min(max(half - left, 0), n_cols)
        if cut > 0:
            put(p, left, 0, cut)
        if cut < n_cols:
            put(p, left, cut, n_cols)
        left += n_cols


def put_halves(m, ref, own, next_to, sent):
    rows, width = own.shape[1], own.shape[0]

    def of(k):
        return ref[:, pl.ds(pl.multiple_of((m ^ k) * rows, rows), rows)]

    own[...], next_to[...] = of(0), of(2)
    sent[0:width, :] = of(1).astype(BF16)
    sent[width:, :] = of(3).astype(BF16)


def halve_kernel(own, next_to, recv, own_o, sent):
    width = own.shape[0]
    own_o[...] = own[...] + recv[0:width, :].astype(F32)
    sent[...] = (next_to[...] + recv[width:, :].astype(F32)).astype(BF16)


def put_blocks(parts, here, grads):
    at = 0
    for p in parts:
        cols = slice(at, at + p.shape[1])
        at += p.shape[1]
        if len(grads) == 1:
            grads[0][:, cols] = p
            continue
        sent, kept = grads
        n = kept.shape[0] // 4
        for b in range(4):
            even, odd = p[2 * b * n : (2 * b + 1) * n], p[(2 * b + 1) * n : (2 * b + 2) * n]
            sent[b * n : (b + 1) * n, cols] = pick(here, odd, even)
            kept[b * n : (b + 1) * n, cols] = pick(here, even, odd)


def pick(bit, a, b):
    return jnp.where(bit == 0, a, b)


def back_kernel(
    place, lengths, d0, d1, d2, d3, qkv, pt, xt, h1, stat, nb, cols, wq_t, vec,
    p0, p2, p13, vec_o, *rest,
):
    grads, (dqkv_o, score, ds, acc, buckets_of, wide, sums) = rest[:-7], rest[-7:]
    m = place[0]
    channels, tokens = d0.shape
    heads = channels // HEAD_DIM
    width = xt.shape[0]
    rows = p0.shape[1]
    blk = 128
    n_blk = tokens // blk
    n_rows = buckets_of.shape[0]
    buckets = n_rows // heads
    half = buckets // 2
    live = (page_ids(lengths, (1, tokens), 1, -1) >= 0).astype(F32)
    off = lax.broadcasted_iota(jnp.int32, (blk, blk), 1) - lax.broadcasted_iota(
        jnp.int32, (blk, blk), 0
    )

    def one_head(h):
        def rows_of(which):
            return pl.ds(which * channels + h * HEAD_DIM, HEAD_DIM)

        q, k, v = qkv[rows_of(0), :], qkv[rows_of(1), :], qkv[rows_of(2), :]
        mine = rows_of(0)
        d_att = (
            d0[mine, :].astype(F32) + d1[mine, :].astype(F32)
            + d2[mine, :].astype(F32) + d3[mine, :].astype(F32)
        )
        d_att = (d_att.astype(BF16).astype(F32) * live).astype(BF16)
        dqkv_o[rows_of(2), :] = nt(d_att, pt[h]).astype(BF16)
        score[h] = nn(v.T, d_att)
        acc[h] = jnp.zeros(acc.shape[1:], F32)
        for i in range(n_blk):
            lanes = slice(i * blk, (i + 1) * blk)
            total = jnp.zeros((8, blk), F32)
            for j in range(n_blk):
                at = slice(j * blk, (j + 1) * blk)
                prod = score[h, at, lanes] * pt[h, at, lanes].astype(F32)
                score[h, at, lanes] = prod
                total = total + fold(prod)
            total = across(total)
            for j in range(n_blk):
                at = slice(j * blk, (j + 1) * blk)
                g = score[h, at, lanes] - pt[h, at, lanes].astype(F32) * total
                g = g.astype(BF16)
                ds[h, at, lanes] = g
                slot = max(min(i - j, 2), -2) + 2
                acc[h, slot] = acc[h, slot] + g.astype(F32)
        dqkv_o[rows_of(0), :] = (nn(k, ds[h]) * HEAD_DIM**-0.5).astype(BF16)
        dqkv_o[rows_of(1), :] = nt(q, ds[h]).astype(BF16)
        near, before, after = acc[h, 2], acc[h, 1], acc[h, 3]
        corner_b, off_b = before[0:16, :], off[0:16, :] - blk
        corner_a, off_a = after[blk - 16 : blk, :], off[blk - 16 : blk, :] + blk
        first = h * buckets
        for b in range(buckets):
            if b == 0:
                v = fold(acc[h, 0]) + fold(jnp.where(off - blk <= -half, before, 0.0))
                v = v + fold(jnp.where(off <= -half, near, 0.0))
            elif b == buckets - 1:
                v = fold(acc[h, 4]) + fold(jnp.where(off + blk >= half - 1, after, 0.0))
                v = v + fold(jnp.where(off >= half - 1, near, 0.0))
            else:
                v = fold(jnp.where(off == b - half, near, 0.0))
                if b < half:
                    v = v + fold(jnp.where(off_b == b - half, corner_b, 0.0))
                elif b > half:
                    v = v + fold(jnp.where(off_a == b - half, corner_a, 0.0))
            buckets_of[first + b : first + b + 1, :] = across(v)

    for h in range(heads):
        one_head(h)
    wide[...] = nn(wq_t[...], dqkv_o[...])
    weight_grad = nt(h1[...], dqkv_o[...]).astype(BF16)
    mean, rstd = stat[0:1, :], stat[1:2, :]
    zero = jnp.zeros((8, tokens), F32)

    def gather(i, part):
        d = wide[chunk(i), :]
        hat = (xt[chunk(i), :].astype(F32) - mean) * rstd
        u = d * cols[chunk(i), :][:, GAIN0 : GAIN0 + 1]
        sums[chunk(i), 0:1] = jnp.sum(d * hat, axis=1, keepdims=True)
        sums[chunk(i), 1:2] = jnp.sum(d, axis=1, keepdims=True)
        return part[0] + fold(u), part[1] + fold(u * hat)

    first, second = passes(width, gather, (zero, zero))
    first, second = across(first) / width, across(second) / width

    def back(i, carry):
        hat = (xt[chunk(i), :].astype(F32) - mean) * rstd
        u = wide[chunk(i), :] * cols[chunk(i), :][:, GAIN0 : GAIN0 + 1]
        wide[chunk(i), :] = nb[chunk(i), :] + rstd * (u - first - hat * second)
        return carry

    passes(width, back, 0)
    put_halves(m, wide, p0, p2, p13)
    turned = sums[...].T
    vec_o[...] = vec[...]
    vec_o[0:1, :] = turned[0:1, :]
    vec_o[2:3, :] = turned[1:2, :]
    each = jnp.sum(buckets_of[...], axis=1, keepdims=True)
    shape = (n_rows, width)
    lane = lax.broadcasted_iota(jnp.int32, shape, 1)
    row = lax.broadcasted_iota(jnp.int32, shape, 0)
    vec_o[6:7, :] = across(jnp.where(lane == row + m * n_rows, each, 0.0))
    put_blocks([weight_grad], place[1] & 1, grads)
    if len(grads) > 1:
        put_vec(vec_o[...], grads[0])


def put_vec(vec, ref):
    half = vec.shape[1] // 2
    v = jnp.concatenate([vec[:, :half], vec[:, half:]])
    high = v.astype(BF16)
    n, rows = ref.shape[0], v.shape[0]
    ref[n - 2 * rows : n - rows, :half] = high
    ref[n - rows :, :half] = (v - high.astype(F32)).astype(BF16)


def get_vec(ref, width):
    n, rows, half = ref.shape[0], 16, width // 2
    v = ref[n - 2 * rows : n - rows, :half].astype(F32) + ref[n - rows :, :half].astype(F32)
    return jnp.concatenate([v[:8], v[8:]], axis=1)


def grads_second_kernel(place, a_keep, a_recv, b_keep, b_recv, s0, s1, s2, kept):
    core = place[1] & 1
    half, n, third = a_keep.shape[1], kept.shape[0] // 2, s0.shape[1]
    for j, sent in enumerate((s0, s1, s2)):
        for keep, recv, low, high in (
            (a_keep, a_recv, j * third, min((j + 1) * third, half)),
            (b_keep, b_recv, max(j * third, half) - half, (j + 1) * third - half),
        ):
            if low >= high:
                continue
            at = low + (half if keep is b_keep else 0)
            from_, to = slice(low, high), slice(at - j * third, at - j * third + high - low)
            for i in range(2):
                rows = pl.ds(pl.multiple_of(2 * i * n, 2 * n), 2 * n)
                out = slice(i * n, (i + 1) * n)
                halve_rows(
                    core, keep.at[rows, from_], recv.at[rows, from_],
                    sent.at[out, to], kept.at[out, at : at + high - low],
                )


def grads_third_kernel(place, keep, r0, r1, r2, a_sent, a_kept, b_sent, b_kept):
    x, y = (place[1] >> 1) & 1, (place[1] >> 2) & 1
    half, third = a_kept.shape[1], r0.shape[1]
    for j, recv in enumerate((r0, r1, r2)):
        low, high = j * third, (j + 1) * third
        for bit, sent, kept, first, start, stop in (
            (y, a_sent, a_kept, 0, low, min(high, half)),
            (x, b_sent, b_kept, half, max(low, half), high),
        ):
            if start >= stop:
                continue
            out = slice(start - first, stop - first)
            halve_rows(
                bit, keep.at[:, start:stop], recv.at[:, start - low : stop - low],
                sent.at[:, out], kept.at[:, out],
            )


def halve_rows(bit, keep, recv, sent, kept):
    n = kept.shape[0]
    for ref, b in ((sent, 1 - bit), (kept, bit)):
        rows = pl.ds(pl.multiple_of(b * n, n), n)
        total = keep[rows, :].astype(F32) + recv[rows, :].astype(F32)
        ref[0:n, :] = total.astype(ref.dtype)


def qkv_second_kernel(place, vec, keep, recv, sent, kept, vec_o):
    x = (place[1] >> 1) & 1
    n = kept.shape[0] // 2
    for i in range(2):
        for ref, b in ((sent, 1 - x), (kept, x)):
            rows = pl.ds(pl.multiple_of((2 * i + b) * n, n), n)
            total = keep[rows, :].astype(F32) + recv[rows, :].astype(F32)
            ref[i * n : (i + 1) * n, :] = total.astype(ref.dtype)
    vec_o[...] = vec[...] + get_vec(recv, vec.shape[1])
    put_vec(vec_o[...], sent)


def qkv_third_kernel(place, vec, keep, recv, sent, kept, vec_o):
    halve_rows((place[1] >> 2) & 1, keep, recv, sent, kept)
    vec_o[...] = vec[...] + get_vec(recv, vec.shape[1])
    put_vec(vec_o[...], sent)


def message_kernel(place, vec, b_keep, b_recv, q_recv, vec_o, o0, o1, o2, o3, turned):
    m = place[0]
    channels = o0.shape[0]
    width, share = turned.shape
    cols = slice(b_keep.shape[1] - width, b_keep.shape[1])
    turned[...] = (b_keep[:, cols] + b_recv[:, cols].astype(F32)).T
    v = vec[...] + get_vec(q_recv, vec.shape[1])
    vec_o[...] = v
    tiles = v.shape[1] // 128
    high = v.astype(BF16)
    low = (v - high.astype(F32)).astype(BF16)
    both = jnp.concatenate([high.astype(F32), low.astype(F32)]).astype(BF16)
    for k, ref in enumerate((o0, o1, o2, o3)):
        t = turned[pl.ds(pl.multiple_of((m ^ k) * channels, channels), channels), :]
        ref[0:channels, 0:share] = t.astype(ref.dtype)
        if k:
            for i in range(tiles):
                at = channels + 16 * i
                ref[at : at + 16, :] = both[:, 128 * i : 128 * (i + 1)]


def last_kernel(a_keep, a_recv, b_keep, b_recv, q_keep, q_recv, up_o, down_o, qkv_o):
    hidden = up_o.shape[1]
    channels = qkv_o.shape[2]
    a = a_keep[...] + a_recv[...].astype(F32)
    share, half = a.shape
    rest = slice(0, 2 * hidden - half)
    up_o[...] = a[:, :hidden]
    down_o[:, : half - hidden] = a[:, hidden:]
    down_o[:, half - hidden :] = b_keep[:, rest] + b_recv[:, rest].astype(F32)
    q = q_keep[...] + q_recv[0:share, :].astype(F32)
    for i in range(3):
        qkv_o[i] = q[:, i * channels : (i + 1) * channels]


def small_kernel(vec, o0, o1, o2, o3, out, gains, biases, scales, table):
    channels, share = out.shape
    others = (o1, o2, o3)
    total = o0[...]
    v = vec[...]
    for ref in others:
        total = total + ref[0:channels, 0:share].astype(F32)
        parts = []
        for i in range(v.shape[1] // 128):
            at = channels + 16 * i
            both = ref[at : at + 16, :].astype(F32)
            parts.append(both[:8] + both[8:])
        v = v + jnp.concatenate(parts, axis=1)
    out[...] = total
    gains[...] = v[0:2]
    biases[...] = v[2:4]
    scales[...] = v[4:6]
    n = table.shape[1]
    for h in range(table.shape[0]):
        table[h : h + 1, :] = v[6:7, h * n : (h + 1) * n]


def input_kernel(own, recv, dy, out):
    total = own[...] + recv[...].astype(F32)
    out[...] = (dy[...].astype(F32) + total.T).astype(BF16)


def output_kernel(own, recv, mid, cols, out):
    total = own[...] + recv[...].astype(F32)
    out[...] = (mid[...] + cols[:, SCALE1 : SCALE1 + 1] * total).T.astype(BF16)


def body(
    tokens,
    page_lengths,
    norm_gains,
    norm_biases,
    layer_scales,
    w_qkv,
    rel_table,
    w_out,
    w_up,
    w_down,
    cotangent,
):
    mp, dp = lax.axis_size("mp"), lax.axis_size("dp")
    rows, width = tokens.shape
    group = rows * mp
    channels = w_qkv.shape[2]
    hidden = w_up.shape[1]
    heads = channels // HEAD_DIM
    buckets = rel_table.shape[0]
    m, d = lax.axis_index("mp"), lax.axis_index("dp")
    place = jnp.stack([m, d]).astype(jnp.int32)

    def swap(v, k, axis="mp", name="rows"):
        n = mp if axis == "mp" else dp
        with jax.named_scope(name):
            return lax.ppermute(v, axis, [(i, i ^ k) for i in range(n)])

    def after(v, *seen):
        return lax.optimization_barrier((v,) + seen)[0]

    fast = dp == 8 and (width // dp) % 16 == 0 and hidden == width

    cols = jnp.concatenate(
        [norm_gains[0:1], norm_biases[0:1], norm_gains[1:2], norm_biases[1:2], layer_scales]
    ).T
    wq = jnp.transpose(w_qkv, (1, 2, 0)).reshape(3 * channels, width)

    piece = channels // 4
    sent = jnp.concatenate([tokens, lax.dynamic_slice_in_dim(w_out, (d & 3) * piece, piece, 0)])
    x1, x2 = swap(sent, 1, name="x"), swap(sent, 2, name="x")
    wq_t, w_up_t, w_down_t = call(
        turn_kernel,
        [like((width, 3 * channels), BF16), like((hidden, width), BF16), like((width, hidden), BF16)],
        [wq, w_up, w_down],
    )
    pattern, ids = call(
        bias_kernel,
        [like((heads, 3, 128, 128), F32), like((group, 128), jnp.int32)],
        [place, page_lengths, rel_table],
        n_smem=3,
    )
    x = [sent, x1, x2, swap(after(x2, x1, wq_t, pattern, cols), 1, name="x")]
    dy2 = swap(after(cotangent, *x[1:]), 2, name="dy")
    dy1 = swap(after(cotangent, *x[1:]), 1, name="dy")
    x[1:] = lax.optimization_barrier((x[1:], wq_t, pattern))[0]
    (part,) = call(pieces_kernel, [like((4, piece, width), BF16)], x)
    part_x = swap(part, 2, "dp", name="w")
    wq_now = after(wq, wq_t, w_up_t, w_down_t)
    xt, h1, stat, qkv, pt, att, att_top, att_low = call(
        head_kernel,
        [
            like((width, group), BF16),
            like((width, group), BF16),
            like((8, group), F32),
            like((3 * channels, group), BF16),
            like((heads, group, group), BF16),
            like((channels, group), BF16),
            like((channels // 2, group), BF16),
            like((channels // 2, group), BF16),
        ],
        [place, page_lengths, rel_table] + x + [pattern, ids, cols, wq_now],
        n_smem=3,
        scratch=[
            pltpu.VMEM((heads, group, group), F32),
        ],
        limit=24,
        us=10,
    )
    (parts,) = call(
        pair_kernel, [like((8, piece, width), BF16)], [part, after(part_x, att, dy1, dy2)]
    )
    att_top, att_low, att_sent = after(att_top, parts), after(att_low, parts), after(att, parts)
    a2t, a2b = swap(att_top, 2, name="att"), swap(att_low, 2, name="att")
    a3b, a1 = swap(att_low, 3, name="att"), swap(att_sent, 1, name="att")
    atts = [att, a1, a2t, a2b, swap(a2t, 1, name="att"), a3b]
    dy = [cotangent, dy1, dy2, swap(after(dy2, parts), 1, name="dy")]
    w_pieces = [parts, swap(parts, 1, "dp", name="w")]
    w_out_full, w_out_t = call(
        out_weight_kernel, [like((width, width), BF16)] * 2, [place] + w_pieces, n_smem=1
    )
    act_like = like((width, group), BF16)
    hid_like = like((hidden, group), BF16)
    wide_like = like((width, group), F32)
    block = like((width, rows), F32)
    blocks = [block, block, like((2 * width, rows), BF16)]
    att_all, attn, hat, rstd, h2, act, slope, mid, mlp_part, m0, m2, m13 = call(
        up_kernel,
        [act_like, wide_like, wide_like, like((8, group), F32), act_like, hid_like]
        + [like((hidden, group), F32), block, wide_like]
        + blocks,
        [place] + atts + [after(xt, dy1), cols, w_out_t, w_up_t, w_down_t],
        n_smem=1,
        scratch=[pltpu.VMEM((hidden, group), F32)],
        us=10,
    )
    m_recv = swap(m13, 1, name="mlp")
    d0, d1, d2, d3, nb, dup, gm, ga, dy_t, vec = call(
        down_kernel,
        [like((channels, group), BF16)] * 4
        + [wide_like, hid_like, act_like, act_like, act_like, like((8, width), F32)],
        [place] + dy + [cols, attn, hat, rstd, slope, w_out_full, w_up, w_down],
        n_smem=1,
        scratch=[pltpu.VMEM((max(width, hidden), group), F32), pltpu.VMEM((width, 128), F32)],
        us=10,
    )
    d_att = [d0] + [swap(v, k, name="d_att") for k, v in ((1, d1), (2, d2), (3, d3))]
    grad_cols = 2 * hidden + width
    share = width // dp
    half = grad_cols // 2
    if fast:
        grad_like = [like((width // 2, half), BF16)] * 4
    else:
        grad_like = [like((width, grad_cols), BF16)]
    vec, *grads = call(
        mlp_grad_kernel,
        [like((8, width), F32)] + grad_like,
        [place, vec, mlp_part, act, dup, gm, ga, att_all, h2, dy_t],
        n_smem=1,
        scratch=[pltpu.VMEM((width, 128), F32)],
    )
    if fast:
        a_sent, a_kept, b_sent, b_kept = grads
        a_recv = swap(a_sent, 2, "dp", name="grads_a")
        b_recv = swap(b_sent, 4, "dp", name="grads_b")

    def halved(own, next_to, recv, name, us=0.01, seen=()):
        half_like = [block, like((width, rows), BF16)]
        own, sent = call(halve_kernel, half_like, [own, next_to, recv], us=us)
        return [own, swap(after(sent, *seen), 2, name=name)]

    mlp = halved(m0, m2, m_recv, "mlp", seen=d_att[1:])

    n = 3 * channels
    extra = 4 * vec.shape[0]
    if fast:
        grad_like = [like((width // 2 + extra, n), BF16), like((width // 2, n), BF16)]
    else:
        grad_like = [like((width, n), BF16)]
    p0, p2, p13, vec, *qkv_grads = call(
        back_kernel,
        blocks + [like((8, width), F32)] + grad_like,
        [place, page_lengths] + d_att + [qkv, pt, xt, h1, stat, nb, cols, wq_t, vec],
        n_smem=2,
        scratch=[
            pltpu.VMEM((n, group), BF16),
            pltpu.VMEM((heads, group, group), F32),
            pltpu.VMEM((heads, group, group), BF16),
            pltpu.VMEM((heads, 5, 128, 128), F32),
            pltpu.VMEM((heads * buckets, 128), F32),
            pltpu.VMEM((width, group), F32),
            pltpu.VMEM((width, 128), F32),
        ],
        limit=24,
        us=10,
    )
    p_recv = swap(p13, 1, name="back")
    back = halved(p0, p2, p_recv, "back", us=10)

    def reduced(g):
        g = g.reshape(dp, width // dp, g.shape[1])
        bit = 1
        while bit < dp:
            g = g.reshape(g.shape[0] // 2, 2, width // dp, g.shape[-1])
            here = (d & bit) // bit
            sent = lax.dynamic_index_in_dim(g, 1 - here, 1, keepdims=False)
            kept = lax.dynamic_index_in_dim(g, here, 1, keepdims=False)
            g = kept.astype(F32) + swap(sent, bit, "dp").astype(F32)
            bit *= 2
            if bit < dp:
                g = g.astype(BF16)
        return g[0]

    if fast:
        q_recv = swap(after(qkv_grads[0], mlp[1]), 1, "dp", name="qkv_core")
        vec_like = [like(vec.shape, F32)]
        sent, kept, vec = call(
            qkv_second_kernel,
            [like((2 * share + extra, n), BF16), like((2 * share, n), F32)] + vec_like,
            [place, vec, qkv_grads[1], q_recv],
            n_smem=1,
        )
        recv = swap(sent, 2, "dp", name="qkv_x")
        g0, g1, g2, g_kept = call(
            grads_second_kernel,
            [like((2 * share, grad_cols // 3), BF16)] * 3 + [like((2 * share, grad_cols), BF16)],
            [place, after(a_kept, vec), a_recv, b_kept, b_recv],
            n_smem=1,
        )
        g_recv = [swap(g, 1, "dp", name="grads_core") for g in (g0, g1, g2)]
        a_sent, a_kept, b_sent, b_kept = call(
            grads_third_kernel,
            [like((share, half), BF16), like((share, half), F32)] * 2,
            [place, g_kept] + g_recv,
            n_smem=1,
        )
        a_recv = swap(a_sent, 4, "dp", name="grads_a")
        b_recv = swap(b_sent, 2, "dp", name="grads_b")
        sent, kept, vec = call(
            qkv_third_kernel,
            [like((share + extra, n), BF16), like((share, n), F32)] + vec_like,
            [place, after(vec, a_kept, back[0]), kept, recv],
            n_smem=1,
        )
        recv = swap(sent, 4, "dp", name="qkv_y")
        message = like((channels + 2 * vec.size // 128, 128), BF16)
        vec, o0, o1, o2, o3 = call(
            message_kernel,
            vec_like + [like((channels, share), F32)] + [message] * 3,
            [place, after(vec, a_recv), b_kept, b_recv, recv],
            n_smem=1,
            scratch=[pltpu.VMEM((width, share), F32)],
        )
        grad_up, grad_down, grad_qkv = call(
            last_kernel,
            [like((share, hidden), F32)] * 2 + [like((3, share, channels), F32)],
            [a_kept, a_recv, b_kept, b_recv, after(kept, o1), recv],
        )
        o1, o2, o3 = (swap(v, k, name="out") for k, v in ((1, o1), (2, o2), (3, o3)))
        grad_out, gains, biases, scales, grad_table = call(
            small_kernel,
            [like((channels, share), F32)]
            + [like((2, width), F32)] * 3
            + [like((heads * mp, buckets), F32)],
            [vec, o0, o1, o2, o3],
        )
        grad_qkv = jnp.transpose(grad_qkv, (1, 0, 2))
    else:
        summed = reduced(grads[0])
        grad_qkv = reduced(qkv_grads[0]).reshape(share, 3, channels)
        grad_up, grad_down = summed[:, :hidden], summed[:, hidden : 2 * hidden]
        turned = summed[:, 2 * hidden :].T

        def out_part(k):
            return lax.dynamic_slice_in_dim(turned, (m ^ k) * channels, channels, 0)

        grad_out = out_part(0)
        for k in range(1, mp):
            grad_out = grad_out + swap(out_part(k).astype(BF16), k).astype(F32)
        bit = 1
        while bit < dp:
            vec = vec + swap(vec, bit, "dp", name="vec")
            bit *= 2
        for k in (1, 2):
            vec = vec + swap(vec, k, name="vec")
        gains, biases, scales = vec[0:2], vec[2:4], vec[4:6]
        grad_table = vec[6, : heads * mp * buckets].reshape(heads * mp, buckets)

    (output,) = call(output_kernel, [like((rows, width), BF16)], mlp + [mid, cols])
    (grad_input,) = call(input_kernel, [like((rows, width), BF16)], back + [cotangent], us=10)
    return (
        output,
        grad_input,
        gains,
        biases,
        scales,
        grad_qkv,
        grad_table.T,
        grad_out,
        grad_up,
        grad_down.T,
    )


def solution(mesh):
    placed = (
        P(("dp", "mp"), None),
        P("dp", None),
        P(),
        P(),
        P(),
        P(None, None, "mp"),
        P(),
        P("mp", None),
        P(None, "mp"),
        P("mp", None),
        P(("dp", "mp"), None),
    )
    return jax.shard_map(
        body,
        mesh=mesh,
        in_specs=placed,
        out_specs=(
            P(("dp", "mp"), None),
            P(("dp", "mp"), None),
            P(),
            P(),
            P(),
            P("dp", None, "mp"),
            P(),
            P("mp", "dp"),
            P("dp", "mp"),
            P("mp", "dp"),
        ),
        check_vma=False,
    )
```

```python
import jax
import jax.numpy as jnp
from jax import lax
from jax.experimental import pallas as pl
from jax.experimental.pallas import tpu as pltpu
from jax.sharding import PartitionSpec as P

HEAD_DIM = 64
SPEED = 1.15e9
norm_eps = 1e-06
masked_score = -1000000000.0
F32 = jnp.float32
BF16 = jnp.bfloat16
SMEM = pl.BlockSpec(memory_space=pltpu.SMEM)
VMEM = pl.BlockSpec(memory_space=pltpu.VMEM)
CHUNK = 64
GAIN0, BIAS0, GAIN1, BIAS1, SCALE0, SCALE1 = range(6)


def call(kernel, outs, args, n_smem=0, scratch=(), us=0.01, limit=8):
    return pl.pallas_call(
        kernel,
        out_shape=tuple(outs),
        in_specs=[SMEM] * n_smem + [VMEM] * (len(args) - n_smem),
        out_specs=tuple([VMEM] * len(outs)),
        scratch_shapes=list(scratch),
        compiler_params=pltpu.CompilerParams(vmem_limit_bytes=limit << 20),
        name=kernel.__name__,
        cost_estimate=pl.CostEstimate(flops=int(us * SPEED), bytes_accessed=8, transcendentals=0),
    )(*args)


def like(shape, dtype):
    return jax.ShapeDtypeStruct(shape, dtype)


def nn(a, b):
    return lax.dot_general(a, b, (((1,), (0,)), ((), ())), preferred_element_type=F32)


def nt(a, b):
    return lax.dot_general(a, b, (((1,), (1,)), ((), ())), preferred_element_type=F32)


def fold(v):
    return jnp.sum(v.reshape(v.shape[0] // 8, 8, v.shape[1]), axis=0)


def across(v):
    return jnp.sum(v, axis=0, keepdims=True)


def passes(rows, step, start):
    return lax.fori_loop(0, rows // CHUNK, step, start, unroll=True)


def chunk(i):
    return pl.ds(pl.multiple_of(i * CHUNK, CHUNK), CHUNK)


def page_ids(lengths, shape, axis, dead):
    at = lax.broadcasted_iota(jnp.int32, shape, axis)
    page = jnp.zeros(shape, jnp.int32)
    end = jnp.int32(0)
    pages = lengths.shape[1]
    for p in range(pages):
        end = end + lengths[0, p]
        page = page + (at >= end).astype(jnp.int32)
    return jnp.where(page < pages - 1, page, dead)


def turn_kernel(wq, wu, wd, wq_o, wu_o, wd_o):
    wq_o[...] = wq[...].T
    wu_o[...] = wu[...].T
    wd_o[...] = wd[...].T


def pieces_kernel(x0, x1, x2, x3, out):
    n = out.shape[1]
    for k, ref in enumerate((x0, x1, x2, x3)):
        out[k] = ref[ref.shape[0] - n :, :]


def pair_kernel(a, b, out):
    out[0:4] = a[...]
    out[4:8] = b[...]


def out_weight_kernel(place, here, there, w_o, wt_o):
    m, d = place[0], place[1]
    rows = here.shape[1]
    for c, ref in enumerate((here, there)):
        for b in range(2):
            part = (d & 3) ^ (c + 2 * b)
            for k in range(4):
                at = pl.multiple_of((m ^ k) * 4 * rows + part * rows, rows)
                w_o[pl.ds(at, rows), :] = ref[4 * b + k]
    wt_o[...] = w_o[...].T


def bias_kernel(place, lengths, table, pattern, ids):
    buckets = table.shape[0]
    half = buckets // 2
    heads, _, blk, _ = pattern.shape
    ids[...] = page_ids(lengths, ids.shape, 0, -2)
    off = lax.broadcasted_iota(jnp.int32, (blk, blk), 1) - lax.broadcasted_iota(
        jnp.int32, (blk, blk), 0
    )
    for h in range(heads):
        col = place[0] * heads + h
        low, high = table[0, col], table[buckets - 1, col]
        near = jnp.where(off >= half - 1, high, low)
        for b in range(1, buckets - 1):
            near = jnp.where(off == b - half, table[b, col], near)
        before = jnp.full((blk, blk), low, F32)
        for b in range(1, half):
            before = jnp.where(off - blk == b - half, table[b, col], before)
        after = jnp.full((blk, blk), high, F32)
        for b in range(half + 1, buckets - 1):
            after = jnp.where(off + blk == b - half, table[b, col], after)
        pattern[h, 0], pattern[h, 1], pattern[h, 2] = before, near, after


def head_kernel(
    place, lengths, table, x0, x1, x2, x3, pattern, ids, cols, wq,
    xt_o, h1_o, stat_o, qkv_o, pt_o, att_o, top_o, low_o,
    score,
):
    m = place[0]
    width, tokens = xt_o.shape
    rows = tokens // 4
    channels = att_o.shape[0]
    heads = channels // HEAD_DIM
    buckets = table.shape[0]
    for k, ref in enumerate((x0, x1, x2, x3)):
        at = pl.multiple_of((m ^ k) * rows, rows)
        xt_o[:, pl.ds(at, rows)] = ref[0:rows, :].T

    def add(i, acc):
        return acc + fold(xt_o[chunk(i), :].astype(F32))

    zero = jnp.zeros((8, tokens), F32)
    mean = across(passes(width, add, zero)) / width

    def spread(i, acc):
        v = xt_o[chunk(i), :].astype(F32) - mean
        return acc + fold(v * v)

    rstd = lax.rsqrt(across(passes(width, spread, zero)) / width + norm_eps)
    stat_o[0:1, :] = mean
    stat_o[1:2, :] = rstd

    def norm(i, carry):
        v = (xt_o[chunk(i), :].astype(F32) - mean) * rstd
        w = cols[chunk(i), :]
        h1_o[chunk(i), :] = (v * w[:, GAIN0 : GAIN0 + 1] + w[:, BIAS0 : BIAS0 + 1]).astype(BF16)
        return carry

    passes(width, norm, 0)
    qkv_o[...] = nn(wq[...], h1_o[...]).astype(BF16)
    qkv_o[0:channels, :] = qkv_o[0:channels, :] * BF16(HEAD_DIM**-0.5)

    own_ids = page_ids(lengths, (1, tokens), 1, -1)
    live = (own_ids >= 0).astype(F32)
    blk = 128
    n_blk = tokens // blk

    def one_head(h):
        col = m * heads + h
        low, high = table[0, col], table[buckets - 1, col]

        def rows_of(which):
            return pl.ds(which * channels + h * HEAD_DIM, HEAD_DIM)

        q, k, v = qkv_o[rows_of(0), :], qkv_o[rows_of(1), :], qkv_o[rows_of(2), :]
        score[h] = nn(k.T, q)
        for i in range(n_blk):
            lanes = slice(i * blk, (i + 1) * blk)
            query_id = own_ids[:, lanes]
            top = jnp.full((8, blk), -3e38, F32)
            for j in range(n_blk):
                at = slice(j * blk, (j + 1) * blk)
                if abs(i - j) <= 1:
                    bias = pattern[h, i - j + 1]
                else:
                    bias = low if i < j else high
                s = jnp.where(ids[at, :] == query_id, score[h, at, lanes] + bias, masked_score)
                score[h, at, lanes] = s
                top = jnp.maximum(top, jnp.max(s.reshape(blk // 8, 8, blk), axis=0))
            top = jnp.max(top, axis=0, keepdims=True)
            total = jnp.zeros((8, blk), F32)
            for j in range(n_blk):
                at = slice(j * blk, (j + 1) * blk)
                e = jnp.exp(score[h, at, lanes] - top)
                score[h, at, lanes] = e
                total = total + fold(e)
            scale = 1.0 / across(total)
            for j in range(n_blk):
                at = slice(j * blk, (j + 1) * blk)
                pt_o[h, at, lanes] = (score[h, at, lanes] * scale).astype(BF16)
        mixed = nn(v, pt_o[h]) * live
        att_o[h * HEAD_DIM : (h + 1) * HEAD_DIM, :] = mixed.astype(BF16)

    for h in range(heads):
        one_head(h)
    half_rows = channels // 2
    top_o[...], low_o[...] = att_o[0:half_rows, :], att_o[half_rows:, :]


def up_kernel(
    place, a0, a1, a2t, a2b, a3t, a3b, xt, cols, w_out_t, w_up_t, w_down_t,
    at_o, attn_o, hat_o, rstd_o, h2_o, act_o, slope_o, mid_o, mlp_o, m0, m2, m13,
    wide,
):
    m = place[0]
    rows = mid_o.shape[1]
    channels = a0.shape[0]
    width, tokens = xt.shape
    hidden = act_o.shape[0]
    top = channels // 2
    for k, first, a in ((0, 0, a0), (1, 0, a1), (2, 0, a2t), (2, top, a2b), (3, 0, a3t), (3, top, a3b)):
        at = pl.multiple_of((m ^ k) * channels + first, top)
        at_o[pl.ds(at, a.shape[0]), :] = a[...]
    attn_o[...] = nn(w_out_t[...], at_o[...])
    zero = jnp.zeros((8, tokens), F32)

    def residual(i, acc):
        scale = cols[chunk(i), :][:, SCALE0 : SCALE0 + 1]
        v = xt[chunk(i), :].astype(F32) + scale * attn_o[chunk(i), :]
        hat_o[chunk(i), :] = v
        return acc + fold(v)

    mean = across(passes(width, residual, zero)) / width
    mid_o[...] = hat_o[:, pl.ds(pl.multiple_of(m * rows, rows), rows)]

    def spread(i, acc):
        v = hat_o[chunk(i), :] - mean
        return acc + fold(v * v)

    rstd = lax.rsqrt(across(passes(width, spread, zero)) / width + norm_eps)
    rstd_o[0:1, :] = rstd

    def norm(i, carry):
        w = cols[chunk(i), :]
        v = (hat_o[chunk(i), :] - mean) * rstd
        hat_o[chunk(i), :] = v
        h2_o[chunk(i), :] = (v * w[:, GAIN1 : GAIN1 + 1] + w[:, BIAS1 : BIAS1 + 1]).astype(BF16)
        return carry

    passes(width, norm, 0)
    wide[...] = nn(w_up_t[...], h2_o[...])

    def gelu(i, carry):
        u = wide[chunk(i), :]
        cdf = 0.5 + 0.5 * lax.erf(u * (0.5**0.5))
        act_o[chunk(i), :] = (u * cdf).astype(BF16)
        slope_o[chunk(i), :] = cdf + u * (jnp.exp(-0.5 * u * u) * 0.3989422804014327)
        return carry

    passes(hidden, gelu, 0)
    mlp_o[...] = nn(w_down_t[...], act_o[...])
    put_halves(m, mlp_o, m0, m2, m13)


def down_kernel(
    place, c0, c1, c2, c3, cols, attn, hat, rstd, slope, w_out, w_up, w_down,
    d0, d1, d2, d3, nb_o, dup_o, gm_o, ga_o, dy_o, vec_o,
    wide, sums,
):
    m = place[0]
    rows = c0.shape[0]
    channels = d0.shape[0]
    width, tokens = hat.shape
    hidden = slope.shape[0]
    for k, c in enumerate((c0, c1, c2, c3)):
        at = pl.ds(pl.multiple_of((m ^ k) * rows, rows), rows)
        turned = c[...].T
        dy_o[:, at] = turned
        scale = cols[:, SCALE1 : SCALE1 + 1]
        gm_o[:, at] = (turned.astype(F32) * scale).astype(BF16)
    wide[...] = nn(w_down[...], gm_o[...])

    def d_up(i, carry):
        dup_o[chunk(i), :] = (slope[chunk(i), :] * wide[chunk(i), :]).astype(BF16)
        return carry

    passes(hidden, d_up, 0)
    wide[...] = nn(w_up[...], dup_o[...])
    zero = jnp.zeros((8, tokens), F32)

    def gather(i, acc):
        d = wide[chunk(i), :]
        u = d * cols[chunk(i), :][:, GAIN1 : GAIN1 + 1]
        return acc[0] + fold(u), acc[1] + fold(u * hat[chunk(i), :])

    first, second = passes(width, gather, (zero, zero))
    first, second = across(first) / width, across(second) / width
    lane = lax.broadcasted_iota(jnp.int32, (1, tokens), 1)
    mine = ((lane >= m * rows) & (lane < (m + 1) * rows)).astype(F32)
    rstd = rstd[0:1, :]

    def back(i, carry):
        w = cols[chunk(i), :]
        d = wide[chunk(i), :]
        h = hat[chunk(i), :]
        v = rstd * (d * w[:, GAIN1 : GAIN1 + 1] - first - h * second)
        nb_o[chunk(i), :] = v
        v = v + mine * dy_o[chunk(i), :].astype(F32)
        ga_o[chunk(i), :] = (v * w[:, SCALE0 : SCALE0 + 1]).astype(BF16)
        sums[chunk(i), 0:1] = jnp.sum(d * h, axis=1, keepdims=True)
        sums[chunk(i), 1:2] = jnp.sum(d, axis=1, keepdims=True)
        sums[chunk(i), 2:3] = jnp.sum(v * attn[chunk(i), :], axis=1, keepdims=True)
        return carry

    passes(width, back, 0)
    wide[...] = nn(w_out[...], ga_o[...])
    for k, ref in enumerate((d0, d1, d2, d3)):
        at = pl.ds(pl.multiple_of((m ^ k) * channels, channels), channels)
        ref[...] = wide[at, :].astype(BF16)
    turned = sums[...].T
    vec_o[...] = jnp.zeros(vec_o.shape, F32)
    vec_o[1:2, :] = turned[0:1, :]
    vec_o[3:4, :] = turned[1:2, :]
    vec_o[4:5, :] = turned[2:3, :]


def mlp_grad_kernel(place, vec, mlp, act, dup, gm, ga, att, h2, dy, vec_o, *rest):
    grads, sums = rest[:-1], rest[-1]

    def scale(i, carry):
        v = dy[chunk(i), :].astype(F32) * mlp[chunk(i), :]
        sums[chunk(i), 0:1] = jnp.sum(v, axis=1, keepdims=True)
        return carry

    passes(dy.shape[0], scale, 0)
    vec_o[...] = vec[...]
    vec_o[5:6, :] = sums[...].T[0:1, :]
    if len(grads) == 1:
        at = 0
        for a, b in ((h2, dup), (gm, act), (ga, att)):
            grads[0][:, at : at + b.shape[0]] = nt(a[...], b[...]).astype(BF16)
            at += b.shape[0]
        return
    x, y = (place[1] >> 1) & 1, (place[1] >> 2) & 1
    a_sent, a_kept, b_sent, b_kept = grads
    n, half = a_sent.shape[0] // 4, a_sent.shape[1]

    def put(p, left, low, high):
        block = [p[i * n : (i + 1) * n, low:high] for i in range(8)]
        first = left + low < half
        at = left + low - (0 if first else half)
        cols = slice(at, at + high - low)
        for i in range(4):
            out = slice(i * n, (i + 1) * n)
            if first:
                zero, one = 4 * (i // 2) + i % 2, 4 * (i // 2) + 2 + i % 2
                a_sent[out, cols] = pick(x, block[one], block[zero])
                a_kept[out, cols] = pick(x, block[zero], block[one])
            else:
                b_sent[out, cols] = pick(y, block[4 + i], block[i])
                b_kept[out, cols] = pick(y, block[i], block[4 + i])

    left = 0
    for a, b in ((h2, dup), (gm, act), (ga, att)):
        p = nt(a[...], b[...]).astype(BF16)
        n_cols = p.shape[1]
        cut = min(max(half - left, 0), n_cols)
        if cut > 0:
            put(p, left, 0, cut)
        if cut < n_cols:
            put(p, left, cut, n_cols)
        left += n_cols


def put_halves(m, ref, own, next_to, sent):
    rows, width = own.shape[1], own.shape[0]

    def of(k):
        return ref[:, pl.ds(pl.multiple_of((m ^ k) * rows, rows), rows)]

    own[...], next_to[...] = of(0), of(2)
    sent[0:width, :] = of(1).astype(BF16)
    sent[width:, :] = of(3).astype(BF16)


def halve_kernel(own, next_to, recv, own_o, sent):
    width = own.shape[0]
    own_o[...] = own[...] + recv[0:width, :].astype(F32)
    sent[...] = (next_to[...] + recv[width:, :].astype(F32)).astype(BF16)


def put_blocks(parts, here, grads):
    at = 0
    for p in parts:
        cols = slice(at, at + p.shape[1])
        at += p.shape[1]
        if len(grads) == 1:
            grads[0][:, cols] = p
            continue
        sent, kept = grads
        n = kept.shape[0] // 4
        for b in range(4):
            even, odd = p[2 * b * n : (2 * b + 1) * n], p[(2 * b + 1) * n : (2 * b + 2) * n]
            sent[b * n : (b + 1) * n, cols] = pick(here, odd, even)
            kept[b * n : (b + 1) * n, cols] = pick(here, even, odd)


def pick(bit, a, b):
    return jnp.where(bit == 0, a, b)


def back_kernel(
    place, lengths, d0, d1, d2, d3, qkv, pt, xt, h1, stat, nb, cols, wq_t, vec,
    p0, p2, p13, vec_o, *rest,
):
    grads, (dqkv_o, score, ds, acc, buckets_of, wide, sums) = rest[:-7], rest[-7:]
    m = place[0]
    channels, tokens = d0.shape
    heads = channels // HEAD_DIM
    width = xt.shape[0]
    rows = p0.shape[1]
    blk = 128
    n_blk = tokens // blk
    n_rows = buckets_of.shape[0]
    buckets = n_rows // heads
    half = buckets // 2
    live = (page_ids(lengths, (1, tokens), 1, -1) >= 0).astype(F32)
    off = lax.broadcasted_iota(jnp.int32, (blk, blk), 1) - lax.broadcasted_iota(
        jnp.int32, (blk, blk), 0
    )

    def one_head(h):
        def rows_of(which):
            return pl.ds(which * channels + h * HEAD_DIM, HEAD_DIM)

        q, k, v = qkv[rows_of(0), :], qkv[rows_of(1), :], qkv[rows_of(2), :]
        mine = rows_of(0)
        d_att = (
            d0[mine, :].astype(F32) + d1[mine, :].astype(F32)
            + d2[mine, :].astype(F32) + d3[mine, :].astype(F32)
        )
        d_att = (d_att.astype(BF16).astype(F32) * live).astype(BF16)
        dqkv_o[rows_of(2), :] = nt(d_att, pt[h]).astype(BF16)
        score[h] = nn(v.T, d_att)
        acc[h] = jnp.zeros(acc.shape[1:], F32)
        for i in range(n_blk):
            lanes = slice(i * blk, (i + 1) * blk)
            total = jnp.zeros((8, blk), F32)
            for j in range(n_blk):
                at = slice(j * blk, (j + 1) * blk)
                prod = score[h, at, lanes] * pt[h, at, lanes].astype(F32)
                score[h, at, lanes] = prod
                total = total + fold(prod)
            total = across(total)
            for j in range(n_blk):
                at = slice(j * blk, (j + 1) * blk)
                g = score[h, at, lanes] - pt[h, at, lanes].astype(F32) * total
                g = g.astype(BF16)
                ds[h, at, lanes] = g
                slot = max(min(i - j, 2), -2) + 2
                acc[h, slot] = acc[h, slot] + g.astype(F32)
        dqkv_o[rows_of(0), :] = (nn(k, ds[h]) * HEAD_DIM**-0.5).astype(BF16)
        dqkv_o[rows_of(1), :] = nt(q, ds[h]).astype(BF16)
        near, before, after = acc[h, 2], acc[h, 1], acc[h, 3]
        corner_b, off_b = before[0:16, :], off[0:16, :] - blk
        corner_a, off_a = after[blk - 16 : blk, :], off[blk - 16 : blk, :] + blk
        first = h * buckets
        for b in range(buckets):
            if b == 0:
                v = fold(acc[h, 0]) + fold(jnp.where(off - blk <= -half, before, 0.0))
                v = v + fold(jnp.where(off <= -half, near, 0.0))
            elif b == buckets - 1:
                v = fold(acc[h, 4]) + fold(jnp.where(off + blk >= half - 1, after, 0.0))
                v = v + fold(jnp.where(off >= half - 1, near, 0.0))
            else:
                v = fold(jnp.where(off == b - half, near, 0.0))
                if b < half:
                    v = v + fold(jnp.where(off_b == b - half, corner_b, 0.0))
                elif b > half:
                    v = v + fold(jnp.where(off_a == b - half, corner_a, 0.0))
            buckets_of[first + b : first + b + 1, :] = across(v)

    for h in range(heads):
        one_head(h)
    wide[...] = nn(wq_t[...], dqkv_o[...])
    weight_grad = nt(h1[...], dqkv_o[...]).astype(BF16)
    mean, rstd = stat[0:1, :], stat[1:2, :]
    zero = jnp.zeros((8, tokens), F32)

    def gather(i, part):
        d = wide[chunk(i), :]
        hat = (xt[chunk(i), :].astype(F32) - mean) * rstd
        u = d * cols[chunk(i), :][:, GAIN0 : GAIN0 + 1]
        sums[chunk(i), 0:1] = jnp.sum(d * hat, axis=1, keepdims=True)
        sums[chunk(i), 1:2] = jnp.sum(d, axis=1, keepdims=True)
        return part[0] + fold(u), part[1] + fold(u * hat)

    first, second = passes(width, gather, (zero, zero))
    first, second = across(first) / width, across(second) / width

    def back(i, carry):
        hat = (xt[chunk(i), :].astype(F32) - mean) * rstd
        u = wide[chunk(i), :] * cols[chunk(i), :][:, GAIN0 : GAIN0 + 1]
        wide[chunk(i), :] = nb[chunk(i), :] + rstd * (u - first - hat * second)
        return carry

    passes(width, back, 0)
    put_halves(m, wide, p0, p2, p13)
    turned = sums[...].T
    vec_o[...] = vec[...]
    vec_o[0:1, :] = turned[0:1, :]
    vec_o[2:3, :] = turned[1:2, :]
    each = jnp.sum(buckets_of[...], axis=1, keepdims=True)
    shape = (n_rows, width)
    lane = lax.broadcasted_iota(jnp.int32, shape, 1)
    row = lax.broadcasted_iota(jnp.int32, shape, 0)
    vec_o[6:7, :] = across(jnp.where(lane == row + m * n_rows, each, 0.0))
    put_blocks([weight_grad], place[1] & 1, grads)
    if len(grads) > 1:
        put_vec(vec_o[...], grads[0])


def put_vec(vec, ref):
    half = vec.shape[1] // 2
    v = jnp.concatenate([vec[:, :half], vec[:, half:]])
    high = v.astype(BF16)
    n, rows = ref.shape[0], v.shape[0]
    ref[n - 2 * rows : n - rows, :half] = high
    ref[n - rows :, :half] = (v - high.astype(F32)).astype(BF16)


def get_vec(ref, width):
    n, rows, half = ref.shape[0], 16, width // 2
    v = ref[n - 2 * rows : n - rows, :half].astype(F32) + ref[n - rows :, :half].astype(F32)
    return jnp.concatenate([v[:8], v[8:]], axis=1)


def grads_second_kernel(place, a_keep, a_recv, b_keep, b_recv, s0, s1, s2, kept):
    core = place[1] & 1
    half, n, third = a_keep.shape[1], kept.shape[0] // 2, s0.shape[1]
    for j, sent in enumerate((s0, s1, s2)):
        for keep, recv, low, high in (
            (a_keep, a_recv, j * third, min((j + 1) * third, half)),
            (b_keep, b_recv, max(j * third, half) - half, (j + 1) * third - half),
        ):
            if low >= high:
                continue
            at = low + (half if keep is b_keep else 0)
            from_, to = slice(low, high), slice(at - j * third, at - j * third + high - low)
            for i in range(2):
                rows = pl.ds(pl.multiple_of(2 * i * n, 2 * n), 2 * n)
                out = slice(i * n, (i + 1) * n)
                halve_rows(
                    core, keep.at[rows, from_], recv.at[rows, from_],
                    sent.at[out, to], kept.at[out, at : at + high - low],
                )


def grads_third_kernel(place, keep, r0, r1, r2, a_sent, a_kept, b_sent, b_kept):
    x, y = (place[1] >> 1) & 1, (place[1] >> 2) & 1
    half, third = a_kept.shape[1], r0.shape[1]
    for j, recv in enumerate((r0, r1, r2)):
        low, high = j * third, (j + 1) * third
        for bit, sent, kept, first, start, stop in (
            (y, a_sent, a_kept, 0, low, min(high, half)),
            (x, b_sent, b_kept, half, max(low, half), high),
        ):
            if start >= stop:
                continue
            out = slice(start - first, stop - first)
            halve_rows(
                bit, keep.at[:, start:stop], recv.at[:, start - low : stop - low],
                sent.at[:, out], kept.at[:, out],
            )


def halve_rows(bit, keep, recv, sent, kept):
    n = kept.shape[0]
    for ref, b in ((sent, 1 - bit), (kept, bit)):
        rows = pl.ds(pl.multiple_of(b * n, n), n)
        total = keep[rows, :].astype(F32) + recv[rows, :].astype(F32)
        ref[0:n, :] = total.astype(ref.dtype)


def qkv_second_kernel(place, vec, keep, recv, sent, kept, vec_o):
    x = (place[1] >> 1) & 1
    n = kept.shape[0] // 2
    for i in range(2):
        for ref, b in ((sent, 1 - x), (kept, x)):
            rows = pl.ds(pl.multiple_of((2 * i + b) * n, n), n)
            total = keep[rows, :].astype(F32) + recv[rows, :].astype(F32)
            ref[i * n : (i + 1) * n, :] = total.astype(ref.dtype)
    vec_o[...] = vec[...] + get_vec(recv, vec.shape[1])
    put_vec(vec_o[...], sent)


def qkv_third_kernel(place, vec, keep, recv, sent, kept, vec_o):
    halve_rows((place[1] >> 2) & 1, keep, recv, sent, kept)
    vec_o[...] = vec[...] + get_vec(recv, vec.shape[1])
    put_vec(vec_o[...], sent)


def message_kernel(place, vec, b_keep, b_recv, q_recv, vec_o, o0, o1, o2, o3, turned):
    m = place[0]
    channels = o0.shape[0]
    width, share = turned.shape
    cols = slice(b_keep.shape[1] - width, b_keep.shape[1])
    turned[...] = (b_keep[:, cols] + b_recv[:, cols].astype(F32)).T
    v = vec[...] + get_vec(q_recv, vec.shape[1])
    vec_o[...] = v
    tiles = v.shape[1] // 128
    high = v.astype(BF16)
    low = (v - high.astype(F32)).astype(BF16)
    both = jnp.concatenate([high.astype(F32), low.astype(F32)]).astype(BF16)
    for k, ref in enumerate((o0, o1, o2, o3)):
        t = turned[pl.ds(pl.multiple_of((m ^ k) * channels, channels), channels), :]
        ref[0:channels, 0:share] = t.astype(ref.dtype)
        if k:
            for i in range(tiles):
                at = channels + 16 * i
                ref[at : at + 16, :] = both[:, 128 * i : 128 * (i + 1)]


def last_kernel(a_keep, a_recv, b_keep, b_recv, q_keep, q_recv, up_o, down_o, qkv_o):
    hidden = up_o.shape[1]
    channels = qkv_o.shape[2]
    a = a_keep[...] + a_recv[...].astype(F32)
    share, half = a.shape
    rest = slice(0, 2 * hidden - half)
    up_o[...] = a[:, :hidden]
    down_o[:, : half - hidden] = a[:, hidden:]
    down_o[:, half - hidden :] = b_keep[:, rest] + b_recv[:, rest].astype(F32)
    q = q_keep[...] + q_recv[0:share, :].astype(F32)
    for i in range(3):
        qkv_o[i] = q[:, i * channels : (i + 1) * channels]


def small_kernel(vec, o0, o1, o2, o3, out, gains, biases, scales, table):
    channels, share = out.shape
    others = (o1, o2, o3)
    total = o0[...]
    v = vec[...]
    for ref in others:
        total = total + ref[0:channels, 0:share].astype(F32)
        parts = []
        for i in range(v.shape[1] // 128):
            at = channels + 16 * i
            both = ref[at : at + 16, :].astype(F32)
            parts.append(both[:8] + both[8:])
        v = v + jnp.concatenate(parts, axis=1)
    out[...] = total
    gains[...] = v[0:2]
    biases[...] = v[2:4]
    scales[...] = v[4:6]
    n = table.shape[1]
    for h in range(table.shape[0]):
        table[h : h + 1, :] = v[6:7, h * n : (h + 1) * n]


def input_kernel(own, recv, dy, out):
    total = own[...] + recv[...].astype(F32)
    out[...] = (dy[...].astype(F32) + total.T).astype(BF16)


def output_kernel(own, recv, mid, cols, out):
    total = own[...] + recv[...].astype(F32)
    out[...] = (mid[...] + cols[:, SCALE1 : SCALE1 + 1] * total).T.astype(BF16)


def body(
    tokens,
    page_lengths,
    norm_gains,
    norm_biases,
    layer_scales,
    w_qkv,
    rel_table,
    w_out,
    w_up,
    w_down,
    cotangent,
):
    mp, dp = lax.axis_size("mp"), lax.axis_size("dp")
    rows, width = tokens.shape
    group = rows * mp
    channels = w_qkv.shape[2]
    hidden = w_up.shape[1]
    heads = channels // HEAD_DIM
    buckets = rel_table.shape[0]
    m, d = lax.axis_index("mp"), lax.axis_index("dp")
    place = jnp.stack([m, d]).astype(jnp.int32)

    def swap(v, k, axis="mp", name="rows"):
        n = mp if axis == "mp" else dp
        with jax.named_scope(name):
            return lax.ppermute(v, axis, [(i, i ^ k) for i in range(n)])

    def after(v, *seen):
        return lax.optimization_barrier((v,) + seen)[0]

    fast = dp == 8 and (width // dp) % 16 == 0 and hidden == width

    cols = jnp.concatenate(
        [norm_gains[0:1], norm_biases[0:1], norm_gains[1:2], norm_biases[1:2], layer_scales]
    ).T
    wq = jnp.transpose(w_qkv, (1, 2, 0)).reshape(3 * channels, width)

    piece = channels // 4
    sent = jnp.concatenate([tokens, lax.dynamic_slice_in_dim(w_out, (d & 3) * piece, piece, 0)])
    x1, x2 = swap(sent, 1, name="x"), swap(sent, 2, name="x")
    x = [sent, x1, x2, swap(after(x2, x1), 1, name="x")]
    dy2 = swap(after(cotangent, *x[1:]), 2, name="dy")
    dy1 = swap(after(cotangent, *x[1:]), 1, name="dy")
    wq_t, w_up_t, w_down_t = call(
        turn_kernel,
        [like((width, 3 * channels), BF16), like((hidden, width), BF16), like((width, hidden), BF16)],
        [wq, w_up, w_down],
    )
    pattern, ids = call(
        bias_kernel,
        [like((heads, 3, 128, 128), F32), like((group, 128), jnp.int32)],
        [place, page_lengths, rel_table],
        n_smem=3,
    )
    x[1:] = lax.optimization_barrier((x[1:], wq_t, pattern))[0]
    (part,) = call(pieces_kernel, [like((4, piece, width), BF16)], x)
    part_x = swap(part, 2, "dp", name="w")
    wq_now = after(wq, wq_t, w_up_t, w_down_t)
    xt, h1, stat, qkv, pt, att, att_top, att_low = call(
        head_kernel,
        [
            like((width, group), BF16),
            like((width, group), BF16),
            like((8, group), F32),
            like((3 * channels, group), BF16),
            like((heads, group, group), BF16),
            like((channels, group), BF16),
            like((channels // 2, group), BF16),
            like((channels // 2, group), BF16),
        ],
        [place, page_lengths, rel_table] + x + [pattern, ids, cols, wq_now],
        n_smem=3,
        scratch=[
            pltpu.VMEM((heads, group, group), F32),
        ],
        limit=24,
        us=10,
    )
    (parts,) = call(
        pair_kernel, [like((8, piece, width), BF16)], [part, after(part_x, att, dy1, dy2)]
    )
    att_top, att_low, att_sent = after(att_top, parts), after(att_low, parts), after(att, parts)
    a2t, a2b = swap(att_top, 2, name="att"), swap(att_low, 2, name="att")
    a3b, a1 = swap(att_low, 3, name="att"), swap(att_sent, 1, name="att")
    atts = [att, a1, a2t, a2b, swap(a2t, 1, name="att"), a3b]
    dy = [cotangent, dy1, dy2, swap(after(dy2, parts), 1, name="dy")]
    w_pieces = [parts, swap(parts, 1, "dp", name="w")]
    w_out_full, w_out_t = call(
        out_weight_kernel, [like((width, width), BF16)] * 2, [place] + w_pieces, n_smem=1
    )
    act_like = like((width, group), BF16)
    hid_like = like((hidden, group), BF16)
    wide_like = like((width, group), F32)
    block = like((width, rows), F32)
    blocks = [block, block, like((2 * width, rows), BF16)]
    att_all, attn, hat, rstd, h2, act, slope, mid, mlp_part, m0, m2, m13 = call(
        up_kernel,
        [act_like, wide_like, wide_like, like((8, group), F32), act_like, hid_like]
        + [like((hidden, group), F32), block, wide_like]
        + blocks,
        [place] + atts + [after(xt, dy1), cols, w_out_t, w_up_t, w_down_t],
        n_smem=1,
        scratch=[pltpu.VMEM((hidden, group), F32)],
        us=10,
    )
    m_recv = swap(m13, 1, name="mlp")
    d0, d1, d2, d3, nb, dup, gm, ga, dy_t, vec = call(
        down_kernel,
        [like((channels, group), BF16)] * 4
        + [wide_like, hid_like, act_like, act_like, act_like, like((8, width), F32)],
        [place] + dy + [cols, attn, hat, rstd, slope, w_out_full, w_up, w_down],
        n_smem=1,
        scratch=[pltpu.VMEM((max(width, hidden), group), F32), pltpu.VMEM((width, 128), F32)],
        us=10,
    )
    d_att = [d0] + [swap(v, k, name="d_att") for k, v in ((1, d1), (2, d2), (3, d3))]
    grad_cols = 2 * hidden + width
    share = width // dp
    half = grad_cols // 2
    if fast:
        grad_like = [like((width // 2, half), BF16)] * 4
    else:
        grad_like = [like((width, grad_cols), BF16)]
    vec, *grads = call(
        mlp_grad_kernel,
        [like((8, width), F32)] + grad_like,
        [place, vec, mlp_part, act, dup, gm, ga, att_all, h2, dy_t],
        n_smem=1,
        scratch=[pltpu.VMEM((width, 128), F32)],
    )
    if fast:
        a_sent, a_kept, b_sent, b_kept = grads
        a_recv = swap(a_sent, 2, "dp", name="grads_a")
        b_recv = swap(b_sent, 4, "dp", name="grads_b")

    def halved(own, next_to, recv, name, us=0.01, seen=()):
        half_like = [block, like((width, rows), BF16)]
        own, sent = call(halve_kernel, half_like, [own, next_to, recv], us=us)
        return [own, swap(after(sent, *seen), 2, name=name)]

    mlp = halved(m0, m2, m_recv, "mlp", seen=d_att[1:])

    n = 3 * channels
    extra = 4 * vec.shape[0]
    if fast:
        grad_like = [like((width // 2 + extra, n), BF16), like((width // 2, n), BF16)]
    else:
        grad_like = [like((width, n), BF16)]
    p0, p2, p13, vec, *qkv_grads = call(
        back_kernel,
        blocks + [like((8, width), F32)] + grad_like,
        [place, page_lengths] + d_att + [qkv, pt, xt, h1, stat, nb, cols, wq_t, vec],
        n_smem=2,
        scratch=[
            pltpu.VMEM((n, group), BF16),
            pltpu.VMEM((heads, group, group), F32),
            pltpu.VMEM((heads, group, group), BF16),
            pltpu.VMEM((heads, 5, 128, 128), F32),
            pltpu.VMEM((heads * buckets, 128), F32),
            pltpu.VMEM((width, group), F32),
            pltpu.VMEM((width, 128), F32),
        ],
        limit=24,
        us=10,
    )
    p_recv = swap(after(p13, mlp[1]), 1, name="back")
    back = halved(p0, p2, p_recv, "back", us=10)

    def reduced(g):
        g = g.reshape(dp, width // dp, g.shape[1])
        bit = 1
        while bit < dp:
            g = g.reshape(g.shape[0] // 2, 2, width // dp, g.shape[-1])
            here = (d & bit) // bit
            sent = lax.dynamic_index_in_dim(g, 1 - here, 1, keepdims=False)
            kept = lax.dynamic_index_in_dim(g, here, 1, keepdims=False)
            g = kept.astype(F32) + swap(sent, bit, "dp").astype(F32)
            bit *= 2
            if bit < dp:
                g = g.astype(BF16)
        return g[0]

    if fast:
        q_recv = swap(after(qkv_grads[0], mlp[1]), 1, "dp", name="qkv_core")
        vec_like = [like(vec.shape, F32)]
        sent, kept, vec = call(
            qkv_second_kernel,
            [like((2 * share + extra, n), BF16), like((2 * share, n), F32)] + vec_like,
            [place, vec, qkv_grads[1], q_recv],
            n_smem=1,
        )
        recv = swap(sent, 2, "dp", name="qkv_x")
        g0, g1, g2, g_kept = call(
            grads_second_kernel,
            [like((2 * share, grad_cols // 3), BF16)] * 3 + [like((2 * share, grad_cols), BF16)],
            [place, after(a_kept, vec), a_recv, b_kept, b_recv],
            n_smem=1,
        )
        g_recv = [swap(g, 1, "dp", name="grads_core") for g in (g0, g1, g2)]
        a_sent, a_kept, b_sent, b_kept = call(
            grads_third_kernel,
            [like((share, half), BF16), like((share, half), F32)] * 2,
            [place, g_kept] + g_recv,
            n_smem=1,
        )
        a_recv = swap(a_sent, 4, "dp", name="grads_a")
        b_recv = swap(b_sent, 2, "dp", name="grads_b")
        sent, kept, vec = call(
            qkv_third_kernel,
            [like((share + extra, n), BF16), like((share, n), F32)] + vec_like,
            [place, after(vec, a_recv, back[0]), kept, recv],
            n_smem=1,
        )
        recv = swap(sent, 4, "dp", name="qkv_y")
        message = like((channels + 2 * vec.size // 128, 128), BF16)
        vec, o0, o1, o2, o3 = call(
            message_kernel,
            vec_like + [like((channels, share), F32)] + [message] * 3,
            [place, after(vec, a_recv), b_kept, b_recv, recv],
            n_smem=1,
            scratch=[pltpu.VMEM((width, share), F32)],
        )
        grad_up, grad_down, grad_qkv = call(
            last_kernel,
            [like((share, hidden), F32)] * 2 + [like((3, share, channels), F32)],
            [a_kept, a_recv, b_kept, b_recv, after(kept, o1), recv],
        )
        o1, o2, o3 = (swap(v, k, name="out") for k, v in ((1, o1), (2, o2), (3, o3)))
        grad_out, gains, biases, scales, grad_table = call(
            small_kernel,
            [like((channels, share), F32)]
            + [like((2, width), F32)] * 3
            + [like((heads * mp, buckets), F32)],
            [vec, o0, o1, o2, o3],
        )
        grad_qkv = jnp.transpose(grad_qkv, (1, 0, 2))
    else:
        summed = reduced(grads[0])
        grad_qkv = reduced(qkv_grads[0]).reshape(share, 3, channels)
        grad_up, grad_down = summed[:, :hidden], summed[:, hidden : 2 * hidden]
        turned = summed[:, 2 * hidden :].T

        def out_part(k):
            return lax.dynamic_slice_in_dim(turned, (m ^ k) * channels, channels, 0)

        grad_out = out_part(0)
        for k in range(1, mp):
            grad_out = grad_out + swap(out_part(k).astype(BF16), k).astype(F32)
        bit = 1
        while bit < dp:
            vec = vec + swap(vec, bit, "dp", name="vec")
            bit *= 2
        for k in (1, 2):
            vec = vec + swap(vec, k, name="vec")
        gains, biases, scales = vec[0:2], vec[2:4], vec[4:6]
        grad_table = vec[6, : heads * mp * buckets].reshape(heads * mp, buckets)

    (output,) = call(output_kernel, [like((rows, width), BF16)], mlp + [mid, cols])
    (grad_input,) = call(input_kernel, [like((rows, width), BF16)], back + [cotangent], us=10)
    return (
        output,
        grad_input,
        gains,
        biases,
        scales,
        grad_qkv,
        grad_table.T,
        grad_out,
        grad_up,
        grad_down.T,
    )


def solution(mesh):
    placed = (
        P(("dp", "mp"), None),
        P("dp", None),
        P(),
        P(),
        P(),
        P(None, None, "mp"),
        P(),
        P("mp", None),
        P(None, "mp"),
        P("mp", None),
        P(("dp", "mp"), None),
    )
    return jax.shard_map(
        body,
        mesh=mesh,
        in_specs=placed,
        out_specs=(
            P(("dp", "mp"), None),
            P(("dp", "mp"), None),
            P(),
            P(),
            P(),
            P("dp", None, "mp"),
            P(),
            P("mp", "dp"),
            P("dp", "mp"),
            P("mp", "dp"),
        ),
        check_vma=False,
    )
```
